32 devices in a mesh: dp: 8 (over z, y), heads: 4 (over x, core).
Axes of the slice: x: 2, y: 2, z: 4, core: 2. Of those that a mesh axis runs over, the one named last changes fastest.
Arguments:
- tokens: bfloat16 [8192, 768], P('dp'), may hold values from -6 to 6
- cotangent: bfloat16 [8192, 768], P('dp'), as said below
- clip_ids: int32 [8, 1024], P('dp'), may hold values from 0 to 3, as said below
- frame_ids: int32 [8, 1024], P('dp'), may hold values from -1 to 21, as said below
- patch_ids: int32 [8, 1024], P('dp'), may hold values from -1 to 63, as said below
- weights: float32 [768, 13056], P('dp', 'heads'), as said below
- weights_m: float32 [768, 13056], P('dp', 'heads'), may hold values from -3 to 3
- weights_v: float32 [768, 13056], P('dp', 'heads'), may hold values from 0.25 to 1
- weights_ema: float32 [768, 13056], P('dp', 'heads'), as said below
- vectors: float32 [10, 768], P(None, 'dp'), as said below
- vectors_m: float32 [10, 768], P(None, 'dp'), may hold values from -9 to 9
- vectors_v: float32 [10, 768], P(None, 'dp'), may hold values from 2.25 to 9
- vectors_ema: float32 [10, 768], P(None, 'dp'), as said below
Outputs:
- layer_out: float32 [8192, 768], P('dp')
- input_grad: float32 [8192, 768], P('dp')
- weight_grad: float32 [768, 13056], P('dp', 'heads')
- vector_grad: float32 [10, 768], P(None, 'dp')
- grad_norm: float32 [], replicated
- weights_new: float32 [768, 13056], P('dp', 'heads')
- weights_m_new: float32 [768, 13056], P('dp', 'heads')
- weights_v_new: float32 [768, 13056], P('dp', 'heads')
- weights_ema_new: float32 [768, 13056], P('dp', 'heads')
- vectors_new: float32 [10, 768], P(None, 'dp')
- vectors_m_new: float32 [10, 768], P(None, 'dp')
- vectors_v_new: float32 [10, 768], P(None, 'dp')
- vectors_ema_new: float32 [10, 768], P(None, 'dp')
The draws below stay inside these ranges and needn't reach their ends.
Inputs may be any that keep to these rules, and one draw needn't show every extreme that they name: `clip_ids`: within a sequence clip ids never fall and start at 0 on the first row; each clip begins with its class row (frame and patch id -1). `frame_ids`: after its class row a clip holds frames of one patch count between 24 and 64 in order; its last frame may be short. `patch_ids`: patch ids count from 0 within each frame. `cotangent`: entries of order one. `weights`: matrices scaled by their fan-in. `weights_ema`: of the size of weights. `vectors`: gains near one and small biases. `vectors_ema`: of the size of vectors.
All inputs are finite; a program needn't handle non-finite values.
Results may differ from the reference program's by a relative error of at most 0.02.
The reference program's roundings to bfloat16 on the way count: a program that leaves them out, or rounds other values in their place, can miss the bound.
Values may be sent and summed in bfloat16 or wider, within the bound.
No kernel may reach another device: no remote copies, remote signals or barrier semaphores. Data moves between devices by JAX's collectives and lax.ppermute only.
A program may use at most 192 MiB of HBM per device.

```python
import math
import jax
import jax.numpy as jnp
from jax import lax

D = 768
HEADS = 12
HEAD_DIM = 64
MLP = 3072
SEQ_LEN = 1024
CLIPS = 4
PATCH_MIN = 24
PATCH_MAX = 64
STEP = 5
NPARAM = 10034688
SEQS = 8
TOKENS = 8192
N_HEADS = 4


def clip_layout(key):
    cut_key, count_key = jax.random.split(key)
    first_len = SEQ_LEN // 2 + 1
    spare = SEQ_LEN - first_len - 1
    seq_keys = jax.random.split(cut_key, SEQS)

    def later_cuts(one_key):
        return jnp.sort(jax.random.permutation(one_key, spare)[:CLIPS - 2]) + first_len + 1
    rest = jax.vmap(later_cuts)(seq_keys).astype(jnp.int32)
    cuts = jnp.concatenate([jnp.full((SEQS, 1), first_len, jnp.int32), rest], 1)
    bounds = jnp.concatenate([jnp.zeros((SEQS, 1), jnp.int32), cuts, jnp.full((SEQS, 1), SEQ_LEN, jnp.int32)], 1)
    clip_lens = bounds[:, 1:] - bounds[:, :-1]
    longest = 1 + jnp.argmax(clip_lens[:, 1:], axis=-1).astype(jnp.int32)
    position = jnp.arange(SEQ_LEN)
    passed = cuts[:, None, :] <= position[None, :, None]
    clip_index = jnp.sum(passed.astype(jnp.int32), -1)
    clip_start = jnp.max(jnp.where(passed, cuts[:, None, :], 0), -1, initial=0)
    offset = position[None, :] - clip_start
    clip_range = jnp.arange(CLIPS)[None, :]
    patch_counts = jax.random.randint(count_key, (SEQS, CLIPS), PATCH_MIN, PATCH_MAX + 1)
    patch_counts = jnp.where(clip_range == 0, PATCH_MIN, jnp.where(clip_range == longest[:, None], PATCH_MAX, patch_counts))
    chosen = clip_index[:, :, None] == jnp.arange(CLIPS)[None, None, :]
    per_frame = jnp.sum(jnp.where(chosen, patch_counts[:, None, :], 0), -1)
    frame_index = jnp.where(offset == 0, -1, (offset - 1) // per_frame)
    patch_index = jnp.where(offset == 0, -1, (offset - 1) % per_frame)
    return (clip_index.astype(jnp.int32), frame_index.astype(jnp.int32), patch_index.astype(jnp.int32))


def draw_clip_ids(key, part):
    layout = clip_layout(key)
    return layout[0]


def draw_frame_ids(key, part):
    layout = clip_layout(key)
    return layout[1]


def draw_patch_ids(key, part):
    layout = clip_layout(key)
    return layout[2]


def column_scales(rise):
    group_count = N_HEADS
    group_width = D // group_count
    hidden_width = MLP // group_count
    group_cols = 9 * group_width + 2 * hidden_width
    column = jnp.arange(group_count * group_cols)
    group_pos = (column // group_cols).astype(jnp.float32)
    inner = column % group_cols
    lift = rise ** (0.5 * group_pos / max(group_count - 1, 1))
    mean_patch = (PATCH_MIN + PATCH_MAX) // 2
    time_keys = max(2, SEQ_LEN // CLIPS // mean_patch)
    space_keys = mean_patch + 1
    base = D ** (-0.5)
    ones_row = jnp.ones_like(lift)
    conditions = [inner < 2 * group_width, inner < 3 * group_width, inner < 4 * group_width, inner < 5 * group_width, inner < 7 * group_width, inner < 8 * group_width, inner < 9 * group_width, inner < 9 * group_width + hidden_width]
    choices_list = [base * ones_row, base * lift, base * lift * time_keys ** 0.5, base * ones_row, base * ones_row, base * lift, base * lift * space_keys ** 0.5, base * lift]
    scales = jnp.select(conditions, choices_list, MLP ** (-0.5) * lift)
    return scales[None, :]


def draw_weights(key, part):
    key = jax.random.fold_in(key, 11)
    shape = (D, 9 * D + 2 * MLP)
    noise = jnp.clip(jax.random.normal(key, shape, jnp.float32), -4.0, 4.0)
    rise = 3.0
    return noise * column_scales(rise)


def draw_weights_ema(key, part):
    key = jax.random.fold_in(key, 12)
    shape = (D, 9 * D + 2 * MLP)
    noise = jnp.clip(jax.random.normal(key, shape, jnp.float32), -4.0, 4.0)
    rise = 3.0
    return noise * column_scales(rise)


def vector_rows(noise, rise):
    position = jnp.arange(D).astype(jnp.float32) / max(D - 1, 1)
    lift = rise ** (0.5 * position)
    row = jnp.arange(10)[:, None]
    is_gain = (row == 0) | (row == 4) | (row == 7)
    return jnp.where(is_gain, 0.8 * lift[None, :] * (1.0 + 0.1 * noise), 0.2 * noise)


def draw_vectors(key, part):
    key = jax.random.fold_in(key, 21)
    noise = jnp.clip(jax.random.normal(key, (10, D), jnp.float32), -4.0, 4.0)
    rise = 3.0
    return vector_rows(noise, rise)


def draw_vectors_ema(key, part):
    key = jax.random.fold_in(key, 22)
    noise = jnp.clip(jax.random.normal(key, (10, D), jnp.float32), -4.0, 4.0)
    rise = 3.0
    return vector_rows(noise, rise)


def draw_cotangent(key, part):
    key = jax.random.fold_in(key, 31)
    noise = jnp.clip(jax.random.normal(key, (TOKENS, D), jnp.float32), -4.0, 4.0)
    rise = 3.0
    position = jnp.arange(D).astype(jnp.float32) / max(D - 1, 1)
    return (0.8 * noise * rise ** (0.5 * position)[None, :]).astype(jnp.bfloat16)


def steps_of(stream_key, extent, cuts, low, largest):
    level = 1.0
    for dim, blocks in cuts:
        steps = jax.random.uniform(jax.random.fold_in(jax.random.fold_in(stream_key, 6), dim), (blocks,), jnp.float32, low / len(cuts), largest / len(cuts))
        level = level * jnp.repeat(jnp.exp(steps), extent[dim] // blocks).reshape((-1,) + (1,) * (len(extent) - 1 - dim))
    return level


def gaussian(key, extent, scale, most, cuts=(), held_as=jnp.bfloat16):
    array = jax.random.normal(key, extent, jnp.float32) * scale
    if len(cuts) > 0:
        array = steps_of(key, extent, cuts, -0.22, 0.18) * array
    return jnp.clip(array, min=-most, max=most).astype(held_as)


def setup_inputs(seed: int = 0) -> dict:
    streams_of = jax.random.split(jax.random.key(seed), 14)
    return {
        "tokens": gaussian(streams_of[0], (TOKENS, D), 1.0, 6.0, ((0, 8),)),
        "cotangent": draw_cotangent(jax.random.fold_in(streams_of[13], 71), 0),
        "clip_ids": draw_clip_ids(jax.random.fold_in(streams_of[13], 71), 0),
        "frame_ids": draw_frame_ids(jax.random.fold_in(streams_of[13], 71), 0),
        "patch_ids": draw_patch_ids(jax.random.fold_in(streams_of[13], 71), 0),
        "weights": draw_weights(jax.random.fold_in(streams_of[13], 71), 0),
        "weights_m": gaussian(streams_of[6], (D, 9 * D + 2 * MLP), 0.5, 3.0, ((0, 8), (1, 4)), jnp.float32),
        "weights_v": jnp.clip(jnp.exp(math.log(1.0) - 1.3862944 * jax.random.uniform(streams_of[7], (D, 9 * D + 2 * MLP), jnp.float32) ** steps_of(streams_of[7], (D, 9 * D + 2 * MLP), ((0, 8), (1, 4)), -0.2, 0.2)), 0.25, 1.0),
        "weights_ema": draw_weights_ema(jax.random.fold_in(streams_of[13], 71), 0),
        "vectors": draw_vectors(jax.random.fold_in(streams_of[13], 71), 0),
        "vectors_m": gaussian(streams_of[10], (10, D), 1.5, 9.0, ((1, 8),), jnp.float32),
        "vectors_v": jnp.clip(jnp.exp(math.log(9.0) - 1.3862944 * jax.random.uniform(streams_of[11], (10, D), jnp.float32) ** steps_of(streams_of[11], (10, D), ((1, 8),), -0.2, 0.2)), 2.25, 9.0),
        "vectors_ema": draw_vectors_ema(jax.random.fold_in(streams_of[13], 71), 0),
    }


@jax.custom_vjp
def low(v):
    return lax.optimization_barrier(v.astype(jnp.bfloat16)).astype(jnp.float32)

@jax.custom_vjp
def low_back(v):
    return v

def low_keep(v):
    return (low(v), None)

def low_pass(kept, grad):
    return (grad,)

def back_keep(v):
    return (v, None)

def back_low(kept, grad):
    return (low(grad),)
low.defvjp(low_keep, low_pass)
low_back.defvjp(back_keep, back_low)
NORM_EPS = 1e-06
BETA_FIRST = 0.5
BETA_SECOND = 0.5
AVERAGE_RATE = 0.5
MATRIX_RATE = 0.03
VECTOR_RATE = 0.3
MATRIX_DECAY = 0.05
ADAM_EPS = 1e-08
MASKED = -1e+30
HIGHEST = lax.Precision.HIGHEST

def rounded_both(value):
    return low(low_back(value))

def layer_norm(stream, gain, shift):
    center = stream - lax.optimization_barrier(jnp.mean(stream, -1, keepdims=True))
    spread = lax.optimization_barrier(jnp.mean(center * center, -1, keepdims=True))
    return center * lax.rsqrt(spread + NORM_EPS) * gain + shift

def allowed_pairs(clip_row, frame_row, patch_row, mask_kind):
    same_clip = clip_row[:, None] == clip_row[None, :]
    if mask_kind == 'temporal':
        return same_clip & (patch_row[:, None] == patch_row[None, :])
    same_frame = (frame_row[:, None] == frame_row[None, :]) | (frame_row[:, None] < 0) | (frame_row[None, :] < 0)
    return same_clip & same_frame

def attention(head_inputs, clip_rows, frame_rows, patch_rows, mask_kind, seq_count):
    group_width = D // N_HEADS
    row_count = head_inputs.shape[0]

    def split_part(lower, upper):
        return rounded_both(head_inputs[:, :, lower:upper]).reshape(seq_count, SEQ_LEN, HEADS, HEAD_DIM)
    queries = split_part(0, group_width)
    keys_all = split_part(group_width, 2 * group_width)
    values = split_part(2 * group_width, 3 * group_width)

    def one_sequence(sequence_item):
        query_seq, key_seq, value_seq, clip_row, frame_row, patch_row = sequence_item
        scores = jnp.einsum('qhd,khd->hqk', query_seq, key_seq, precision=HIGHEST) * HEAD_DIM ** (-0.5)
        scores = low_back(scores)
        allowed = allowed_pairs(clip_row, frame_row, patch_row, mask_kind)
        scores = jnp.where(allowed[None], scores, MASKED)
        row_top = lax.optimization_barrier(jnp.max(scores, -1, keepdims=True))
        exp_scores = jnp.exp(scores - row_top)
        soft_probs = exp_scores / lax.optimization_barrier(jnp.sum(exp_scores, -1, keepdims=True))
        return jnp.einsum('hqk,khd->qhd', low(soft_probs), value_seq, precision=HIGHEST)
    outputs = lax.map(jax.checkpoint(one_sequence), (queries, keys_all, values, clip_rows, frame_rows, patch_rows))
    return rounded_both(outputs.reshape(row_count, N_HEADS, group_width))

def branch_sum(inputs, block):
    parts = jnp.einsum('tge,gde->gtd', inputs, block, precision=HIGHEST)
    return low_back(lax.optimization_barrier(jnp.sum(parts, 0)))

def layer(stream, weights, vectors, clip_rows, frame_rows, patch_rows):
    group_count = N_HEADS
    group_width = D // group_count
    hidden_width = MLP // group_count
    column_count = weights.shape[1] // group_count
    blocks = low(weights).reshape(D, group_count, column_count).transpose(1, 0, 2)
    vector_low = low(vectors)
    row_count = stream.shape[0]
    seq_count = row_count // SEQ_LEN
    first = low(layer_norm(stream, vector_low[0], vector_low[1]))
    time_inputs = jnp.einsum('td,gdc->tgc', first, blocks[:, :, :3 * group_width], precision=HIGHEST)
    time_heads = attention(time_inputs, clip_rows, frame_rows, patch_rows, 'temporal', seq_count)
    mixed = branch_sum(time_heads, blocks[:, :, 3 * group_width:4 * group_width]) + vector_low[2]
    fc_inputs = low(mixed).reshape(row_count, group_count, group_width)
    stream_one = stream + branch_sum(fc_inputs, blocks[:, :, 4 * group_width:5 * group_width]) + vector_low[3]
    second = low(layer_norm(stream_one, vector_low[4], vector_low[5]))
    space_inputs = jnp.einsum('td,gdc->tgc', second, blocks[:, :, 5 * group_width:8 * group_width], precision=HIGHEST)
    space_heads = attention(space_inputs, clip_rows, frame_rows, patch_rows, 'spatial', seq_count)
    stream_two = stream_one + branch_sum(space_heads, blocks[:, :, 8 * group_width:9 * group_width]) + vector_low[6]
    third = low(layer_norm(stream_two, vector_low[7], vector_low[8]))
    up_blocks = blocks[:, :, 9 * group_width:9 * group_width + hidden_width]
    pre_act = low_back(jnp.einsum('td,gdf->tgf', third, up_blocks, precision=HIGHEST))
    activ = low(jax.nn.gelu(pre_act, approximate=False))
    down_blocks = blocks[:, :, 9 * group_width + hidden_width:]
    return stream_two + branch_sum(activ, down_blocks) + vector_low[9]

def adam_update(master, first_moment, second_moment, average, gradient, factor, rate, decay):
    clipped = gradient * factor
    first_new = BETA_FIRST * first_moment + (1.0 - BETA_FIRST) * clipped
    second_new = BETA_SECOND * second_moment + (1.0 - BETA_SECOND) * clipped * clipped
    first_hat = first_new / (1.0 - BETA_FIRST ** STEP)
    second_hat = second_new / (1.0 - BETA_SECOND ** STEP)
    master_new = master - rate * (first_hat / (jnp.sqrt(second_hat) + ADAM_EPS) + decay * master)
    average_new = AVERAGE_RATE * average + (1.0 - AVERAGE_RATE) * master_new
    return (master_new, first_new, second_new, average_new)

def reference(tokens, cotangent, clip_ids, frame_ids, patch_ids, weights, weights_m, weights_v, weights_ema, vectors, vectors_m, vectors_v, vectors_ema):
    batch_seqs = math.gcd(SEQS, max(1, 4096 // SEQ_LEN))
    batch_count = SEQS // batch_seqs
    batch_rows = batch_seqs * SEQ_LEN
    stream_in = tokens.astype(jnp.float32).reshape(batch_count, batch_rows, D)
    grad_in = cotangent.astype(jnp.float32).reshape(batch_count, batch_rows, D)
    clip_in = clip_ids.reshape(batch_count, batch_seqs, SEQ_LEN)
    frame_in = frame_ids.reshape(batch_count, batch_seqs, SEQ_LEN)
    patch_in = patch_ids.reshape(batch_count, batch_seqs, SEQ_LEN)

    def one_batch(carry, batch_item):
        weight_total, vector_total = carry
        stream, grad_out, clip_rows, frame_rows, patch_rows = batch_item

        def forward(stream_arg, weight_arg, vector_arg):
            return layer(stream_arg, weight_arg, vector_arg, clip_rows, frame_rows, patch_rows)
        output, pull_back = jax.vjp(forward, stream, weights, vectors)
        grad_stream, grad_weights, grad_vectors = pull_back(grad_out)
        return ((weight_total + grad_weights, vector_total + grad_vectors), (output, grad_stream))
    start_carry = (jnp.zeros(weights.shape, jnp.float32), jnp.zeros(vectors.shape, jnp.float32))
    (weight_grad, vector_grad), (outputs, input_grads) = lax.scan(one_batch, start_carry, (stream_in, grad_in, clip_in, frame_in, patch_in))
    layer_out = outputs.reshape(TOKENS, D)
    input_grad = input_grads.reshape(TOKENS, D)
    grad_norm = jnp.sqrt(jnp.sum(weight_grad * weight_grad) + jnp.sum(vector_grad * vector_grad))
    limit = 0.5 * math.sqrt(NPARAM)
    factor = limit / jnp.maximum(grad_norm, limit)
    weights_new, weights_m_new, weights_v_new, weights_ema_new = adam_update(weights, weights_m, weights_v, weights_ema, weight_grad, factor, MATRIX_RATE, MATRIX_DECAY)
    vectors_new, vectors_m_new, vectors_v_new, vectors_ema_new = adam_update(vectors, vectors_m, vectors_v, vectors_ema, vector_grad, factor, VECTOR_RATE, 0.0)
    return (layer_out, input_grad, weight_grad, vector_grad, grad_norm, weights_new, weights_m_new, weights_v_new, weights_ema_new, vectors_new, vectors_m_new, vectors_v_new, vectors_ema_new)
```

```python
import math

import jax
import jax.numpy as jnp
from jax import lax
from jax.sharding import PartitionSpec as P

HEAD_DIM = 64
STEP = 5
NPARAM = 10034688

NORM_EPS = 1e-06
BETA_FIRST = 0.5
BETA_SECOND = 0.5
AVERAGE_RATE = 0.5
MATRIX_RATE = 0.03
VECTOR_RATE = 0.3
MATRIX_DECAY = 0.05
ADAM_EPS = 1e-08
MASKED = -1e30
SCALE = HEAD_DIM ** (-0.5)
F32 = jnp.float32
BF16 = jnp.bfloat16


def core_swap(value):
    return lax.ppermute(value, "heads", [(i, i ^ 1) for i in range(4)])


def x_swap(value):
    return lax.ppermute(value, "heads", [(i, i ^ 2) for i in range(4)])


def dp_swap(value, mask):
    count = lax.axis_size("dp")
    return lax.ppermute(value, "dp", [(i, i ^ mask) for i in range(count)])


def pick(stacked, index):
    return lax.dynamic_index_in_dim(stacked, index, 0, keepdims=False)


def gather_rows(piece):
    count = lax.axis_size("dp")
    half = count // 2
    place = lax.axis_index("dp")
    z_place, y_place = place // 2, place % 2
    blocks = jnp.stack([piece] + [dp_swap(piece, 2 * k) for k in range(1, half)])
    other = dp_swap(blocks, 1)
    both = jnp.concatenate([blocks, other], 0)
    ordered = []
    for z in range(half):
        for y in range(2):
            ordered.append(pick(both, (z_place ^ z) + half * (y_place ^ y)))
    return jnp.concatenate(ordered, 0)


def scatter_rows(total):
    count = lax.axis_size("dp")
    half = count // 2
    place = lax.axis_index("dp")
    z_place, y_place = place // 2, place % 2
    rows = total.shape[0] // count
    blocks = total.reshape(half, 2, rows, total.shape[1])

    def of_y(index):
        return lax.dynamic_index_in_dim(blocks, index, 1, keepdims=False)

    received = dp_swap(of_y(1 - y_place).astype(BF16), 1)
    summed = of_y(y_place).astype(F32) + received.astype(F32)
    result = pick(summed, z_place)
    for k in range(1, half):
        result = result + dp_swap(pick(summed, z_place ^ k).astype(BF16), 2 * k).astype(F32)
    return result


def core_sum(own, other):
    return own + core_swap(other.astype(BF16)).astype(F32)


def layer_norm(stream, gain, shift):
    center = stream - jnp.mean(stream, -1, keepdims=True)
    spread = jnp.mean(center * center, -1, keepdims=True)
    return center * lax.rsqrt(spread + NORM_EPS) * gain + shift


def dot(left, right):
    return jnp.dot(left, right, preferred_element_type=F32)


def dot_nt(left, right):
    return lax.dot_general(left, right, (((1,), (1,)), ((), ())), preferred_element_type=F32)


def dot_tn(left, right):
    return lax.dot_general(left, right, (((0,), (0,)), ((), ())), preferred_element_type=F32)


def masks(clip_q, frame_q, patch_q, clip_k, frame_k, patch_k):
    same_clip = clip_q[:, None] == clip_k[None, :]
    temporal = same_clip & (patch_q[:, None] == patch_k[None, :])
    spatial = same_clip & (
        (frame_q[:, None] == frame_k[None, :]) | (frame_q[:, None] < 0) | (frame_k[None, :] < 0)
    )
    return temporal, spatial


def to_heads(rows):
    return rows.reshape(rows.shape[0], rows.shape[1] // HEAD_DIM, HEAD_DIM)


def attend_forward(queries, keys, values, allowed):
    scores = jnp.einsum("qhd,khd->hqk", to_heads(queries), to_heads(keys), preferred_element_type=F32) * SCALE
    scores = jnp.where(allowed[None], scores, MASKED)
    top = jnp.max(scores, -1, keepdims=True)
    exps = jnp.exp(scores - top)
    total = jnp.sum(exps, -1, keepdims=True)
    probs = (exps / total).astype(BF16)
    out = jnp.einsum("hqk,khd->qhd", probs, to_heads(values), preferred_element_type=F32)
    return out.reshape(queries.shape).astype(BF16), (top + jnp.log(total))[:, :, 0]


def attend_backward(queries, keys, values, grad_out, logs, allowed):
    q, k, v, g = to_heads(queries), to_heads(keys), to_heads(values), to_heads(grad_out)
    scores = jnp.einsum("qhd,khd->hqk", q, k, preferred_element_type=F32) * SCALE
    scores = jnp.where(allowed[None], scores, MASKED)
    probs = jnp.exp(scores - logs[:, :, None])
    grad_probs = jnp.einsum("qhd,khd->hqk", g, v, preferred_element_type=F32)
    delta = jnp.sum(probs * grad_probs, -1, keepdims=True)
    grad_scores = (probs * (grad_probs - delta)).astype(BF16)
    grad_q = jnp.einsum("hqk,khd->qhd", grad_scores, k, preferred_element_type=F32) * SCALE
    grad_k = jnp.einsum("hqk,qhd->khd", grad_scores, q, preferred_element_type=F32) * SCALE
    grad_v = jnp.einsum("hqk,qhd->khd", probs.astype(BF16), g, preferred_element_type=F32)
    return grad_q.reshape(queries.shape), grad_k.reshape(keys.shape), grad_v.reshape(values.shape)


def x_sum(part):
    low = part.astype(BF16)
    return low.astype(F32) + x_swap(low).astype(F32)


def project(rows, maps, width):
    parts = [dot(rows, one).astype(BF16) for one in maps]
    queries = jnp.concatenate([one[:, :width] for one in parts], 1)
    pairs = jnp.concatenate([one[:, width : 2 * width] for one in parts] + [one[:, 2 * width :] for one in parts], 1)
    return queries, pairs


def heads_backward(queries, pairs, grad_heads, logs, allowed, width):
    rows = queries.shape[0]
    keys, values = pairs[:, : 2 * width], pairs[:, 2 * width :]
    grad_q, grad_k, grad_v = attend_backward(queries, keys, values, grad_heads, logs, allowed)
    grad_pairs = jnp.concatenate([grad_k, grad_v], 1)
    received = core_swap(grad_pairs[rows:].astype(BF16))
    grad_pairs = grad_pairs[:rows] + received_in_order(received, width).astype(F32)
    grad_q, grad_pairs = grad_q.astype(BF16), grad_pairs.astype(BF16)
    grad_k, grad_v = grad_pairs[:, : 2 * width], grad_pairs[:, 2 * width :]
    return [
        jnp.concatenate([one[:, g * width : (g + 1) * width] for one in (grad_q, grad_k, grad_v)], 1)
        for g in range(2)
    ]


def received_in_order(pairs, width):
    return jnp.concatenate([pairs[:, i * width : (i + 1) * width] for i in (1, 0, 3, 2)], 1)


def both_groups(own):
    return [own, core_swap(own)]


def adam_update(master, first_moment, second_moment, average, gradient, factor, rate, decay):
    clipped = gradient * factor
    first_new = BETA_FIRST * first_moment + (1.0 - BETA_FIRST) * clipped
    second_new = BETA_SECOND * second_moment + (1.0 - BETA_SECOND) * clipped * clipped
    first_hat = first_new / (1.0 - BETA_FIRST**STEP)
    second_hat = second_new / (1.0 - BETA_SECOND**STEP)
    master_new = master - rate * (first_hat / (jnp.sqrt(second_hat) + ADAM_EPS) + decay * master)
    average_new = AVERAGE_RATE * average + (1.0 - AVERAGE_RATE) * master_new
    return (master_new, first_new, second_new, average_new)


def gelu_parts(pre):
    cdf = 0.5 * (1.0 + lax.erf(pre * (0.5**0.5)))
    slope = cdf + pre * jnp.exp(-0.5 * pre * pre) * (1.0 / math.sqrt(2.0 * math.pi))
    return pre * cdf, slope


def local(
    tokens,
    cotangent,
    clip_ids,
    frame_ids,
    patch_ids,
    weights,
    weights_m,
    weights_v,
    weights_ema,
    vectors,
    vectors_m,
    vectors_v,
    vectors_ema,
):
    group_count = lax.axis_size("heads")
    place = lax.axis_index("heads")
    core = place % 2
    features = tokens.shape[1]
    width = features // group_count
    hidden = (weights.shape[1] - 9 * width) // 2
    rows = tokens.shape[0] // 2

    low = weights.astype(BF16)
    vector_low = vectors.astype(BF16)
    time_piece = gather_rows(jnp.concatenate([low[:, : 3 * width], vector_low.T], 1))
    out_piece = gather_rows(low[:, 3 * width : 5 * width])
    space_piece = gather_rows(low[:, 5 * width : 9 * width])
    mlp_piece = gather_rows(low[:, 9 * width :])
    vector_f = time_piece[:, 3 * width :].T.astype(F32)
    time_maps = both_groups(time_piece[:, : 3 * width])
    time_out, time_mix = zip(*[(one[:, :width], one[:, width:]) for one in both_groups(out_piece)])
    space_both = both_groups(space_piece)
    space_maps = [one[:, : 3 * width] for one in space_both]
    space_out = jnp.concatenate([one[:, 3 * width :] for one in space_both], 1)
    mlp_both = both_groups(mlp_piece)
    up_maps = jnp.concatenate([one[:, :hidden] for one in mlp_both], 1)
    down_maps = jnp.concatenate([one[:, hidden:] for one in mlp_both], 1)

    mix_far = x_swap(jnp.concatenate(time_mix, 1))
    mix_all = jnp.concatenate([time_mix[0], time_mix[1], mix_far], 1)

    def group_rows(value):
        return jnp.concatenate(
            [lax.dynamic_slice_in_dim(value, (place ^ k) * width, width, 0) for k in range(group_count)], 0
        )

    out_both = jnp.concatenate(time_out, 1)
    out_grouped = group_rows(out_both)
    fused = dot(mix_all, out_grouped).astype(BF16)
    bias_grouped = group_rows(vector_f[2])
    mix_bias = jnp.sum(mix_all.astype(F32) * bias_grouped[None, :], 1) + vector_f[3]

    def own_rows(value):
        return lax.dynamic_slice_in_dim(value, core * rows, rows, 0)

    def key_ids(value):
        return jnp.concatenate([own_rows(value), lax.dynamic_slice_in_dim(value, (1 - core) * rows, rows, 0)], 0)

    stream_in = own_rows(tokens).astype(F32)
    grad_out_low = own_rows(cotangent)
    grad_out = grad_out_low.astype(F32)
    ids = [key_ids(one[0]) for one in (clip_ids, frame_ids, patch_ids)]
    temporal, spatial = masks(*[one[:rows] for one in ids], *ids)

    def all_pairs(pairs):
        return jnp.concatenate([pairs, received_in_order(core_swap(pairs), width)], 0)

    first = layer_norm(stream_in, vector_f[0], vector_f[1]).astype(BF16)
    time_q, time_pairs = project(first, time_maps, width)
    time_pairs = all_pairs(time_pairs)
    time_heads, time_logs = attend_forward(time_q, time_pairs[:, : 2 * width], time_pairs[:, 2 * width :], temporal)
    stream_one = stream_in + x_sum(dot_nt(time_heads, fused)) + mix_bias

    second = layer_norm(stream_one, vector_f[4], vector_f[5]).astype(BF16)
    space_q, space_pairs = project(second, space_maps, width)
    space_pairs = all_pairs(space_pairs)
    space_heads, space_logs = attend_forward(
        space_q, space_pairs[:, : 2 * width], space_pairs[:, 2 * width :], spatial
    )
    stream_two = stream_one + x_sum(dot_nt(space_heads, space_out)) + vector_f[6]

    third = layer_norm(stream_two, vector_f[7], vector_f[8]).astype(BF16)
    grad_act = dot(grad_out_low, down_maps)
    act, slope = gelu_parts(dot(third, up_maps))
    activ = act.astype(BF16)
    grad_pre = (grad_act * slope).astype(BF16)
    grad_third = x_sum(dot_nt(grad_pre, up_maps))
    layer_out = stream_two + x_sum(dot_nt(activ, down_maps)) + vector_f[9]
    grad_up = dot_tn(third, grad_pre)
    grad_down = dot_tn(grad_out_low, activ)
    mlp_total = core_sum(
        jnp.concatenate([grad_up[:, :hidden], grad_down[:, :hidden]], 1),
        jnp.concatenate([grad_up[:, hidden:], grad_down[:, hidden:]], 1),
    )
    mlp_shard = scatter_rows(mlp_total)
    unused_third, third_pull = jax.vjp(layer_norm, stream_two, vector_f[7], vector_f[8])
    grad_two_norm, grad_gain_three, grad_shift_three = third_pull(grad_third)
    grad_two = grad_out + grad_two_norm

    grad_two_low = grad_two.astype(BF16)
    grad_space_out = dot_tn(grad_two_low, space_heads)
    grad_space_heads = dot(grad_two_low, space_out).astype(BF16)
    grad_space = heads_backward(space_q, space_pairs, grad_space_heads, space_logs, spatial, width)
    grad_second = x_sum(sum(dot_nt(one, maps) for one, maps in zip(grad_space, space_maps)))
    space_total = core_sum(
        *[
            jnp.concatenate([dot_tn(second, grad_space[g]), grad_space_out[:, g * width : (g + 1) * width]], 1)
            for g in range(2)
        ]
    )
    space_shard = scatter_rows(space_total)
    unused_second, second_pull = jax.vjp(layer_norm, stream_one, vector_f[4], vector_f[5])
    grad_one_norm, grad_gain_two, grad_shift_two = second_pull(grad_second)
    grad_one = grad_two + grad_one_norm

    grad_one_low = grad_one.astype(BF16)
    grad_fused = dot_tn(grad_one_low, time_heads).astype(BF16)
    grad_time_heads = dot(grad_one_low, fused).astype(BF16)
    low_sum = jnp.sum(grad_one_low.astype(F32), 0)
    grad_bias_time = group_rows_back(dot_tn(mix_all, low_sum.astype(BF16)[:, None]), place, group_count)[:, 0]
    grad_time_out = group_rows_back(dot_tn(mix_all, grad_fused), place, group_count)
    grad_mix = dot_nt(grad_fused, out_grouped)
    bias_term = low_sum[:, None] * bias_grouped[None, : 2 * width]
    mix_near = grad_mix[:, : 2 * width] + bias_term
    mix_far_part = grad_mix[:, 2 * width :]
    mix_keep = jnp.concatenate([mix_near[:, :width], mix_far_part[:, :width]], 1)
    mix_send = jnp.concatenate([mix_near[:, width:], mix_far_part[:, width:]], 1)
    mix_sum = mix_keep + core_swap(mix_send.astype(BF16)).astype(F32)
    mix_total = mix_sum[:, :width] + x_swap(mix_sum[:, width:].astype(BF16)).astype(F32)
    out_total = core_sum(grad_time_out[:, :width], grad_time_out[:, width:])
    out_shard = scatter_rows(jnp.concatenate([out_total, mix_total], 1))
    grad_time = heads_backward(time_q, time_pairs, grad_time_heads, time_logs, temporal, width)
    grad_first = x_sum(sum(dot_nt(one, maps) for one, maps in zip(grad_time, time_maps)))
    unused_first, first_pull = jax.vjp(layer_norm, stream_in, vector_f[0], vector_f[1])
    grad_in_norm, grad_gain_one, grad_shift_one = first_pull(grad_first)
    grad_in = grad_one + grad_in_norm
    vector_rows = jnp.stack(
        [
            grad_gain_one,
            grad_shift_one,
            grad_bias_time,
            jnp.sum(grad_one, 0),
            grad_gain_two,
            grad_shift_two,
            jnp.sum(grad_two, 0),
            grad_gain_three,
            grad_shift_three,
            jnp.sum(grad_out, 0),
        ]
    )
    time_total = core_sum(
        *[jnp.concatenate([dot_tn(first, grad_time[g]), vector_rows.T], 1) for g in range(2)]
    )
    last_shard = scatter_rows(time_total)
    time_shard, vector_grad = last_shard[:, : 3 * width], last_shard[:, 3 * width :].T
    weight_grad = jnp.concatenate([time_shard, out_shard, space_shard, mlp_shard], 1)

    square = jnp.sum(weight_grad * weight_grad) + jnp.sum(vector_grad * vector_grad) / group_count
    square = jnp.full((8, 128), square, F32)
    square = square + core_swap(square)
    square = square + x_swap(square)
    count = lax.axis_size("dp")
    step = 1
    while step < count:
        square = square + dp_swap(square, step)
        step *= 2
    grad_norm = jnp.sqrt(square[0, 0])
    limit = 0.5 * math.sqrt(NPARAM)
    factor = limit / jnp.maximum(grad_norm, limit)
    weights_out = adam_update(
        weights, weights_m, weights_v, weights_ema, weight_grad, factor, MATRIX_RATE, MATRIX_DECAY
    )
    vectors_out = adam_update(vectors, vectors_m, vectors_v, vectors_ema, vector_grad, factor, VECTOR_RATE, 0.0)

    def whole(value):
        other = core_swap(value.astype(BF16)).astype(F32)
        mine = value.astype(BF16).astype(F32)
        lower = jnp.where(core == 0, mine, other)
        upper = jnp.where(core == 0, other, mine)
        return jnp.concatenate([lower, upper], 0)

    return (
        whole(layer_out),
        whole(grad_in),
        weight_grad,
        vector_grad,
        grad_norm,
        *weights_out,
        *vectors_out,
    )


def group_rows_back(value, place, group_count):
    blocks = value.reshape(group_count, value.shape[0] // group_count, *value.shape[1:])
    return jnp.concatenate([pick(blocks, place ^ k) for k in range(group_count)], 0)


def solution(mesh):
    rows, square, line = P("dp", None), P("dp", "heads"), P(None, "dp")
    placed = (rows,) * 5 + (square,) * 4 + (line,) * 4
    return jax.shard_map(
        local,
        mesh=mesh,
        in_specs=placed,
        out_specs=(rows, rows, square, line, P()) + (square,) * 4 + (line,) * 4,
        check_vma=False,
    )
```

```python
import math
from functools import partial

import jax
import jax.numpy as jnp
from jax import lax
from jax.experimental import pallas as pl
from jax.experimental.pallas import tpu as pltpu
from jax.sharding import PartitionSpec as P

HEAD_DIM = 64
STEP = 5
NPARAM = 10034688
VECTORS = 10

NORM_EPS = 1e-06
BETA_FIRST = 0.5
BETA_SECOND = 0.5
AVERAGE_RATE = 0.5
MATRIX_RATE = 0.03
VECTOR_RATE = 0.3
MATRIX_DECAY = 0.05
ADAM_EPS = 1e-08
MASKED = -1e30
SCALE = HEAD_DIM ** (-0.5)
F32 = jnp.float32
BF16 = jnp.bfloat16

BLOCK = 128
WINDOW = 256
CLASSES = 8
CHUNK = 256
LONG = 40_000_000_000

VMEM = pl.BlockSpec(memory_space=pltpu.VMEM)
SMEM = pl.BlockSpec(memory_space=pltpu.SMEM)


def core_swap(value):
    return lax.ppermute(value, "heads", [(i, i ^ 1) for i in range(4)])


def x_swap(value):
    return lax.ppermute(value, "heads", [(i, i ^ 2) for i in range(4)])


def dp_swap(value, mask):
    count = lax.axis_size("dp")
    return lax.ppermute(value, "dp", [(i, i ^ mask) for i in range(count)])


def after(value, *others):
    return lax.optimization_barrier((value, *others))[0]


def together(*groups):
    flat = lax.optimization_barrier([one for group in groups for one in group])
    split, at = [], 0
    for group in groups:
        split.append(list(flat[at : at + len(group)]))
        at += len(group)
    return split


def shaped(shape, dtype):
    return jax.ShapeDtypeStruct(shape, dtype)


def local_call(name, kernel, outs, *operands, scratch=(), smem=(), extra=6, flops=0):
    held = sum(math.prod(one.shape) * jnp.dtype(one.dtype).itemsize for one in scratch)
    return pl.pallas_call(
        kernel,
        name=name,
        out_shape=list(outs),
        in_specs=[SMEM if i in smem else VMEM for i in range(len(operands))],
        out_specs=[VMEM] * len(outs),
        scratch_shapes=list(scratch),
        compiler_params=pltpu.CompilerParams(
            vmem_limit_bytes=held + extra * 2**20
        ),
        cost_estimate=pl.CostEstimate(flops=flops, bytes_accessed=0, transcendentals=0),
    )(*operands)


def dot(left, right):
    return jnp.dot(left, right, preferred_element_type=F32)


def dot_nt(left, right):
    return lax.dot_general(left, right, (((1,), (1,)), ((), ())), preferred_element_type=F32)


def dot_tn(left, right):
    return lax.dot_general(left, right, (((0,), (0,)), ((), ())), preferred_element_type=F32)


def dot_tn_exact(left, right):
    return lax.dot_general(
        left, right, (((0,), (0,)), ((), ())), preferred_element_type=F32, precision=lax.Precision.HIGHEST
    )


def chunk_loop(rows, body, size=CHUNK):
    def step(i, carry):
        body(pl.ds(pl.multiple_of(i * size, size), size))
        return carry

    lax.fori_loop(0, rows // size, step, 0)


def normed(stream):
    center = stream - jnp.mean(stream, -1, keepdims=True)
    factor = lax.rsqrt(jnp.mean(center * center, -1, keepdims=True) + NORM_EPS)
    return center * factor, factor


def norm_grad(hat, factor, gain, grad):
    scaled = grad * gain
    return factor * (
        scaled - jnp.mean(scaled, -1, keepdims=True) - hat * jnp.mean(scaled * hat, -1, keepdims=True)
    )


def column_sum(value):
    return jnp.sum(value, 0, keepdims=True)


def z_blocks(piece):
    return [piece] + [dp_swap(piece, 2 * k) for k in range(1, lax.axis_size("dp") // 2)]


def y_blocks(mine, fine=False):
    return [dp_swap(one, 1) for one in mine] if fine else [dp_swap(jnp.stack(mine), 1)]


def assemble(name, mine, other):
    half, count, fine = len(mine), lax.axis_size("dp"), len(other) > 1
    rows, columns = mine[0].shape

    def kernel(place_ref, *refs):
        out_ref = refs[-1]
        z, y = place_ref[0], place_ref[1]
        for k in range(half):
            out_ref[(z ^ k) * 2 + y] = refs[k][...]
            out_ref[(z ^ k) * 2 + (1 - y)] = refs[half + k][...] if fine else refs[half][k]

    (out,) = local_call(
        name, kernel, [shaped((count, rows, columns), mine[0].dtype)], places(), *mine, *other, smem=(0,)
    )
    return out.reshape(count * rows, columns)


def places():
    dp, heads = lax.axis_index("dp"), lax.axis_index("heads")
    return jnp.stack([dp // 2, dp % 2, heads, heads % 2]).astype(jnp.int32)


def split_rows(name, totals, fine=False):
    count = lax.axis_size("dp")
    half = count // 2
    operands, columns = [], 0
    for own, received in totals:
        rows = own.shape[0] // count
        operands += [one.reshape(count, rows, own.shape[1]) for one in (own, received) if one is not None]
        columns += own.shape[1]

    def kernel(place_ref, *refs):
        ins, outs = refs[: len(operands)], refs[len(operands) :]
        z, y = place_ref[0], place_ref[1]
        for k in range(half):
            for side in range(2):
                block = (z ^ k) * 2 + (1 - y if side == 0 else y)
                at, column = 0, 0
                for own, received in totals:
                    value = ins[at][block].astype(F32)
                    at += 1
                    if received is not None:
                        value = value + ins[at][block].astype(F32)
                        at += 1
                    part = slice(column, column + own.shape[1])
                    column += own.shape[1]
                    if side == 1:
                        outs[-1][k, :, part] = value
                    elif fine:
                        outs[k][:, part] = value.astype(BF16)
                    else:
                        outs[0][k, :, part] = value.astype(BF16)

    sends = [shaped((rows, columns), BF16)] * half if fine else [shaped((half, rows, columns), BF16)]
    outs = local_call(
        name, kernel, [*sends, shaped((half, rows, columns), F32)], places(), *operands, smem=(0,)
    )
    return outs[:-1], outs[-1]


def y_sums(keep, arrived):
    half = keep.shape[0]
    arrived = arrived if len(arrived) > 1 else [arrived[0][k] for k in range(half)]
    return [keep[k] + arrived[k].astype(F32) for k in range(half)]


def z_swaps(summed):
    return [dp_swap(summed[k].astype(BF16), 2 * k) for k in range(1, len(summed))]


def head_parts(width):
    parts = []
    for head in range(width // HEAD_DIM):
        start = head // 2 * 2 * HEAD_DIM
        stop = min(start + 2 * HEAD_DIM, width)
        parts.append((start, stop, head % 2 if stop - start == 2 * HEAD_DIM else None))
    return parts


def half_only(value, half):
    if half is None:
        return value
    lane = lax.broadcasted_iota(jnp.int32, value.shape, 1)
    return jnp.where((lane >= HEAD_DIM) == bool(half), value, jnp.zeros_like(value))


def softmax_columns(score_parts):
    top = jnp.max(score_parts[0], 0, keepdims=True)
    for one in score_parts[1:]:
        top = jnp.maximum(top, jnp.max(one, 0, keepdims=True))
    exps = [jnp.exp(one - top) for one in score_parts]
    total = sum(jnp.sum(one, 0, keepdims=True) for one in exps)
    return exps, top, total


def masked_bias(allowed):
    return jnp.where(allowed, 0.0, MASKED).astype(F32)


def head_forward(q, half, key_parts, value_parts, biases):
    q = half_only(q, half)
    scores = [dot_nt(k, q) + bias for k, bias in zip(key_parts, biases)]
    exps, top, total = softmax_columns(scores)
    out = sum(dot_tn(v, e.astype(BF16)) for v, e in zip(value_parts, exps)) / total
    if half is not None:
        out = out[half * HEAD_DIM : (half + 1) * HEAD_DIM]
    return out, top + jnp.log(total)


def head_backward(q, grad, half, key_parts, value_parts, biases, log_row):
    q, grad = half_only(q, half), half_only(grad, half)
    probs = [jnp.exp(dot_nt(k, q) + bias - log_row) for k, bias in zip(key_parts, biases)]
    grad_probs = [dot_nt(v, grad) for v in value_parts]
    delta = sum(jnp.sum(p * d, 0, keepdims=True) for p, d in zip(probs, grad_probs))
    grad_scores = [(p * (d - delta)).astype(BF16) for p, d in zip(probs, grad_probs)]
    grad_q = sum(dot_tn(k, s) for k, s in zip(key_parts, grad_scores))
    if half is not None:
        grad_q = grad_q[half * HEAD_DIM : (half + 1) * HEAD_DIM]
    grad_k = [dot(s, q) for s in grad_scores]
    grad_v = [dot(p.astype(BF16), grad) for p in probs]
    return grad_q * SCALE, grad_k, grad_v


def sort_kernel(col_ref, row_ref, tokens_ref, sorted_ref, order_ref, back_ref, code_col_ref, code_row_ref):
    count = tokens_ref.shape[0]
    key_row = (row_ref[0:1] * 128 + row_ref[2:3] + 1) * 64 + row_ref[1:2] + 1
    key_col = (col_ref[:, 0:1] * 128 + col_ref[:, 2:3] + 1) * 64 + col_ref[:, 1:2] + 1
    rank_row = jnp.zeros((1, count), jnp.int32)
    for i in range(0, count, CHUNK):
        smaller = key_col[i : i + CHUNK] < key_row
        rank_row = rank_row + jnp.sum(smaller.astype(jnp.int32), 0, keepdims=True)
    for i in range(0, count, CHUNK):
        at = slice(i, i + CHUNK)
        place = lax.broadcasted_iota(jnp.int32, (CHUNK, count), 0) + i
        order = (place == rank_row).astype(F32).astype(BF16)
        order_ref[at, :] = order
        rank_col = jnp.sum((key_row < key_col[at]).astype(jnp.int32), 1, keepdims=True)
        place = lax.broadcasted_iota(jnp.int32, (CHUNK, count), 1)
        back_ref[at, :] = (place == rank_col).astype(F32).astype(BF16)
        sorted_ref[at, :] = dot(order, tokens_ref[...]).astype(BF16)
        cols = dot(order, col_ref[...].astype(F32).astype(BF16))
        code_col_ref[at, :] = cols
        code_row_ref[:, at] = dot_nt(row_ref[...].astype(F32).astype(BF16), order)


def same_clip_patch(col_ref, row_ref, keys, queries):
    key = col_ref[keys, :]
    query = row_ref[:, queries]
    return (key[:, 0:1] * 128 + key[:, 2:3]) == (query[0:1] * 128 + query[2:3])


def temporal_window(i, count):
    first = i * BLOCK
    start = jnp.clip(first - (WINDOW - BLOCK) // 2, 0, count - WINDOW)
    return (
        pl.ds(pl.multiple_of(first, BLOCK), BLOCK),
        pl.ds(pl.multiple_of(start, (WINDOW - BLOCK) // 2), WINDOW),
    )


def time_forward_kernel(
    maps_ref, tokens_ref, back_ref, col_ref, row_ref,
    vec_ref, first_ref, inputs_ref, own_ref, far_ref, log_ref, heads_ref,
):
    count, width = tokens_ref.shape[0], own_ref.shape[1]
    columns = maps_ref.shape[1]
    lanes = maps_ref[:, columns - 128 :].astype(F32).T
    offset = 3 * width - (columns - 128)
    vec_ref[...] = lanes[offset : offset + 16]
    gain, shift = vec_ref[0:1], vec_ref[1:2]

    def project(at):
        hat, _ = normed(tokens_ref[at, :].astype(F32))
        first = (hat * gain + shift).astype(BF16)
        first_ref[at, :] = first
        inputs_ref[at, :] = dot(first, maps_ref[:, : 3 * width]).astype(BF16)

    chunk_loop(count, project)

    def step(i, carry):
        queries, keys = temporal_window(i, count)
        bias = masked_bias(same_clip_patch(col_ref, row_ref, keys, queries))
        outs, logs = [], []
        for start, stop, half in head_parts(width):
            q = inputs_ref[queries, start:stop] * BF16(SCALE)
            k = inputs_ref[keys, width + start : width + stop]
            v = inputs_ref[keys, 2 * width + start : 2 * width + stop]
            out, log = head_forward(q, half, [k], [v], [bias])
            outs.append(out)
            logs.append(log)
        heads_ref[queries, :] = jnp.concatenate(outs, 0).T.astype(BF16)
        log_ref[:, queries] = jnp.concatenate(logs + [logs[0]] * (8 - len(logs)), 0)
        return carry

    lax.fori_loop(0, count // BLOCK, step, 0)
    rows = count // 2
    for i in range(0, rows, CHUNK):
        own_ref[i : i + CHUNK, :] = dot(back_ref[i : i + CHUNK, :], heads_ref[...]).astype(BF16)
        far_ref[i : i + CHUNK, :] = dot(back_ref[rows + i : rows + i + CHUNK, :], heads_ref[...]).astype(BF16)


def time_backward_kernel(
    own_ref, far_ref, order_ref, inputs_ref, log_ref, col_ref, row_ref,
    out_ref, grad_ref, sum_ref,
):
    count, width = inputs_ref.shape[0], own_ref.shape[1]
    rows = count // 2
    for i in range(0, count, CHUNK):
        grad_ref[i : i + CHUNK, :] = (
            dot(order_ref[i : i + CHUNK, :rows], own_ref[...]) + dot(order_ref[i : i + CHUNK, rows:], far_ref[...])
        ).astype(BF16)
    sum_ref[...] = jnp.zeros_like(sum_ref)

    def step(i, carry):
        queries, keys = temporal_window(i, count)
        bias = masked_bias(same_clip_patch(col_ref, row_ref, keys, queries))
        grad_qs, pairs = [], {}
        for head, (start, stop, half) in enumerate(head_parts(width)):
            q = inputs_ref[queries, start:stop] * BF16(SCALE)
            k = inputs_ref[keys, width + start : width + stop]
            v = inputs_ref[keys, 2 * width + start : 2 * width + stop]
            grad_q, grad_k, grad_v = head_backward(
                q, grad_ref[queries, start:stop], half, [k], [v], [bias], log_ref[head : head + 1, queries]
            )
            grad_qs.append(grad_q)
            before = pairs.get((start, stop))
            pairs[start, stop] = (
                (grad_k[0], grad_v[0]) if before is None else (before[0] + grad_k[0], before[1] + grad_v[0])
            )
        out_ref[queries, :width] = jnp.concatenate(grad_qs, 0).T.astype(BF16)
        for (start, stop), (grad_k, grad_v) in pairs.items():
            sum_ref[keys, start:stop] += grad_k
            sum_ref[keys, width + start : width + stop] += grad_v
        return carry

    lax.fori_loop(0, count // BLOCK, step, 0)

    def store(at):
        out_ref[at, width:] = sum_ref[at, :].astype(BF16)

    chunk_loop(count, store)


def space_window(i, core, rows):
    first = core * rows + i * BLOCK
    start = jnp.clip(first - (WINDOW - BLOCK) // 2, 0, 2 * rows - WINDOW)
    return (
        pl.ds(pl.multiple_of(i * BLOCK, BLOCK), BLOCK),
        pl.ds(pl.multiple_of(first, BLOCK), BLOCK),
        pl.ds(pl.multiple_of(start, (WINDOW - BLOCK) // 2), WINDOW),
    )


def whole_pairs(core, pairs_ref, got_ref, whole_ref):
    rows, width = pairs_ref.shape[0], pairs_ref.shape[1] // 4
    whole_ref[pl.ds(pl.multiple_of(core * rows, rows), rows), :] = pairs_ref[...]
    there = pl.ds(pl.multiple_of((1 - core) * rows, rows), rows)
    for i, j in enumerate((1, 0, 3, 2)):
        whole_ref[there, i * width : (i + 1) * width] = got_ref[:, j * width : (j + 1) * width]


def class_rows(row):
    number = lax.broadcasted_iota(jnp.int32, (CLASSES, row.shape[1]), 0)
    return (row[0:1] == number) & (row[1:2] < 0)


def space_biases(col_ref, row_ref, queries, keys):
    key, query = col_ref[keys, :], row_ref[:, queries]
    frame = jnp.where(key[:, 1:2] < 0, -1, key[:, 0:1] * 128 + key[:, 1:2]) == query[0:1] * 128 + query[1:2]
    number = lax.broadcasted_iota(jnp.int32, (CLASSES, BLOCK), 0)
    return [masked_bias(frame & (query[1:2] >= 0)), masked_bias(number == query[0:1])]


def class_allowed(row_ref):
    number = lax.broadcasted_iota(jnp.int32, (CLASSES, row_ref.shape[1]), 0)
    return row_ref[0:1] == number


def space_forward_kernel(
    place_ref, q_ref, pairs_ref, got_ref, col_ref, row_ref, out_own_ref, out_far_ref,
    heads_ref, log_ref, class_log_ref, part_ref, whole_ref, class_ref,
):
    core = place_ref[3]
    rows, width = q_ref.shape
    whole_pairs(core, pairs_ref, got_ref, whole_ref)
    here = pl.ds(pl.multiple_of(core * rows, rows), rows)
    classes = class_rows(row_ref[...]).astype(F32).astype(BF16)
    own_classes = class_rows(row_ref[:, here]).astype(F32).astype(BF16)
    class_ref[...] = dot(classes, whole_ref[...]).astype(BF16)
    parts = head_parts(width)

    def step(i, carry):
        local, queries, keys = space_window(i, core, rows)
        biases = space_biases(col_ref, row_ref, queries, keys)
        outs, logs = [], []
        for start, stop, half in parts:
            out, log = head_forward(
                q_ref[local, start:stop] * BF16(SCALE),
                half,
                [whole_ref[keys, start:stop], class_ref[:, start:stop]],
                [whole_ref[keys, width + start : width + stop], class_ref[:, width + start : width + stop]],
                biases,
            )
            outs.append(out)
            logs.append(log)
        heads_ref[local, :] = jnp.concatenate(outs, 0).T.astype(BF16)
        log_ref[:, local] = jnp.concatenate(logs + [logs[0]] * (8 - len(logs)), 0)
        return carry

    lax.fori_loop(0, rows // BLOCK, step, 0)

    bias = masked_bias(class_allowed(row_ref))
    class_q = dot(own_classes, q_ref[...]).astype(BF16) * BF16(SCALE)
    outs, logs = [], []
    for start, stop, half in parts:
        scores = dot_nt(half_only(class_q[:, start:stop], half), whole_ref[:, start:stop]) + bias
        top = jnp.max(scores, 1, keepdims=True)
        exps = jnp.exp(scores - top)
        total = jnp.sum(exps, 1, keepdims=True)
        out = dot(exps.astype(BF16), whole_ref[:, width + start : width + stop]) / total
        if half:
            outs[-1] = jnp.where(lax.broadcasted_iota(jnp.int32, out.shape, 1) >= HEAD_DIM, out, outs[-1])
        else:
            outs.append(out)
        logs.append(top + jnp.log(total))
    class_log_ref[...] = jnp.concatenate(logs + [logs[0]] * (8 - len(logs)), 1)
    class_out = jnp.concatenate(outs, 1).astype(BF16)
    is_class = col_ref[here, 1:2] < 0

    def replace(at):
        back = dot_tn(own_classes, class_out).astype(BF16)
        heads_ref[...] = jnp.where(is_class, back, heads_ref[...])

    replace(None)
    group = width // 2

    def project(at):
        part_ref[at, :] = (
            dot_nt(heads_ref[at, :group], out_own_ref[:, 3 * group :])
            + dot_nt(heads_ref[at, group:], out_far_ref[:, 3 * group :])
        ).astype(BF16)

    chunk_loop(rows, project)


def space_back_in_kernel(
    part_ref, got_ref, stream_ref, vec_ref, dy_ref, out_own_ref, out_far_ref, grad_ref, low_ref, sums_ref, heads_ref
):
    group = heads_ref.shape[1] // 2
    gain = vec_ref[7:8]
    sums_ref[...] = jnp.zeros_like(sums_ref)

    def through_norm(at):
        grad = part_ref[at, :].astype(F32) + got_ref[at, :].astype(F32)
        hat, factor = normed(stream_ref[at, :])
        dy = dy_ref[at, :].astype(F32)
        dx = dy + norm_grad(hat, factor, gain, grad)
        grad_ref[at, :] = dx
        low = dx.astype(BF16)
        low_ref[at, :] = low
        heads_ref[at, :group] = dot(low, out_own_ref[:, 3 * group :]).astype(BF16)
        heads_ref[at, group:] = dot(low, out_far_ref[:, 3 * group :]).astype(BF16)
        sums_ref[0:4] += jnp.concatenate(
            [column_sum(dx), column_sum(grad * hat), column_sum(grad), column_sum(dy)], 0
        )

    chunk_loop(grad_ref.shape[0], through_norm)


def space_backward_kernel(
    place_ref, heads_ref, q_ref, pairs_ref, got_ref, log_ref, class_log_ref, col_ref, row_ref,
    dq_ref, keep_ref, send_ref,
    whole_ref, class_ref, total_ref, class_total_ref, class_dq_ref,
):
    core = place_ref[3]
    rows, width = q_ref.shape
    whole_pairs(core, pairs_ref, got_ref, whole_ref)
    here = pl.ds(pl.multiple_of(core * rows, rows), rows)
    there = pl.ds(pl.multiple_of((1 - core) * rows, rows), rows)
    classes = class_rows(row_ref[...]).astype(F32)
    own_classes = class_rows(row_ref[:, here]).astype(F32).astype(BF16)
    class_ref[...] = dot(classes.astype(BF16), whole_ref[...]).astype(BF16)
    class_total_ref[...] = jnp.zeros_like(class_total_ref)
    parts = head_parts(width)
    is_class_row = row_ref[1:2, here] < 0

    bias = masked_bias(class_allowed(row_ref))
    class_q = dot(own_classes, q_ref[...]).astype(BF16) * BF16(SCALE)
    class_g = dot(own_classes, heads_ref[...]).astype(BF16)
    for head, (start, stop, half) in enumerate(parts):
        keys, values = whole_ref[:, start:stop], whole_ref[:, width + start : width + stop]
        q, grad = half_only(class_q[:, start:stop], half), half_only(class_g[:, start:stop], half)
        probs = jnp.exp(dot_nt(q, keys) + bias - class_log_ref[:, head : head + 1])
        grad_probs = dot_nt(grad, values)
        grad_scores = (probs * (grad_probs - jnp.sum(probs * grad_probs, 1, keepdims=True))).astype(BF16)
        grad_q = half_only(dot(grad_scores, keys) * SCALE, half).astype(BF16)
        grad_k, grad_v = dot_tn(grad_scores, q), dot_tn(probs.astype(BF16), grad)
        if half:
            class_dq_ref[:, start:stop] += grad_q
            total_ref[:, start:stop] += grad_k
            total_ref[:, width + start : width + stop] += grad_v
        else:
            class_dq_ref[:, start:stop] = grad_q
            total_ref[:, start:stop] = grad_k
            total_ref[:, width + start : width + stop] = grad_v

    def step(i, carry):
        local, queries, keys = space_window(i, core, rows)
        biases = space_biases(col_ref, row_ref, queries, keys)
        is_class = row_ref[1:2, queries] < 0
        grad_qs, pairs = [], {}
        for head, (start, stop, half) in enumerate(parts):
            log_row = jnp.where(is_class, -MASKED, log_ref[head : head + 1, local])
            grad_q, grad_k, grad_v = head_backward(
                q_ref[local, start:stop] * BF16(SCALE),
                heads_ref[local, start:stop],
                half,
                [whole_ref[keys, start:stop], class_ref[:, start:stop]],
                [whole_ref[keys, width + start : width + stop], class_ref[:, width + start : width + stop]],
                biases,
                log_row,
            )
            grad_qs.append(grad_q)
            new = grad_k + grad_v
            before = pairs.get((start, stop))
            pairs[start, stop] = new if before is None else [a + b for a, b in zip(before, new)]
        dq_ref[local, :] = jnp.concatenate(grad_qs, 0).T.astype(BF16)
        for (start, stop), (frame_k, class_k, frame_v, class_v) in pairs.items():
            total_ref[keys, start:stop] += frame_k
            total_ref[keys, width + start : width + stop] += frame_v
            class_total_ref[:, start:stop] += class_k
            class_total_ref[:, width + start : width + stop] += class_v
        return carry

    lax.fori_loop(0, rows // BLOCK, step, 0)
    dq_ref[...] = jnp.where(
        col_ref[here, 1:2] < 0, dot_tn(own_classes, class_dq_ref[...]).astype(BF16), dq_ref[...]
    )
    total_ref[...] += dot_tn_exact(classes, class_total_ref[...])
    keep_ref[...] = total_ref[here, :]
    send_ref[...] = total_ref[there, :].astype(BF16)


def mix_kernel(place_ref, out_ref, own_ref, x_ref, core_ref, vec_ref, mix_ref, fused_ref, bias_ref):
    place = place_ref[2]
    width = out_ref.shape[1]
    mix_ref[0] = own_ref[...]
    mix_ref[1] = core_ref[:, :width]
    mix_ref[2] = x_ref[...]
    mix_ref[3] = core_ref[:, width:]
    total, bias = 0.0, 0.0
    low = vec_ref[...].astype(BF16)
    for j in range(4):
        block = mix_ref[place ^ j]
        total = total + dot(block, out_ref[j * width : (j + 1) * width, :])
        bias = bias + dot_nt(low[:, j * width : (j + 1) * width], block)
    fused_ref[...] = total.astype(BF16)
    bias_ref[...] = bias[2:3] + vec_ref[3:4]


def time_out_kernel(own_ref, got_ref, fused_ref, far_ref, part_ref):
    def project(at):
        part_ref[at, :] = (dot_nt(own_ref[at, :], fused_ref[...]) + dot_nt(got_ref[at, :], far_ref[...])).astype(BF16)

    chunk_loop(part_ref.shape[0], project)


def norm_in_kernel(gain_row, before_ref, part_ref, got_ref, shift_ref, vec_ref, stream_ref, normed_ref):
    gain, shift = vec_ref[gain_row : gain_row + 1], vec_ref[gain_row + 1 : gain_row + 2]

    def body(at):
        stream = (
            before_ref[at, :].astype(F32)
            + (part_ref[at, :].astype(F32) + got_ref[at, :].astype(F32))
            + shift_ref[0:1]
        )
        stream_ref[at, :] = stream
        hat, _ = normed(stream)
        normed_ref[at, :] = (hat * gain + shift).astype(BF16)

    chunk_loop(stream_ref.shape[0], body)


def space_in_kernel(second_ref, own_ref, far_ref, q_ref, pairs_ref):
    width = q_ref.shape[1] // 2

    def project(at):
        for g, maps_ref in enumerate((own_ref, far_ref)):
            inputs = dot(second_ref[at, :], maps_ref[:, : 3 * width]).astype(BF16)
            q_ref[at, g * width : (g + 1) * width] = inputs[:, :width]
            pairs_ref[at, g * width : (g + 1) * width] = inputs[:, width : 2 * width]
            pairs_ref[at, (2 + g) * width : (3 + g) * width] = inputs[:, 2 * width :]

    chunk_loop(q_ref.shape[0], project)


def gelu_parts(pre):
    cdf = 0.5 * (1.0 + lax.erf(pre * (0.5**0.5)))
    slope = cdf + pre * jnp.exp(-0.5 * pre * pre) * (1.0 / math.sqrt(2.0 * math.pi))
    return pre * cdf, slope


def feed_kernel(
    third_ref, dy_ref, up_ref, up_far_ref, down_ref, down_far_ref, activ_ref, grad_ref, back_ref
):
    hidden = activ_ref.shape[1] // 2

    def project(at):
        back = 0.0
        for g, (ups_ref, downs_ref) in enumerate(((up_ref, down_ref), (up_far_ref, down_far_ref))):
            act, slope = gelu_parts(dot(third_ref[at, :], ups_ref[...]))
            part = slice(g * hidden, (g + 1) * hidden)
            activ_ref[at, part] = act.astype(BF16)
            grad = (dot(dy_ref[at, :], downs_ref[...]) * slope).astype(BF16)
            grad_ref[at, part] = grad
            back = back + dot_nt(grad, ups_ref[...])
        back_ref[at, :] = back.astype(BF16)

    chunk_loop(third_ref.shape[0], project)


def feed_out_kernel(activ_ref, own_ref, far_ref, part_ref):
    hidden = activ_ref.shape[1] // 2

    def project(at):
        part_ref[at, :] = (
            dot_nt(activ_ref[at, :hidden], own_ref[...]) + dot_nt(activ_ref[at, hidden:], far_ref[...])
        ).astype(BF16)

    chunk_loop(part_ref.shape[0], project)


def outer_kernel(left_ref, right_ref, own_ref, far_ref):
    hidden = own_ref.shape[1]
    for g, ref in ((1, far_ref), (0, own_ref)):
        ref[...] = dot_tn(left_ref[...], right_ref[:, g * hidden : (g + 1) * hidden]).astype(BF16)


def space_back_kernel(dq_ref, keep_ref, got_ref, own_ref, far_ref, grad_own_ref, grad_far_ref, part_ref):
    width = dq_ref.shape[1] // 2

    def project(at):
        total = 0.0
        for g, (maps_ref, grad_ref) in enumerate(((own_ref, grad_own_ref), (far_ref, grad_far_ref))):
            grad_ref[at, :width] = dq_ref[at, g * width : (g + 1) * width]
            for i in (1, 2):
                mine = slice((2 * i - 2 + g) * width, (2 * i - 1 + g) * width)
                theirs = slice((2 * i - 1 - g) * width, (2 * i - g) * width)
                grad_ref[at, i * width : (i + 1) * width] = (
                    keep_ref[at, mine] + got_ref[at, theirs].astype(F32)
                ).astype(BF16)
            total = total + dot_nt(grad_ref[at, :], maps_ref[:, : 3 * width])
        part_ref[at, :] = total.astype(BF16)

    chunk_loop(part_ref.shape[0], project)


def space_grads_kernel(second_ref, own_grad_ref, far_grad_ref, low_ref, heads_ref, own_ref, far_ref):
    width = heads_ref.shape[1] // 2
    for g, grad_ref, ref in ((1, far_grad_ref, far_ref), (0, own_grad_ref, own_ref)):
        ref[:, : 3 * width] = dot_tn(second_ref[...], grad_ref[...]).astype(BF16)
        ref[:, 3 * width :] = dot_tn(low_ref[...], heads_ref[:, g * width : (g + 1) * width]).astype(BF16)


def time_back_in_kernel(
    part_ref, got_ref, stream_ref, vec_ref, before_ref, fused_ref, far_ref,
    grad_ref, low_ref, sums_ref, own_ref, send_ref,
):
    gain = vec_ref[4:5]
    sums_ref[...] = jnp.zeros_like(sums_ref)

    def through_norm(at):
        grad = part_ref[at, :].astype(F32) + got_ref[at, :].astype(F32)
        hat, factor = normed(stream_ref[at, :])
        dx = before_ref[at, :] + norm_grad(hat, factor, gain, grad)
        grad_ref[at, :] = dx
        low = dx.astype(BF16)
        low_ref[at, :] = low
        own_ref[at, :] = dot(low, fused_ref[...]).astype(BF16)
        send_ref[at, :] = dot(low, far_ref[...]).astype(BF16)
        sums_ref[0:4] += jnp.concatenate(
            [column_sum(low.astype(F32)), column_sum(dx), column_sum(grad * hat), column_sum(grad)], 0
        )

    chunk_loop(grad_ref.shape[0], through_norm)


def time_grads_kernel(place_ref, first_ref, grad_ref, *refs):
    sends, keep_ref, total_ref = refs[:-2], refs[-2], refs[-1]
    half, rows, columns = keep_ref.shape
    z, y = place_ref[0], place_ref[1]
    total_ref[...] = dot_tn(first_ref[...], grad_ref[...])
    for k in range(half):
        mine = pl.ds(pl.multiple_of(((z ^ k) * 2 + y) * rows, 8), rows)
        theirs = pl.ds(pl.multiple_of(((z ^ k) * 2 + (1 - y)) * rows, 8), rows)
        sends[k][...] = total_ref[theirs, :].astype(BF16)
        keep_ref[k] = total_ref[mine, :]


def time_back_kernel(
    grad_ref, maps_ref, tokens_ref, back_ref, bias_ref, one_ref, two_ref, own_ref, far_ref, sums_ref, sorted_ref
):
    count, width = tokens_ref.shape[0], grad_ref.shape[1] // 3
    sums_ref[...] = jnp.zeros_like(sums_ref)
    sums_ref[2:3] = 0.5 * bias_ref[0:1]
    sums_ref[3:6] = 0.5 * one_ref[1:4]
    sums_ref[6:10] = 0.5 * two_ref[0:4]
    sums_ref[10:11] = 0.5 * one_ref[0:1]

    def project(at):
        grad = dot_nt(grad_ref[at, :], maps_ref[:, : 3 * width])
        hat, _ = normed(tokens_ref[at, :].astype(F32))
        sums_ref[0:2] += jnp.concatenate([column_sum(grad * hat), column_sum(grad)], 0)
        sorted_ref[at, :] = grad.astype(BF16)

    chunk_loop(count, project)
    rows = count // 2
    for i in range(0, rows, CHUNK):
        far_ref[i : i + CHUNK, :] = dot(back_ref[rows + i : rows + i + CHUNK, :], sorted_ref[...]).astype(BF16)
    for i in range(0, rows, CHUNK):
        own_ref[i : i + CHUNK, :] = dot(back_ref[i : i + CHUNK, :], sorted_ref[...]).astype(BF16)


def input_grad_kernel(part_ref, got_ref, tokens_ref, vec_ref, before_ref, out_ref):
    gain = vec_ref[0:1]

    def through_norm(at):
        grad = part_ref[at, :].astype(F32) + got_ref[at, :].astype(F32)
        hat, factor = normed(tokens_ref[at, :].astype(F32))
        out_ref[at, :] = before_ref[at, :] + norm_grad(hat, factor, gain, grad)

    chunk_loop(out_ref.shape[0], through_norm)


def layer_out_kernel(stream_ref, part_ref, got_ref, vec_ref, out_ref):
    out_ref[...] = stream_ref[...] + (part_ref[...].astype(F32) + got_ref[...].astype(F32)) + vec_ref[9:10]


def whole_rows_kernel(place_ref, own_ref, got_ref, out_ref):
    core = place_ref[3]
    rows = own_ref.shape[0]
    out_ref[pl.ds(pl.multiple_of(core * rows, rows), rows), :] = own_ref[...]
    out_ref[pl.ds(pl.multiple_of((1 - core) * rows, rows), rows), :] = got_ref[...]


def fused_grads_kernel(low_ref, heads_ref, got_heads_ref, own_ref, far_ref):
    far_ref[...] = dot_tn(low_ref[...], got_heads_ref[...]).astype(BF16)
    own_ref[...] = dot_tn(low_ref[...], heads_ref[...])


def mix_grads_kernel(
    place_ref, fused_ref, got_ref, mix_ref, sums_ref, grad_out_ref, total_ref, bias_ref
):
    place = place_ref[2]
    width = fused_ref.shape[1]
    fused = (fused_ref[...] + got_ref[...].astype(F32)).astype(BF16)
    total_ref[...] = fused
    for j in range(4):
        block = mix_ref[place ^ j]
        grad_out_ref[j * width : (j + 1) * width, :] = dot_tn(block, fused).astype(BF16)
        bias_ref[:, j * width : (j + 1) * width] = dot(sums_ref[...].astype(BF16), block)


def mix_shard_kernel(place_ref, fused_ref, out_ref, keep_ref, send_ref):
    place = place_ref[2]
    width = out_ref.shape[1]
    fused = fused_ref[...].astype(BF16)
    for m in range(4):
        rows = out_ref[pl.ds(pl.multiple_of((place ^ m) * width, width), width), :]
        part = dot_nt(fused, rows)
        ref = send_ref if m % 2 else keep_ref
        ref[:, m // 2 * width : (m // 2 + 1) * width] = part.astype(ref.dtype)


def whole_grad_kernel(counts, *refs):
    out_ref, square_ref = refs[-2:]
    at, column, square = 0, 0, 0.0
    for count in counts:
        value = refs[at][...].astype(F32)
        for ref in refs[at + 1 : at + count]:
            value = value + ref[...].astype(F32)
        at += count
        out_ref[:, column : column + value.shape[1]] = value
        column += value.shape[1]
        square = square + jnp.sum(value * value)
    square_ref[...] = jnp.full(square_ref.shape, square, F32)


def adam_update(master, first_moment, second_moment, average, gradient, factor, rate, decay):
    clipped = gradient * factor
    first_new = BETA_FIRST * first_moment + (1.0 - BETA_FIRST) * clipped
    second_new = BETA_SECOND * second_moment + (1.0 - BETA_SECOND) * clipped * clipped
    first_hat = first_new / (1.0 - BETA_FIRST**STEP)
    second_hat = second_new / (1.0 - BETA_SECOND**STEP)
    master_new = master - rate * (first_hat / (jnp.sqrt(second_hat) + ADAM_EPS) + decay * master)
    average_new = AVERAGE_RATE * average + (1.0 - AVERAGE_RATE) * master_new
    return (master_new, first_new, second_new, average_new)


def local(
    tokens,
    cotangent,
    clip_ids,
    frame_ids,
    patch_ids,
    weights,
    weights_m,
    weights_v,
    weights_ema,
    vectors,
    vectors_m,
    vectors_v,
    vectors_ema,
):
    group_count = lax.axis_size("heads")
    core = lax.axis_index("heads") % 2
    place = places()
    count, features = tokens.shape
    width = features // group_count
    hidden = (weights.shape[1] - 9 * width) // 2
    rows = count // 2
    half = lax.axis_size("dp") // 2
    shard = weights.shape[0]

    def in_order(value):
        return jnp.concatenate(
            [lax.dynamic_slice_in_dim(value, (core ^ k) * rows, rows, 0) for k in range(2)], 0
        )

    def id_arrays(values):
        return jnp.stack(values + [values[0]] * 5, 1), jnp.stack(values + [values[0]] * 5, 0)

    ids = [one[0] for one in (clip_ids, frame_ids, patch_ids)]
    space_ids = id_arrays(ids)
    order_col, order_row = id_arrays([in_order(one) for one in ids])
    tokens_all = in_order(tokens)
    tokens_own = tokens_all[:rows]
    dy = lax.dynamic_slice_in_dim(cotangent, core * rows, rows, 0)

    wide = lambda n, dtype: shaped((rows, n), dtype)
    tokens_sorted, order, back, time_col, time_row = local_call(
        "sort_rows",
        sort_kernel,
        [
            shaped((count, features), BF16),
            shaped((count, count), BF16),
            shaped((count, count), BF16),
            shaped((count, 8), F32),
            shaped((8, count), F32),
        ],
        order_col, order_row, tokens_all,
    )

    low = weights.astype(BF16)
    spare = jnp.zeros((shard, -(-(3 * width + 16) // 128) * 128 - 3 * width - VECTORS), BF16)
    mix_z = z_blocks(low[:, 4 * width : 5 * width])
    time_z = z_blocks(jnp.concatenate([low[:, : 3 * width], vectors.astype(BF16).T, spare], 1))
    mix_y = y_blocks(mix_z)
    time_z, mix_y, (space_col, space_row, _) = together(time_z, mix_y, [*space_ids, tokens_sorted])
    mix_map = assemble("gather_mix", mix_z, mix_y)
    mix_x = x_swap(mix_map)
    time_y = y_blocks(time_z, True)
    out_z = z_blocks(after(low[:, 3 * width : 4 * width], *time_z))
    time_y, out_z, (mix_map, mix_x) = together(time_y, out_z, [mix_map, mix_x])
    time_maps = assemble("gather_time", time_z, time_y)
    mix_core = core_swap(jnp.concatenate([mix_map, mix_x], 1))
    out_y = y_blocks(out_z)
    space_z = z_blocks(after(low[:, 5 * width : 9 * width], *out_z))

    vec, first, time_inputs, time_own, time_send, time_logs = local_call(
        "time_forward",
        time_forward_kernel,
        [
            shaped((16, features), F32),
            shaped((count, features), BF16),
            shaped((count, 3 * width), BF16),
            wide(width, BF16),
            wide(width, BF16),
            shaped((8, count), F32),
        ],
        time_maps, tokens_sorted, back, time_col, time_row,
        scratch=[pltpu.VMEM((count, width), BF16)],
    )
    out_y, space_z, (mix_core, time_send) = together(out_y, space_z, [mix_core, time_send])
    time_got = core_swap(time_send)
    out_map = assemble("gather_out", out_z, out_y)

    mix_blocks, fused, mix_bias = local_call(
        "mix_maps",
        mix_kernel,
        [
            shaped((group_count, features, width), BF16),
            shaped((features, width), BF16),
            shaped((1, features), F32),
        ],
        place, out_map, mix_map, mix_x, mix_core, vec,
        smem=(0,),
    )
    fused_far = core_swap(fused)
    space_y = y_blocks(space_z)
    up_z = z_blocks(after(low[:, 9 * width : 9 * width + hidden], *space_z))
    (time_part,) = local_call("time_out", time_out_kernel, [wide(features, BF16)], time_own, time_got, fused, fused_far)
    stream_one, second = local_call(
        "space_norm",
        partial(norm_in_kernel, 4),
        [wide(features, F32), wide(features, BF16)],
        tokens_own, time_part, x_swap(time_part), mix_bias, vec,
        flops=LONG,
    )

    space_own = assemble("gather_space", space_z, space_y)
    space_far = core_swap(space_own)
    space_q, space_pairs = local_call(
        "space_in",
        space_in_kernel,
        [wide(2 * width, BF16), wide(4 * width, BF16)],
        second, space_own, space_far,
    )
    up_z, (space_q, space_pairs) = together(up_z, [space_q, space_pairs])
    up_y = y_blocks(up_z)
    down_z = z_blocks(after(low[:, 9 * width + hidden :], *up_z))
    space_got = core_swap(space_pairs)
    space_heads, space_logs, class_logs, space_part = local_call(
        "space_forward",
        space_forward_kernel,
        [wide(2 * width, BF16), shaped((8, rows), F32), shaped((8, CLASSES), F32), wide(features, BF16)],
        place, space_q, space_pairs, space_got, space_col, space_row, space_own, space_far,
        smem=(0,),
        scratch=[pltpu.VMEM((count, 4 * width), BF16), pltpu.VMEM((CLASSES, 4 * width), BF16)],
    )
    up_y, down_z, (space_part,) = together(up_y, down_z, [space_part])
    stream_two, third = local_call(
        "feed_norm",
        partial(norm_in_kernel, 7),
        [wide(features, F32), wide(features, BF16)],
        stream_one, space_part, x_swap(space_part), vec[6:8], vec,
        flops=LONG,
    )

    up_own = assemble("gather_up", up_z, up_y)
    up_far = core_swap(up_own)
    down_own = assemble("gather_down", down_z, y_blocks(down_z))
    down_far = core_swap(down_own)
    activ, grad_pre, third_part = local_call(
        "feed",
        feed_kernel,
        [wide(2 * hidden, BF16), wide(2 * hidden, BF16), wide(features, BF16)],
        third, dy, up_own, up_far, down_own, down_far,
    )
    third_part_got = x_swap(third_part)
    outer = [shaped((features, hidden), BF16)] * 2
    up_grad, up_grad_far = local_call("up_grads", outer_kernel, outer, third, grad_pre)
    down_grad, down_grad_far = local_call("down_grads", outer_kernel, outer, dy, activ)
    (feed_part,) = local_call("feed_out", feed_out_kernel, [wide(features, BF16)], activ, down_own, down_far)
    up_sends, up_keep = split_rows("split_up", [(up_grad, core_swap(up_grad_far))])
    down_sends, down_keep = split_rows("split_down", [(down_grad, core_swap(down_grad_far))])

    grad_two, grad_two_low, sums_two, space_grad_heads = local_call(
        "space_back_in",
        space_back_in_kernel,
        [wide(features, F32), wide(features, BF16), shaped((8, features), F32), wide(2 * width, BF16)],
        third_part, third_part_got, stream_two, vec, dy, space_own, space_far,
        flops=LONG,
    )
    up_sends, down_sends, (space_grad_heads, feed_part) = together(
        up_sends, down_sends, [space_grad_heads, feed_part]
    )
    up_y = [dp_swap(one, 1) for one in up_sends]
    space_dq, space_keep, space_send = local_call(
        "space_backward",
        space_backward_kernel,
        [wide(2 * width, BF16), wide(4 * width, F32), wide(4 * width, BF16)],
        place, space_grad_heads, space_q, space_pairs, space_got, space_logs, class_logs, space_col, space_row,
        smem=(0,),
        scratch=[
            pltpu.VMEM((count, 4 * width), BF16),
            pltpu.VMEM((CLASSES, 4 * width), BF16),
            pltpu.VMEM((count, 4 * width), F32),
            pltpu.VMEM((CLASSES, 4 * width), F32),
            pltpu.VMEM((CLASSES, 2 * width), BF16),
        ],
    )
    up_y, (space_send,) = together(up_y, [space_send])
    space_got_grads = core_swap(space_send)
    up_sums = y_sums(up_keep, up_y)
    up_shards = z_swaps(up_sums)
    down_y = [dp_swap(after(one, *up_y), 1) for one in down_sends]
    grad_space, grad_space_far, second_part = local_call(
        "space_back",
        space_back_kernel,
        [wide(3 * width, BF16), wide(3 * width, BF16), wide(features, BF16)],
        space_dq, space_keep, space_got_grads, space_own, space_far,
    )
    second_part_got = x_swap(second_part)
    space_grad, space_grad_far = local_call(
        "space_grads",
        space_grads_kernel,
        [shaped((features, 4 * width), BF16)] * 2,
        second, grad_space, grad_space_far, grad_two_low, space_heads,
    )
    space_sends, space_own_rows = split_rows("split_space", [(space_grad, core_swap(space_grad_far))])

    grad_one, grad_one_low, sums_one, time_grad_own, time_grad_send = local_call(
        "time_back_in",
        time_back_in_kernel,
        [
            wide(features, F32),
            wide(features, BF16),
            shaped((8, features), F32),
            wide(width, BF16),
            wide(width, BF16),
        ],
        second_part, second_part_got, stream_one, vec, grad_two, fused, fused_far,
    )
    down_y, up_shards, space_sends, (time_grad_own, time_grad_send, grad_one_low) = together(
        down_y, up_shards, space_sends, [time_grad_own, time_grad_send, grad_one_low]
    )
    down_sums = y_sums(down_keep, down_y)
    down_shards = z_swaps(down_sums)
    space_y = [dp_swap(one, 1) for one in space_sends]
    time_grad_got = core_swap(time_grad_send)
    fused_grad, fused_grad_far = local_call(
        "fused_grads",
        fused_grads_kernel,
        [shaped((features, width), F32), shaped((features, width), BF16)],
        grad_one_low, time_own, time_got,
    )
    fused_grad_got = core_swap(fused_grad_far)
    grad_time_out, fused_total, bias_grad = local_call(
        "mix_grads",
        mix_grads_kernel,
        [shaped((features, width), BF16), shaped((features, width), BF16), shaped((8, features), F32)],
        place, fused_grad, fused_grad_got, mix_blocks, sums_one,
        smem=(0,),
    )
    out_sends, out_keep = split_rows("split_out", [(grad_time_out, None), (fused_total, None)])
    out_sends, (time_grad_own, time_grad_got) = together(out_sends, [time_grad_own, time_grad_got])
    out_y = [dp_swap(one, 1) for one in out_sends]
    (grad_time,) = local_call(
        "time_backward",
        time_backward_kernel,
        [shaped((count, 3 * width), BF16)],
        time_grad_own, time_grad_got, order, time_inputs, time_logs, time_col, time_row,
        scratch=[pltpu.VMEM((count, width), BF16), pltpu.VMEM((count, 2 * width), F32)],
    )
    down_shards, space_y, out_y, (grad_time,) = together(down_shards, space_y, out_y, [grad_time])
    *time_sends, time_keep = local_call(
        "time_grads",
        time_grads_kernel,
        [shaped((shard, 3 * width), BF16)] * half + [shaped((half, shard, 3 * width), F32)],
        place, first, grad_time,
        smem=(0,),
        scratch=[pltpu.VMEM((features, 3 * width), F32)],
    )
    time_sends, (grad_time,) = together(time_sends, [grad_time])
    time_y = [dp_swap(one, 1) for one in time_sends]
    space_sums, out_sums = y_sums(space_own_rows, space_y), y_sums(out_keep, out_y)
    space_shards, out_shards = z_swaps(space_sums), z_swaps(out_sums)
    first_own, first_send, vector_sum = local_call(
        "time_back",
        time_back_kernel,
        [wide(features, BF16), wide(features, BF16), shaped((16, features), F32)],
        grad_time, time_maps, tokens_sorted, back, bias_grad, sums_one, sums_two,
        scratch=[pltpu.VMEM((count, features), BF16)],
    )
    time_y, (first_send, vector_sum) = together(time_y, [first_send, vector_sum])
    time_sums = y_sums(time_keep, time_y)
    time_shards = z_swaps(time_sums)
    first_part = (first_own.astype(F32) + core_swap(first_send).astype(F32)).astype(BF16)
    first_part_got = x_swap(first_part)
    feed_part_got = x_swap(after(feed_part, first_part_got))

    out_width = 2 * width
    out_total = sum([one.astype(F32) for one in out_shards], out_sums[0])
    mix_keep, mix_send = local_call(
        "mix_shard",
        mix_shard_kernel,
        [shaped((shard, out_width), F32), shaped((shard, out_width), BF16)],
        place, out_total[:, width:], out_map,
        smem=(0,),
    )
    mix_sum = mix_keep + core_swap(mix_send).astype(F32)
    mix_total = mix_sum[:, :width] + x_swap(mix_sum[:, width:].astype(BF16)).astype(F32)

    dp_count = lax.axis_size("dp")

    def dp_sum(value):
        step = 1
        while step < dp_count:
            value = value + dp_swap(value, step)
            step *= 2
        return value

    def heads_sum(value):
        value = value + core_swap(value)
        return value + x_swap(value)

    vector_whole = dp_sum(heads_sum(vector_sum))
    vector_all = vector_whole[:VECTORS]
    vector_part = lax.dynamic_slice_in_dim(vector_whole, lax.axis_index("dp") * shard, shard, 1)
    vector_grad, low_sum = vector_part[:VECTORS], vector_part[10]
    bias_part = lax.dynamic_slice_in_dim(vec[2], lax.axis_index("heads") * width, width, 0)
    mix_total = mix_total + low_sum[:, None] * bias_part[None, :]
    pieces = [
        [time_sums[0], *time_shards],
        [out_total[:, :width]],
        [mix_total],
        [space_sums[0], *space_shards],
        [up_sums[0], *up_shards],
        [down_sums[0], *down_shards],
    ]
    weight_grad, square = local_call(
        "whole_grad",
        partial(whole_grad_kernel, [len(one) for one in pieces]),
        [shaped(weights.shape, F32), shaped((8, 128), F32)],
        *[one for piece in pieces for one in piece],
    )
    square = dp_sum(heads_sum(square))[0, 0]
    grad_norm = jnp.sqrt(square + jnp.sum(vector_all * vector_all))
    limit = 0.5 * math.sqrt(NPARAM)
    factor = limit / jnp.maximum(grad_norm, limit)
    weights_out = adam_update(
        weights, weights_m, weights_v, weights_ema, weight_grad, factor, MATRIX_RATE, MATRIX_DECAY
    )
    vectors_out = adam_update(vectors, vectors_m, vectors_v, vectors_ema, vector_grad, factor, VECTOR_RATE, 0.0)

    def whole(name, value):
        (out,) = local_call(
            name, whole_rows_kernel, [shaped((count, features), F32)], place, value, core_swap(value), smem=(0,)
        )
        return out

    (layer_rows,) = local_call(
        "layer_out", layer_out_kernel, [wide(features, F32)], stream_two, feed_part, feed_part_got, vec
    )
    (grad_rows,) = local_call(
        "input_grad", input_grad_kernel, [wide(features, F32)], first_part, first_part_got, tokens_own, vec, grad_one
    )
    return (
        whole("layer_rows", layer_rows),
        whole("grad_rows", grad_rows),
        weight_grad,
        vector_grad,
        grad_norm,
        *weights_out,
        *vectors_out,
    )


def solution(mesh):
    rows, square, line = P("dp", None), P("dp", "heads"), P(None, "dp")
    placed = (rows,) * 5 + (square,) * 4 + (line,) * 4
    return jax.shard_map(
        local,
        mesh=mesh,
        in_specs=placed,
        out_specs=(rows, rows, square, line, P()) + (square,) * 4 + (line,) * 4,
        check_vma=False,
    )
```

```python
import math
from functools import partial

import jax
import jax.numpy as jnp
from jax import lax
from jax.experimental import pallas as pl
from jax.experimental.pallas import tpu as pltpu
from jax.sharding import PartitionSpec as P

HEAD_DIM = 64
STEP = 5
NPARAM = 10034688
VECTORS = 10

NORM_EPS = 1e-06
BETA_FIRST = 0.5
BETA_SECOND = 0.5
AVERAGE_RATE = 0.5
MATRIX_RATE = 0.03
VECTOR_RATE = 0.3
MATRIX_DECAY = 0.05
ADAM_EPS = 1e-08
MASKED = -1e30
SCALE = HEAD_DIM ** (-0.5)
F32 = jnp.float32
BF16 = jnp.bfloat16

BLOCK = 128
WINDOW = 256
CLASSES = 16
CHUNK = 256
UNROLL = 4
SPARE = 64
LONG = 40_000_000_000

VMEM = pl.BlockSpec(memory_space=pltpu.VMEM)
SMEM = pl.BlockSpec(memory_space=pltpu.SMEM)
ANY = pl.BlockSpec(memory_space=pl.ANY)


def core_swap(value):
    return lax.ppermute(value, "heads", [(i, i ^ 1) for i in range(4)])


def x_swap(value):
    return lax.ppermute(value, "heads", [(i, i ^ 2) for i in range(4)])


def dp_swap(value, mask):
    count = lax.axis_size("dp")
    return lax.ppermute(value, "dp", [(i, i ^ mask) for i in range(count)])


def all_sum(value):
    count = lax.axis_size("dp") * lax.axis_size("heads")
    value = value + core_swap(value)
    step = 2
    while step < count:
        masks = [step, 2 * step, 3 * step] if 2 * step < count else [step]
        got = [lax.ppermute(value, ("dp", "heads"), [(i, i ^ mask) for i in range(count)]) for mask in masks]
        value = value + got[0]
        if len(got) > 1:
            value = value + (got[1] + got[2])
        step *= 4
    return value


def after(value, *others):
    return lax.optimization_barrier((value, *others))[0]


def together(*groups):
    flat = lax.optimization_barrier([one for group in groups for one in group])
    split, at = [], 0
    for group in groups:
        split.append(list(flat[at : at + len(group)]))
        at += len(group)
    return split


def shaped(shape, dtype):
    return jax.ShapeDtypeStruct(shape, dtype)


def local_call(name, kernel, outs, *operands, scratch=(), smem=(), extra=6, flops=0, staged=False):
    spec = VMEM
    if staged:
        spec, inner, count = ANY, kernel, len(operands)
        moved = [i for i in range(count) if i not in smem]

        def kernel(*refs):
            ins, rest, held, sem = list(refs[:count]), refs[count : -1 - len(moved)], refs[-1 - len(moved) : -1], refs[-1]
            copies = [pltpu.make_async_copy(ins[i], ref, sem.at[j]) for j, (i, ref) in enumerate(zip(moved, held))]
            for copy in copies:
                copy.start()
            for copy, i, ref in zip(copies, moved, held):
                copy.wait()
                ins[i] = ref
            inner(*ins, *rest)

        scratch = [*scratch, *[pltpu.VMEM(operands[i].shape, operands[i].dtype) for i in moved]]
    held = sum(math.prod(one.shape) * jnp.dtype(one.dtype).itemsize for one in scratch)
    return pl.pallas_call(
        kernel,
        name=name,
        out_shape=list(outs),
        in_specs=[SMEM if i in smem else spec for i in range(len(operands))],
        out_specs=[VMEM] * len(outs),
        scratch_shapes=[*scratch, *([pltpu.SemaphoreType.DMA((len(moved),))] if staged else [])],
        compiler_params=pltpu.CompilerParams(
            vmem_limit_bytes=held + extra * 2**20
        ),
        cost_estimate=pl.CostEstimate(flops=flops, bytes_accessed=0, transcendentals=0),
    )(*operands)


def dot(left, right):
    return jnp.dot(left, right, preferred_element_type=F32)


def dot_nt(left, right):
    return lax.dot_general(left, right, (((1,), (1,)), ((), ())), preferred_element_type=F32)


def dot_tn(left, right):
    return lax.dot_general(left, right, (((0,), (0,)), ((), ())), preferred_element_type=F32)


def chunk_loop(rows, body, size=CHUNK):
    def step(i, carry):
        body(pl.ds(pl.multiple_of(i * size, size), size))
        return carry

    lax.fori_loop(0, rows // size, step, 0)


def normed(stream):
    center = stream - jnp.mean(stream, -1, keepdims=True)
    factor = lax.rsqrt(jnp.mean(center * center, -1, keepdims=True) + NORM_EPS)
    return center * factor, factor


def norm_grad(hat, factor, gain, grad):
    scaled = grad * gain
    return factor * (
        scaled - jnp.mean(scaled, -1, keepdims=True) - hat * jnp.mean(scaled * hat, -1, keepdims=True)
    )


def column_sum(value):
    return jnp.sum(value, 0, keepdims=True)


def z_blocks(piece):
    return [piece] + [dp_swap(piece, 2 * k) for k in range(1, lax.axis_size("dp") // 2)]


def y_blocks(mine, fine=False):
    return [dp_swap(one, 1) for one in mine] if fine else [dp_swap(jnp.stack(mine), 1)]


def assemble(name, mine, other, cuts=()):
    half, count, fine = len(mine), lax.axis_size("dp"), len(other) > 1
    rows, columns = mine[0].shape
    bounds = [0, *cuts, columns]
    parts = [slice(start, stop) for start, stop in zip(bounds, bounds[1:])]

    def kernel(place_ref, *refs):
        z, y = place_ref[0], place_ref[1]
        for out_ref, part in zip(refs[half + len(other) :], parts):
            for k in range(half):
                out_ref[(z ^ k) * 2 + y] = refs[k][:, part]
                out_ref[(z ^ k) * 2 + (1 - y)] = refs[half + k][:, part] if fine else refs[half][k, :, part]

    outs = local_call(
        name,
        kernel,
        [shaped((count, rows, part.stop - part.start), mine[0].dtype) for part in parts],
        places(), *mine, *other,
        smem=(0,),
    )
    outs = [one.reshape(count * rows, -1) for one in outs]
    return outs if cuts else outs[0]


def places():
    dp, heads = lax.axis_index("dp"), lax.axis_index("heads")
    return jnp.stack([dp // 2, dp % 2, heads, heads % 2]).astype(jnp.int32)


def split_rows(name, totals, cuts=()):
    count = lax.axis_size("dp")
    half = count // 2
    operands, columns = [], 0
    for own, received in totals:
        rows = own.shape[0] // count
        operands += [one.reshape(count, rows, own.shape[1]) for one in (own, received) if one is not None]
        columns += own.shape[1]
    bounds = [0, *cuts, columns]
    parts = list(zip(bounds, bounds[1:]))

    def kernel(place_ref, *refs):
        ins, outs = refs[: len(operands)], refs[len(operands) :]
        z, y = place_ref[0], place_ref[1]
        for k in range(half):
            for side in range(2):
                block = (z ^ k) * 2 + (1 - y if side == 0 else y)
                at, column = 0, 0
                for own, received in totals:
                    value = ins[at][block].astype(F32)
                    at += 1
                    if received is not None:
                        value = value + ins[at][block].astype(F32)
                        at += 1
                    for i, (start, stop) in enumerate(parts):
                        first, last = max(start, column), min(stop, column + own.shape[1])
                        if first < last:
                            ref = outs[2 * i + side]
                            ref[k, :, first - start : last - start] = value[:, first - column : last - column].astype(
                                ref.dtype
                            )
                    column += own.shape[1]

    outs = []
    for start, stop in parts:
        outs += [shaped((half, rows, stop - start), BF16), shaped((half, rows, stop - start), F32)]
    outs = local_call(name, kernel, outs, places(), *operands, smem=(0,))
    return list(zip(outs[::2], outs[1::2]))


def y_sums(name, pieces, flops=0):
    half, rows, _ = pieces[0][0].shape
    columns = [keep.shape[2] for keep, _ in pieces]
    fine = len(pieces[0][1]) > 1
    operands = [one for keep, arrived in pieces for one in (keep, *arrived)]
    step = 1 + len(pieces[0][1])

    def kernel(*refs):
        ins, outs = refs[: len(operands)], refs[len(operands) :]
        column = 0
        for i, width in enumerate(columns):
            part = slice(column, column + width)
            column += width
            for k in range(half):
                there = ins[i * step + 1 + k][...] if fine else ins[i * step + 1][k]
                value = ins[i * step][k] + there.astype(F32)
                outs[k][:, part] = value.astype(outs[k].dtype)

    outs = [shaped((rows, sum(columns)), F32)] + [shaped((rows, sum(columns)), BF16)] * (half - 1)
    return local_call(name, kernel, outs, *operands, flops=flops)


def z_swaps(summed):
    return [summed[0]] + [dp_swap(summed[k], 2 * k) for k in range(1, len(summed))]


def head_pairs(width):
    pair = 2 * HEAD_DIM
    return [(at, min(at + pair, width), min(2, (width - at) // HEAD_DIM)) for at in range(0, width, pair)]


def by_head(value, heads):
    if heads == 1:
        return value
    lane = lax.broadcasted_iota(jnp.int32, value.shape, 1)
    zero = jnp.zeros_like(value)
    return jnp.concatenate(
        [jnp.where(lane < HEAD_DIM, value, zero), jnp.where(lane < HEAD_DIM, zero, value)], 0
    )


def own_columns(value, heads):
    if heads == 1:
        return value
    count = value.shape[1] // 2
    return jnp.concatenate([value[:HEAD_DIM, :count], value[HEAD_DIM:, count:]], 0)


def own_rows(value, heads):
    if heads == 1:
        return value
    count = value.shape[0] // 2
    lane = lax.broadcasted_iota(jnp.int32, (count, value.shape[1]), 1)
    return jnp.where(lane < HEAD_DIM, value[:count], value[count:])


def masked_bias(allowed):
    return jnp.where(allowed, 0.0, MASKED).astype(F32)


def pair_forward(q, keys, values, bias, heads):
    scores = dot_nt(keys, by_head(q, heads)) + (bias if heads == 1 else jnp.concatenate([bias, bias], 1))
    top = jnp.max(scores, 0, keepdims=True)
    exps = jnp.exp(scores - top)
    total = jnp.sum(exps, 0, keepdims=True)
    out = dot_tn(values, exps.astype(BF16)) / total
    log = top + jnp.log(total)
    count = q.shape[0]
    return own_columns(out, heads), [log[:, h * count : (h + 1) * count] for h in range(heads)]


def pair_backward(q, grad, keys, values, bias, logs, heads):
    q, grad = by_head(q, heads), by_head(grad, heads)
    if heads > 1:
        bias, logs = jnp.concatenate([bias, bias], 1), [jnp.concatenate(logs, 1)]
    probs = jnp.exp(dot_nt(keys, q) + bias - logs[0])
    grad_probs = dot_nt(values, grad)
    delta = jnp.sum(probs * grad_probs, 0, keepdims=True)
    grad_scores = (probs * (grad_probs - delta)).astype(BF16)
    grad_q = own_columns(dot_tn(keys, grad_scores), heads) * SCALE
    return grad_q, dot(grad_scores, q), dot(probs.astype(BF16), grad)


def sort_kernel(
    place_ref, clip_ref, frame_ref, patch_ref, tokens_ref, dy_ref,
    sorted_ref, order_ref, back_ref, col_ref, row_ref, space_col_ref, space_row_ref, own_ref, own_dy_ref,
    all_ref,
):
    count = tokens_ref.shape[0]
    rows = count // 2
    core = place_ref[3]
    own = pl.ds(pl.multiple_of(core * rows, rows), rows)
    far = pl.ds(pl.multiple_of((1 - core) * rows, rows), rows)
    own_ref[...] = tokens_ref[own, :]
    own_dy_ref[...] = dy_ref[own, :]
    all_ref[:rows, :] = tokens_ref[own, :]
    all_ref[rows:, :] = tokens_ref[far, :]
    ids = [clip_ref, frame_ref, patch_ref]
    spare = jnp.zeros((5, count), jnp.int32)
    natural = jnp.concatenate([ref[...] for ref in ids] + [spare], 0)
    space_row_ref[...] = natural
    space_col_ref[...] = natural.astype(F32).T.astype(jnp.int32)
    ordered = jnp.concatenate(
        [jnp.concatenate([ref[:, own], ref[:, far]], 1) for ref in ids] + [spare], 0
    )
    ordered_col = ordered.astype(F32).T.astype(jnp.int32)
    key_row = (ordered[0:1] * 128 + ordered[2:3] + 1) * 64 + ordered[1:2] + 1
    key_col = (ordered_col[:, 0:1] * 128 + ordered_col[:, 2:3] + 1) * 64 + ordered_col[:, 1:2] + 1
    rank_row = jnp.zeros((1, count), jnp.int32)
    for i in range(0, count, CHUNK):
        smaller = key_col[i : i + CHUNK] < key_row
        rank_row = rank_row + jnp.sum(smaller.astype(jnp.int32), 0, keepdims=True)
    for i in range(0, count, CHUNK):
        at = slice(i, i + CHUNK)
        place = lax.broadcasted_iota(jnp.int32, (CHUNK, count), 0) + i
        order = (place == rank_row).astype(F32).astype(BF16)
        order_ref[at, :] = order
        rank_col = jnp.sum((key_row < key_col[at]).astype(jnp.int32), 1, keepdims=True)
        place = lax.broadcasted_iota(jnp.int32, (CHUNK, count), 1)
        back_ref[at, :] = (place == rank_col).astype(F32).astype(BF16)
        sorted_ref[at, :] = dot(order, all_ref[...]).astype(BF16)
        col_ref[at, :] = dot(order, ordered_col.astype(F32).astype(BF16))
        row_ref[:, at] = dot_nt(ordered.astype(F32).astype(BF16), order)


def pack_kernel(weights_ref, vectors_ref, head_ref, space_ref, up_ref, down_ref):
    width, hidden = space_ref.shape[1] // 4, up_ref.shape[1]
    rows = weights_ref.shape[0]
    start = head_ref.shape[1] - 2 * width
    unit = lax.broadcasted_iota(jnp.int32, (rows, rows), 0) == lax.broadcasted_iota(jnp.int32, (rows, rows), 1)
    vectors = jnp.concatenate([vectors_ref[...], jnp.zeros((16 - VECTORS, rows), F32)], 0).astype(BF16)
    head_ref[:, : 3 * width] = weights_ref[:, : 3 * width].astype(BF16)
    head_ref[:, 3 * width : start] = jnp.zeros((rows, start - 3 * width), BF16)
    head_ref[:, 3 * width : 3 * width + 16] = dot_nt(unit.astype(F32).astype(BF16), vectors).astype(BF16)
    head_ref[:, start : start + width] = weights_ref[:, 4 * width : 5 * width].astype(BF16)
    head_ref[:, start + width :] = weights_ref[:, 3 * width : 4 * width].astype(BF16)
    space_ref[...] = weights_ref[:, 5 * width : 9 * width].astype(BF16)
    up_ref[...] = weights_ref[:, 9 * width : 9 * width + hidden].astype(BF16)
    down_ref[...] = weights_ref[:, 9 * width + hidden :].astype(BF16)


def same_clip_patch(col_ref, row_ref, keys, queries):
    key = col_ref[keys, :]
    query = row_ref[:, queries]
    return (key[:, 0:1] * 128 + key[:, 2:3]) == (query[0:1] * 128 + query[2:3])


def temporal_window(i, count):
    first = i * BLOCK
    start = jnp.clip(first - (WINDOW - BLOCK) // 2, 0, count - WINDOW)
    return (
        pl.ds(pl.multiple_of(first, BLOCK), BLOCK),
        pl.ds(pl.multiple_of(start, (WINDOW - BLOCK) // 2), WINDOW),
    )


def time_forward_kernel(
    maps_ref, tokens_ref, back_ref, col_ref, row_ref,
    vec_ref, first_ref, inputs_ref, own_ref, far_ref, log_ref, heads_ref,
):
    count, width = tokens_ref.shape[0], own_ref.shape[1]
    columns = maps_ref.shape[1]
    lanes = maps_ref[:, columns - 128 :].astype(F32).T
    offset = 3 * width - (columns - 128)
    vec_ref[...] = lanes[offset : offset + 16]
    gain, shift = vec_ref[0:1], vec_ref[1:2]

    def project(at):
        hat, _ = normed(tokens_ref[at, :].astype(F32))
        first = (hat * gain + shift).astype(BF16)
        first_ref[at, :] = first
        inputs_ref[at, :] = dot(first, maps_ref[:, : 3 * width]).astype(BF16)

    chunk_loop(count, project)

    def step(i, carry):
        queries, keys = temporal_window(i, count)
        bias = masked_bias(same_clip_patch(col_ref, row_ref, keys, queries))
        outs, logs = [], []
        for start, stop, heads in head_pairs(width):
            out, log = pair_forward(
                inputs_ref[queries, start:stop] * BF16(SCALE),
                inputs_ref[keys, width + start : width + stop],
                inputs_ref[keys, 2 * width + start : 2 * width + stop],
                bias,
                heads,
            )
            outs.append(out)
            logs += log
        heads_ref[queries, :] = jnp.concatenate(outs, 0).T.astype(BF16)
        log_ref[:, queries] = jnp.concatenate(logs + [logs[0]] * (8 - len(logs)), 0)
        return carry

    lax.fori_loop(0, count // BLOCK, step, 0, unroll=8)
    rows = count // 2
    for i in range(0, rows, CHUNK):
        own_ref[i : i + CHUNK, :] = dot(back_ref[i : i + CHUNK, :], heads_ref[...]).astype(BF16)
        far_ref[i : i + CHUNK, :] = dot(back_ref[rows + i : rows + i + CHUNK, :], heads_ref[...]).astype(BF16)


def time_backward_kernel(
    own_ref, far_ref, order_ref, inputs_ref, log_ref, col_ref, row_ref,
    out_ref, grad_ref, sum_ref,
):
    count, width = inputs_ref.shape[0], own_ref.shape[1]
    rows = count // 2
    for i in range(0, count, CHUNK):
        grad_ref[i : i + CHUNK, :] = (
            dot(order_ref[i : i + CHUNK, :rows], own_ref[...]) + dot(order_ref[i : i + CHUNK, rows:], far_ref[...])
        ).astype(BF16)
    sum_ref[...] = jnp.zeros_like(sum_ref)

    def step(i, carry):
        queries, keys = temporal_window(i, count)
        bias = masked_bias(same_clip_patch(col_ref, row_ref, keys, queries))
        grad_qs, head = [], 0
        for start, stop, heads in head_pairs(width):
            grad_q, grad_k, grad_v = pair_backward(
                inputs_ref[queries, start:stop] * BF16(SCALE),
                grad_ref[queries, start:stop],
                inputs_ref[keys, width + start : width + stop],
                inputs_ref[keys, 2 * width + start : 2 * width + stop],
                bias,
                [log_ref[h : h + 1, queries] for h in range(head, head + heads)],
                heads,
            )
            head += heads
            grad_qs.append(grad_q)
            sum_ref[keys, start:stop] += grad_k
            sum_ref[keys, width + start : width + stop] += grad_v
        out_ref[queries, :width] = jnp.concatenate(grad_qs, 0).T.astype(BF16)
        return carry

    lax.fori_loop(0, count // BLOCK, step, 0, unroll=8)

    def store(at):
        out_ref[at, width:] = sum_ref[at, :].astype(BF16)

    chunk_loop(count, store)


def space_window(i, core, rows):
    first = core * rows + i * BLOCK
    start = jnp.clip(first - (WINDOW - BLOCK) // 2, 0, 2 * rows - WINDOW)
    return (
        pl.ds(pl.multiple_of(i * BLOCK, BLOCK), BLOCK),
        pl.ds(pl.multiple_of(first, BLOCK), BLOCK),
        pl.ds(pl.multiple_of(start, (WINDOW - BLOCK) // 2), WINDOW),
    )


def whole_pairs(core, pairs_ref, got_ref, whole_ref):
    rows, width = pairs_ref.shape[0], pairs_ref.shape[1] // 4
    whole_ref[pl.ds(pl.multiple_of(core * rows, rows), rows), :] = pairs_ref[...]
    there = pl.ds(pl.multiple_of((1 - core) * rows, rows), rows)
    for i, j in enumerate((1, 0, 3, 2)):
        whole_ref[there, i * width : (i + 1) * width] = got_ref[:, j * width : (j + 1) * width]


def class_rows(row):
    number = lax.broadcasted_iota(jnp.int32, (CLASSES, row.shape[1]), 0)
    return (row[0:1] == number) & (row[1:2] < 0)


def space_bias(col_ref, row_ref, queries, keys):
    key, query = col_ref[keys, :], row_ref[:, queries]
    frame = jnp.where(key[:, 1:2] < 0, -1, key[:, 0:1] * 128 + key[:, 1:2]) == query[0:1] * 128 + query[1:2]
    number = lax.broadcasted_iota(jnp.int32, (CLASSES, BLOCK), 0)
    return masked_bias(jnp.concatenate([frame & (query[1:2] >= 0), number == query[0:1]], 0))


def class_allowed(row_ref):
    number = lax.broadcasted_iota(jnp.int32, (CLASSES, row_ref.shape[1]), 0)
    return row_ref[0:1] == number


def space_forward_kernel(
    place_ref, q_ref, pairs_ref, got_ref, col_ref, row_ref, out_own_ref, out_far_ref,
    heads_ref, log_ref, class_log_ref, part_ref, whole_ref, class_ref,
):
    core = place_ref[3]
    rows, width = q_ref.shape
    whole_pairs(core, pairs_ref, got_ref, whole_ref)
    here = pl.ds(pl.multiple_of(core * rows, rows), rows)
    classes = class_rows(row_ref[...]).astype(F32).astype(BF16)
    own_classes = class_rows(row_ref[:, here]).astype(F32).astype(BF16)
    class_ref[...] = dot(classes, whole_ref[...]).astype(BF16)
    def both(keys, part):
        return jnp.concatenate([whole_ref[keys, part], class_ref[:, part]], 0)

    def step(i, carry):
        local, queries, keys = space_window(i, core, rows)
        bias = space_bias(col_ref, row_ref, queries, keys)
        outs, logs = [], []
        for start, stop, heads in head_pairs(width):
            out, log = pair_forward(
                q_ref[local, start:stop] * BF16(SCALE),
                both(keys, slice(start, stop)),
                both(keys, slice(width + start, width + stop)),
                bias,
                heads,
            )
            outs.append(out)
            logs += log
        heads_ref[local, :] = jnp.concatenate(outs, 0).T.astype(BF16)
        log_ref[:, local] = jnp.concatenate(logs + [logs[0]] * (8 - len(logs)), 0)
        return carry

    lax.fori_loop(0, rows // BLOCK, step, 0, unroll=UNROLL)

    bias = masked_bias(class_allowed(row_ref))
    class_q = dot(own_classes, q_ref[...]).astype(BF16) * BF16(SCALE)
    outs, logs = [], []
    for start, stop, heads in head_pairs(width):
        scores = dot_nt(by_head(class_q[:, start:stop], heads), whole_ref[:, start:stop])
        scores = scores + (bias if heads == 1 else jnp.concatenate([bias, bias], 0))
        top = jnp.max(scores, 1, keepdims=True)
        exps = jnp.exp(scores - top)
        total = jnp.sum(exps, 1, keepdims=True)
        outs.append(own_rows(dot(exps.astype(BF16), whole_ref[:, width + start : width + stop]) / total, heads))
        log = top + jnp.log(total)
        logs += [log[h * CLASSES : (h + 1) * CLASSES] for h in range(heads)]
    class_log_ref[...] = jnp.concatenate(logs + [logs[0]] * (8 - len(logs)), 1)
    class_out = jnp.concatenate(outs, 1).astype(BF16)
    is_class = col_ref[here, 1:2] < 0

    def replace(at):
        back = dot_tn(own_classes, class_out).astype(BF16)
        heads_ref[...] = jnp.where(is_class, back, heads_ref[...])

    replace(None)
    group = width // 2

    def project(at):
        part_ref[at, :] = (
            dot_nt(heads_ref[at, :group], out_own_ref[:, 3 * group :])
            + dot_nt(heads_ref[at, group:], out_far_ref[:, 3 * group :])
        ).astype(BF16)

    chunk_loop(rows, project)


def space_back_in_kernel(
    part_ref, got_ref, stream_ref, vec_ref, dy_ref, out_own_ref, out_far_ref,
    grad_ref, low_ref, sums_ref, heads_ref,
):
    group = heads_ref.shape[1] // 2
    gain = vec_ref[7:8]
    sums_ref[...] = jnp.zeros_like(sums_ref)

    def through_norm(at):
        grad = part_ref[at, :].astype(F32) + got_ref[at, :].astype(F32)
        hat, factor = normed(stream_ref[at, :])
        dy = dy_ref[at, :].astype(F32)
        dx = dy + norm_grad(hat, factor, gain, grad)
        grad_ref[at, :] = dx
        low = dx.astype(BF16)
        low_ref[at, :] = low
        heads_ref[at, :group] = dot(low, out_own_ref[:, 3 * group :]).astype(BF16)
        heads_ref[at, group:] = dot(low, out_far_ref[:, 3 * group :]).astype(BF16)
        sums_ref[0:4] += jnp.concatenate(
            [column_sum(dx), column_sum(grad * hat), column_sum(grad), column_sum(dy)], 0
        )

    chunk_loop(grad_ref.shape[0], through_norm)


def space_backward_kernel(
    place_ref, heads_ref, q_ref, pairs_ref, got_ref, log_ref, class_log_ref, col_ref, row_ref,
    dq_ref, keep_ref, send_ref,
    whole_ref, class_ref, total_ref, class_total_ref, class_dq_ref,
):
    core = place_ref[3]
    rows, width = q_ref.shape
    whole_pairs(core, pairs_ref, got_ref, whole_ref)
    here = pl.ds(pl.multiple_of(core * rows, rows), rows)
    there = pl.ds(pl.multiple_of((1 - core) * rows, rows), rows)
    classes = class_rows(row_ref[...]).astype(F32)
    own_classes = class_rows(row_ref[:, here]).astype(F32).astype(BF16)
    class_ref[...] = dot(classes.astype(BF16), whole_ref[...]).astype(BF16)
    class_total_ref[...] = jnp.zeros_like(class_total_ref)
    bias = masked_bias(class_allowed(row_ref))
    class_q = dot(own_classes, q_ref[...]).astype(BF16) * BF16(SCALE)
    class_g = dot(own_classes, heads_ref[...]).astype(BF16)
    head = 0
    for start, stop, heads in head_pairs(width):
        keys, values = whole_ref[:, start:stop], whole_ref[:, width + start : width + stop]
        q, grad = by_head(class_q[:, start:stop], heads), by_head(class_g[:, start:stop], heads)
        logs = [class_log_ref[:, h : h + 1] for h in range(head, head + heads)]
        head += heads
        scores = dot_nt(q, keys) + (bias if heads == 1 else jnp.concatenate([bias, bias], 0))
        probs = jnp.exp(scores - jnp.concatenate(logs, 0))
        grad_probs = dot_nt(grad, values)
        grad_scores = (probs * (grad_probs - jnp.sum(probs * grad_probs, 1, keepdims=True))).astype(BF16)
        class_dq_ref[:, start:stop] = own_rows(dot(grad_scores, keys) * SCALE, heads).astype(BF16)
        total_ref[:, start:stop] = dot_tn(grad_scores, q)
        total_ref[:, width + start : width + stop] = dot_tn(probs.astype(BF16), grad)

    def both(keys, part):
        return jnp.concatenate([whole_ref[keys, part], class_ref[:, part]], 0)

    def step(i, carry):
        local, queries, keys = space_window(i, core, rows)
        bias = space_bias(col_ref, row_ref, queries, keys)
        is_class = row_ref[1:2, queries] < 0
        grad_qs, head = [], 0
        for start, stop, heads in head_pairs(width):
            key_part, value_part = slice(start, stop), slice(width + start, width + stop)
            grad_q, grad_k, grad_v = pair_backward(
                q_ref[local, start:stop] * BF16(SCALE),
                heads_ref[local, start:stop],
                both(keys, key_part),
                both(keys, value_part),
                bias,
                [jnp.where(is_class, -MASKED, log_ref[h : h + 1, local]) for h in range(head, head + heads)],
                heads,
            )
            head += heads
            grad_qs.append(grad_q)
            total_ref[keys, key_part] += grad_k[:WINDOW]
            total_ref[keys, value_part] += grad_v[:WINDOW]
            class_total_ref[:, key_part] += grad_k[WINDOW:]
            class_total_ref[:, value_part] += grad_v[WINDOW:]
        dq_ref[local, :] = jnp.concatenate(grad_qs, 0).T.astype(BF16)
        return carry

    lax.fori_loop(0, rows // BLOCK, step, 0, unroll=UNROLL)
    dq_ref[...] = jnp.where(
        col_ref[here, 1:2] < 0, dot_tn(own_classes, class_dq_ref[...]).astype(BF16), dq_ref[...]
    )
    high = class_total_ref[...].astype(BF16)
    rest = (class_total_ref[...] - high.astype(F32)).astype(BF16)
    classes = classes.astype(BF16)
    total_ref[...] += dot_tn(jnp.concatenate([classes, classes], 0), jnp.concatenate([high, rest], 0))
    keep_ref[...] = total_ref[here, :]
    send_ref[...] = total_ref[there, :].astype(BF16)


def mix_kernel(place_ref, out_ref, own_ref, x_ref, core_ref, vec_ref, mix_ref, fused_ref, bias_ref):
    place = place_ref[2]
    width = out_ref.shape[1]
    mix_ref[0] = own_ref[...]
    mix_ref[1] = core_ref[:, :width]
    mix_ref[2] = x_ref[...]
    mix_ref[3] = core_ref[:, width:]
    total, bias = 0.0, 0.0
    low = vec_ref[...].astype(BF16)
    for j in range(4):
        block = mix_ref[place ^ j]
        total = total + dot(block, out_ref[j * width : (j + 1) * width, :])
        bias = bias + dot_nt(low[:, j * width : (j + 1) * width], block)
    fused_ref[...] = total.astype(BF16)
    bias_ref[...] = bias[2:3] + vec_ref[3:4]


def time_out_kernel(own_ref, got_ref, fused_ref, far_ref, part_ref):
    def project(at):
        part_ref[at, :] = (dot_nt(own_ref[at, :], fused_ref[...]) + dot_nt(got_ref[at, :], far_ref[...])).astype(BF16)

    chunk_loop(part_ref.shape[0], project)


def norm_in_kernel(gain_row, before_ref, part_ref, got_ref, shift_ref, vec_ref, stream_ref, normed_ref):
    gain, shift = vec_ref[gain_row : gain_row + 1], vec_ref[gain_row + 1 : gain_row + 2]

    def body(at):
        stream = (
            before_ref[at, :].astype(F32)
            + (part_ref[at, :].astype(F32) + got_ref[at, :].astype(F32))
            + shift_ref[0:1]
        )
        stream_ref[at, :] = stream
        hat, _ = normed(stream)
        normed_ref[at, :] = (hat * gain + shift).astype(BF16)

    chunk_loop(stream_ref.shape[0], body)


def space_in_kernel(second_ref, own_ref, far_ref, q_ref, pairs_ref):
    width = q_ref.shape[1] // 2

    def project(at):
        for g, maps_ref in enumerate((own_ref, far_ref)):
            inputs = dot(second_ref[at, :], maps_ref[:, : 3 * width]).astype(BF16)
            q_ref[at, g * width : (g + 1) * width] = inputs[:, :width]
            pairs_ref[at, g * width : (g + 1) * width] = inputs[:, width : 2 * width]
            pairs_ref[at, (2 + g) * width : (3 + g) * width] = inputs[:, 2 * width :]

    chunk_loop(q_ref.shape[0], project)


def gelu_parts(pre):
    cdf = 0.5 * (1.0 + lax.erf(pre * (0.5**0.5)))
    slope = cdf + pre * jnp.exp(-0.5 * pre * pre) * (1.0 / math.sqrt(2.0 * math.pi))
    return pre * cdf, slope


def feed_kernel(
    third_ref, dy_ref, up_ref, up_far_ref, down_ref, down_far_ref, activ_ref, grad_ref, back_ref
):
    hidden = activ_ref.shape[1] // 2

    def project(at):
        back = 0.0
        for g, (ups_ref, downs_ref) in enumerate(((up_ref, down_ref), (up_far_ref, down_far_ref))):
            act, slope = gelu_parts(dot(third_ref[at, :], ups_ref[...]))
            part = slice(g * hidden, (g + 1) * hidden)
            activ_ref[at, part] = act.astype(BF16)
            grad = (dot(dy_ref[at, :], downs_ref[...]) * slope).astype(BF16)
            grad_ref[at, part] = grad
            back = back + dot_nt(grad, ups_ref[...])
        back_ref[at, :] = back.astype(BF16)

    chunk_loop(third_ref.shape[0], project)


def feed_out_kernel(activ_ref, own_ref, far_ref, part_ref):
    hidden = activ_ref.shape[1] // 2

    def project(at):
        part_ref[at, :] = (
            dot_nt(activ_ref[at, :hidden], own_ref[...]) + dot_nt(activ_ref[at, hidden:], far_ref[...])
        ).astype(BF16)

    chunk_loop(part_ref.shape[0], project)


def feed_grads_kernel(group, third_ref, grad_ref, dy_ref, activ_ref, out_ref):
    hidden = out_ref.shape[1] // 2
    part = slice(group * hidden, (group + 1) * hidden)
    out_ref[:, :hidden] = dot_tn(third_ref[...], grad_ref[:, part]).astype(BF16)
    out_ref[:, hidden:] = dot_tn(dy_ref[...], activ_ref[:, part]).astype(BF16)


def space_back_kernel(
    dq_ref, keep_ref, got_ref, own_ref, far_ref, grad_own_ref, grad_far_ref, part_ref
):
    width = dq_ref.shape[1] // 2

    def project(at):
        total = 0.0
        for g, (maps_ref, grad_ref) in enumerate(((own_ref, grad_own_ref), (far_ref, grad_far_ref))):
            grad_ref[at, :width] = dq_ref[at, g * width : (g + 1) * width]
            for i in (1, 2):
                mine = slice((2 * i - 2 + g) * width, (2 * i - 1 + g) * width)
                theirs = slice((2 * i - 1 - g) * width, (2 * i - g) * width)
                grad_ref[at, i * width : (i + 1) * width] = (
                    keep_ref[at, mine] + got_ref[at, theirs].astype(F32)
                ).astype(BF16)
            total = total + dot_nt(grad_ref[at, :], maps_ref[:, : 3 * width])
        part_ref[at, :] = total.astype(BF16)

    chunk_loop(part_ref.shape[0], project)


def space_grads_kernel(group, second_ref, grad_ref, low_ref, heads_ref, out_ref):
    width = heads_ref.shape[1] // 2
    out_ref[:, : 3 * width] = dot_tn(second_ref[...], grad_ref[...]).astype(BF16)
    out_ref[:, 3 * width :] = dot_tn(low_ref[...], heads_ref[:, group * width : (group + 1) * width]).astype(BF16)


def time_back_in_kernel(
    part_ref, got_ref, stream_ref, vec_ref, before_ref, fused_ref, far_ref,
    grad_ref, low_ref, sums_ref, own_ref, send_ref,
):
    gain = vec_ref[4:5]
    sums_ref[...] = jnp.zeros_like(sums_ref)

    def through_norm(at):
        grad = part_ref[at, :].astype(F32) + got_ref[at, :].astype(F32)
        hat, factor = normed(stream_ref[at, :])
        dx = before_ref[at, :] + norm_grad(hat, factor, gain, grad)
        grad_ref[at, :] = dx
        low = dx.astype(BF16)
        low_ref[at, :] = low
        own_ref[at, :] = dot(low, fused_ref[...]).astype(BF16)
        send_ref[at, :] = dot(low, far_ref[...]).astype(BF16)
        sums_ref[0:4] += jnp.concatenate(
            [column_sum(low.astype(F32)), column_sum(dx), column_sum(grad * hat), column_sum(grad)], 0
        )

    chunk_loop(grad_ref.shape[0], through_norm)


def time_grads_kernel(place_ref, first_ref, grad_ref, row_sum_ref, send_ref, keep_ref, total_ref):
    half, rows, columns = keep_ref.shape
    width = columns - row_sum_ref.shape[1]
    z, y = place_ref[0], place_ref[1]
    total_ref[:, :width] = dot_tn(first_ref[...], grad_ref[...])
    total_ref[:, width:] = row_sum_ref[...]
    for k in range(half):
        mine = pl.ds(pl.multiple_of(((z ^ k) * 2 + y) * rows, 8), rows)
        theirs = pl.ds(pl.multiple_of(((z ^ k) * 2 + (1 - y)) * rows, 8), rows)
        send_ref[k] = total_ref[theirs, :].astype(BF16)
        keep_ref[k] = total_ref[mine, :]


def time_back_kernel(
    grad_ref, maps_ref, tokens_ref, back_ref, bias_ref, one_ref, two_ref, own_ref, far_ref, sums_ref, sorted_ref
):
    count, width = tokens_ref.shape[0], grad_ref.shape[1] // 3
    sums_ref[...] = jnp.zeros_like(sums_ref)
    sums_ref[2:3] = 0.5 * bias_ref[0:1]
    sums_ref[3:6] = 0.5 * one_ref[1:4]
    sums_ref[6:10] = 0.5 * two_ref[0:4]

    def project(at):
        grad = dot_nt(grad_ref[at, :], maps_ref[:, : 3 * width])
        hat, _ = normed(tokens_ref[at, :].astype(F32))
        sums_ref[0:2] += jnp.concatenate([column_sum(grad * hat), column_sum(grad)], 0)
        sorted_ref[at, :] = grad.astype(BF16)

    chunk_loop(count, project)
    rows = count // 2
    for i in range(0, rows, CHUNK):
        far_ref[i : i + CHUNK, :] = dot(back_ref[rows + i : rows + i + CHUNK, :], sorted_ref[...]).astype(BF16)
    for i in range(0, rows, CHUNK):
        own_ref[i : i + CHUNK, :] = dot(back_ref[i : i + CHUNK, :], sorted_ref[...]).astype(BF16)


def input_grad_kernel(part_ref, got_ref, tokens_ref, vec_ref, before_ref, out_ref):
    gain = vec_ref[0:1]

    def through_norm(at):
        grad = part_ref[at, :].astype(F32) + got_ref[at, :].astype(F32)
        hat, factor = normed(tokens_ref[at, :].astype(F32))
        out_ref[at, :] = before_ref[at, :] + norm_grad(hat, factor, gain, grad)

    chunk_loop(out_ref.shape[0], through_norm)


def layer_out_kernel(stream_ref, part_ref, got_ref, vec_ref, out_ref):
    out_ref[...] = stream_ref[...] + (part_ref[...].astype(F32) + got_ref[...].astype(F32)) + vec_ref[9:10]


def whole_rows_kernel(place_ref, own_ref, got_ref, out_ref):
    core = place_ref[3]
    rows = own_ref.shape[0]
    out_ref[pl.ds(pl.multiple_of(core * rows, rows), rows), :] = own_ref[...]
    out_ref[pl.ds(pl.multiple_of((1 - core) * rows, rows), rows), :] = got_ref[...]


def fused_grads_kernel(low_ref, heads_ref, got_heads_ref, own_ref, far_ref):
    ones = jnp.ones((low_ref.shape[0], own_ref.shape[1] - heads_ref.shape[1]), BF16)
    far_ref[...] = dot_tn(low_ref[...], jnp.concatenate([got_heads_ref[...], ones], 1)).astype(BF16)
    own_ref[...] = dot_tn(low_ref[...], jnp.concatenate([heads_ref[...], ones], 1))


def mix_grads_kernel(
    place_ref, fused_ref, got_ref, mix_ref, sums_ref, grad_out_ref, total_ref, row_sum_ref, bias_ref
):
    place = place_ref[2]
    width = total_ref.shape[1]
    both = fused_ref[...] + got_ref[...].astype(F32)
    row_sum_ref[...] = both[:, width:]
    fused = both[:, :width].astype(BF16)
    total_ref[...] = fused
    for j in range(4):
        block = mix_ref[place ^ j]
        grad_out_ref[j * width : (j + 1) * width, :] = dot_tn(block, fused).astype(BF16)
        bias_ref[:, j * width : (j + 1) * width] = dot(sums_ref[...].astype(BF16), block)


def mix_shard_kernel(place_ref, fused_ref, out_ref, keep_ref, send_ref):
    place = place_ref[2]
    width = out_ref.shape[1]
    fused = fused_ref[...].astype(BF16)
    for m in range(4):
        rows = out_ref[pl.ds(pl.multiple_of((place ^ m) * width, width), width), :]
        part = dot_nt(fused, rows)
        ref = send_ref if m % 2 else keep_ref
        ref[:, m // 2 * width : (m // 2 + 1) * width] = part.astype(ref.dtype)


def early_grad_kernel(groups, *refs):
    out_ref, square_ref = refs[-2:]
    count, column, square = (len(refs) - 2) // len(groups), 0, 0.0
    for i, (start, stop) in enumerate(groups):
        value = sum(ref[:, start:stop].astype(F32) for ref in refs[i * count : (i + 1) * count])
        out_ref[:, column : column + value.shape[1]] = value
        column += value.shape[1]
        square = square + jnp.sum(value * value)
    square_ref[...] = jnp.full(square_ref.shape, square, F32)


def whole_grad_kernel(early_ref, square_ref, vector_ref, bias_ref, out_ref, mix_ref, *refs):
    grad_ref, sums_ref = refs[-2:]
    width = mix_ref.shape[1]
    total = sum(ref[...].astype(F32) for ref in refs[:-2])
    row_sum = total[:, 3 * width : 3 * width + 1]
    mix = mix_ref[...] + row_sum * bias_ref[...]
    grad_ref[:, 5 * width :] = early_ref[...]
    square = square_ref[...]
    for i, value in ((0, total[:, : 3 * width]), (3, out_ref[:, :width]), (4, mix)):
        grad_ref[:, i * width : i * width + value.shape[1]] = value
        square = square + jnp.sum(value * value)
    sums_ref[...] = vector_ref[...]
    sums_ref[VECTORS : VECTORS + 1] = square


def adam_update(master, first_moment, second_moment, average, gradient, factor, rate, decay):
    clipped = gradient * factor
    first_new = BETA_FIRST * first_moment + (1.0 - BETA_FIRST) * clipped
    second_new = BETA_SECOND * second_moment + (1.0 - BETA_SECOND) * clipped * clipped
    first_hat = first_new / (1.0 - BETA_FIRST**STEP)
    second_hat = second_new / (1.0 - BETA_SECOND**STEP)
    master_new = master - rate * (first_hat / (jnp.sqrt(second_hat) + ADAM_EPS) + decay * master)
    average_new = AVERAGE_RATE * average + (1.0 - AVERAGE_RATE) * master_new
    return (master_new, first_new, second_new, average_new)


def local(
    tokens,
    cotangent,
    clip_ids,
    frame_ids,
    patch_ids,
    weights,
    weights_m,
    weights_v,
    weights_ema,
    vectors,
    vectors_m,
    vectors_v,
    vectors_ema,
):
    group_count = lax.axis_size("heads")
    core = lax.axis_index("heads") % 2
    place = places()
    count, features = tokens.shape
    width = features // group_count
    hidden = (weights.shape[1] - 9 * width) // 2
    rows = count // 2
    half = lax.axis_size("dp") // 2
    shard = weights.shape[0]

    wide = lambda n, dtype: shaped((rows, n), dtype)

    head_start = -(-(3 * width + 16) // 128) * 128
    head_piece, space_piece, up_piece, down_piece = local_call(
        "pack",
        pack_kernel,
        [shaped((shard, n), BF16) for n in (head_start + 2 * width, 4 * width, hidden, hidden)],
        weights, vectors,
    )
    head_z = z_blocks(head_piece)
    tokens_sorted, order, back, time_col, time_row, space_col, space_row, tokens_own, dy = local_call(
        "sort_rows",
        sort_kernel,
        [
            shaped((count, features), BF16),
            shaped((count, count), BF16),
            shaped((count, count), BF16),
            shaped((count, 8), F32),
            shaped((8, count), F32),
            shaped((count, 8), jnp.int32),
            shaped((8, count), jnp.int32),
            wide(features, BF16),
            wide(features, BF16),
        ],
        place, clip_ids, frame_ids, patch_ids, tokens, cotangent,
        smem=(0,),
        scratch=[pltpu.VMEM((count, features), BF16)],
    )
    head_z, _ = together(head_z, [tokens_sorted])
    head_z[0] = head_piece
    head_y = y_blocks(head_z, True)
    space_z = z_blocks(after(space_piece, *head_z))
    (head_y,) = together(head_y)
    time_maps, mix_map, out_map = assemble(
        "gather_head", head_z, head_y, (head_start, head_start + width)
    )
    mix_x = x_swap(mix_map)

    vec, first, time_inputs, time_own, time_send, time_logs = local_call(
        "time_forward",
        time_forward_kernel,
        [
            shaped((16, features), F32),
            shaped((count, features), BF16),
            shaped((count, 3 * width), BF16),
            wide(width, BF16),
            wide(width, BF16),
            shaped((8, count), F32),
        ],
        time_maps, tokens_sorted, back, time_col, time_row,
        scratch=[pltpu.VMEM((count, width), BF16)],
    )
    space_z, (mix_x, time_send) = together(space_z, [mix_x, time_send])
    mix_core = core_swap(jnp.concatenate([mix_map, mix_x], 1))
    time_got = core_swap(time_send)

    mix_blocks, fused, mix_bias = local_call(
        "mix_maps",
        mix_kernel,
        [
            shaped((group_count, features, width), BF16),
            shaped((features, width), BF16),
            shaped((1, features), F32),
        ],
        place, out_map, mix_map, mix_x, mix_core, vec,
        smem=(0,),
    )
    fused_far = core_swap(fused)
    space_y = y_blocks(space_z)
    up_z = z_blocks(after(up_piece, *space_z))
    (time_part,) = local_call("time_out", time_out_kernel, [wide(features, BF16)], time_own, time_got, fused, fused_far)
    stream_one, second = local_call(
        "space_norm",
        partial(norm_in_kernel, 4),
        [wide(features, F32), wide(features, BF16)],
        tokens_own, time_part, x_swap(time_part), mix_bias, vec,
        flops=LONG,
    )

    space_own = assemble("gather_space", space_z, space_y)
    space_far = core_swap(space_own)
    space_q, space_pairs = local_call(
        "space_in",
        space_in_kernel,
        [wide(2 * width, BF16), wide(4 * width, BF16)],
        second, space_own, space_far,
    )
    up_z, (space_q, space_pairs) = together(up_z, [space_q, space_pairs])
    up_y = y_blocks(up_z)
    down_z = z_blocks(after(down_piece, *up_z))
    space_got = core_swap(space_pairs)
    space_heads, space_logs, class_logs, space_part = local_call(
        "space_forward",
        space_forward_kernel,
        [wide(2 * width, BF16), shaped((8, rows), F32), shaped((CLASSES, 8), F32), wide(features, BF16)],
        place, space_q, space_pairs, space_got, space_col, space_row, space_own, space_far,
        smem=(0,),
        scratch=[pltpu.VMEM((count, 4 * width), BF16), pltpu.VMEM((CLASSES, 4 * width), BF16)],
    )
    up_y, down_z, (space_part,) = together(up_y, down_z, [space_part])
    stream_two, third = local_call(
        "feed_norm",
        partial(norm_in_kernel, 7),
        [wide(features, F32), wide(features, BF16)],
        stream_one, space_part, x_swap(space_part), vec[6:8], vec,
        flops=LONG,
    )

    up_own = assemble("gather_up", up_z, up_y)
    up_far = core_swap(up_own)
    down_own = assemble("gather_down", down_z, y_blocks(down_z))
    down_far = core_swap(down_own)
    activ, grad_pre, third_part = local_call(
        "feed",
        feed_kernel,
        [wide(2 * hidden, BF16), wide(2 * hidden, BF16), wide(features, BF16)],
        third, dy, up_own, up_far, down_own, down_far,
    )
    third_got = x_swap(third_part)
    feed_grad_far, feed_grad_own = [
        local_call(
            name,
            partial(feed_grads_kernel, group),
            [shaped((features, 2 * hidden), BF16)],
            third, grad_pre, dy, activ,
        )[0]
        for name, group in (("feed_grads_far", 1), ("feed_grads_own", 0))
    ]
    (feed_part,) = local_call("feed_out", feed_out_kernel, [wide(features, BF16)], activ, down_own, down_far)
    (up_send, up_keep), (down_send, down_keep) = split_rows(
        "split_feed", [(feed_grad_own, core_swap(feed_grad_far))], (hidden,)
    )
    up_y = [dp_swap(up_send, 1)]
    feed_part_got = x_swap(feed_part)

    grad_two, grad_two_low, sums_two, space_grad_heads = local_call(
        "space_back_in",
        space_back_in_kernel,
        [wide(features, F32), wide(features, BF16), shaped((8, features), F32), wide(2 * width, BF16)],
        third_part, third_got, stream_two, vec, dy, space_own, space_far,
    )
    space_dq, space_keep, space_send = local_call(
        "space_backward",
        space_backward_kernel,
        [wide(2 * width, BF16), wide(4 * width, F32), wide(4 * width, BF16)],
        place, space_grad_heads, space_q, space_pairs, space_got, space_logs, class_logs, space_col, space_row,
        smem=(0,),
        scratch=[
            pltpu.VMEM((count, 4 * width), BF16),
            pltpu.VMEM((CLASSES, 4 * width), BF16),
            pltpu.VMEM((count, 4 * width), F32),
            pltpu.VMEM((CLASSES, 4 * width), F32),
            pltpu.VMEM((CLASSES, 2 * width), BF16),
        ],
    )
    up_y, (space_send, feed_part_got) = together(up_y, [space_send, feed_part_got])
    up_shards = z_swaps(y_sums("sum_up", [(up_keep, up_y)]))
    space_got_grads = core_swap(space_send)
    down_y = [dp_swap(after(down_send, *up_y), 1)]
    grad_space, grad_space_far, second_part = local_call(
        "space_back",
        space_back_kernel,
        [wide(3 * width, BF16), wide(3 * width, BF16), wide(features, BF16)],
        space_dq, space_keep, space_got_grads, space_own, space_far,
    )
    second_got = x_swap(second_part)
    space_grad_far, space_grad_own = [
        local_call(
            name,
            partial(space_grads_kernel, group),
            [shaped((features, 4 * width), BF16)],
            second, grad, grad_two_low, space_heads,
        )[0]
        for name, group, grad in (("space_grads_far", 1, grad_space_far), ("space_grads_own", 0, grad_space))
    ]

    def whole(name, value):
        (out,) = local_call(
            name, whole_rows_kernel, [shaped((count, features), F32)], place, value, core_swap(value), smem=(0,)
        )
        return out

    (layer_half,) = local_call(
        "layer_out", layer_out_kernel, [wide(features, F32)], stream_two, feed_part, feed_part_got, vec
    )
    layer_rows = whole("layer_rows", after(layer_half, space_got_grads))
    up_shards, (second_got, layer_rows) = together(up_shards, [second_got, layer_rows])
    ((space_y_send, space_keep),) = split_rows("split_space", [(space_grad_own, core_swap(space_grad_far))])
    space_y = [dp_swap(space_y_send, 1)]
    grad_one, grad_one_low, sums_one, time_grad_own, time_grad_send = local_call(
        "time_back_in",
        time_back_in_kernel,
        [
            wide(features, F32),
            wide(features, BF16),
            shaped((8, features), F32),
            wide(width, BF16),
            wide(width, BF16),
        ],
        second_part, second_got, stream_one, vec, grad_two, fused, fused_far,
    )
    down_y, (time_grad_own, time_grad_send, grad_one_low) = together(
        down_y, [time_grad_own, time_grad_send, grad_one_low]
    )
    down_shards = z_swaps(y_sums("sum_down", [(down_keep, down_y)]))
    time_grad_got = core_swap(time_grad_send)
    fused_grad, fused_grad_far = local_call(
        "fused_grads",
        fused_grads_kernel,
        [shaped((features, width + SPARE), F32), shaped((features, width + SPARE), BF16)],
        grad_one_low, time_own, time_got,
    )
    fused_grad_got = core_swap(fused_grad_far)
    grad_time_out, fused_total, row_sum, bias_grad = local_call(
        "mix_grads",
        mix_grads_kernel,
        [
            shaped((features, width), BF16),
            shaped((features, width), BF16),
            shaped((features, SPARE), F32),
            shaped((8, features), F32),
        ],
        place, fused_grad, fused_grad_got, mix_blocks, sums_one,
        smem=(0,),
    )
    ((out_send, out_keep),) = split_rows("split_out", [(grad_time_out, None), (fused_total, None)])
    out_send, time_grad_own, time_grad_got = lax.optimization_barrier((out_send, time_grad_own, time_grad_got))
    out_y = [dp_swap(out_send, 1)]
    (grad_time,) = local_call(
        "time_backward",
        time_backward_kernel,
        [shaped((count, 3 * width), BF16)],
        time_grad_own, time_grad_got, order, time_inputs, time_logs, time_col, time_row,
        scratch=[pltpu.VMEM((count, width), BF16), pltpu.VMEM((count, 2 * width), F32)],
    )
    down_shards, space_y, out_y, (grad_time,) = together(down_shards, space_y, out_y, [grad_time])
    time_columns = 3 * width + SPARE
    time_send, time_keep = local_call(
        "time_grads",
        time_grads_kernel,
        [shaped((half, shard, time_columns), BF16), shaped((half, shard, time_columns), F32)],
        place, first, grad_time, row_sum,
        smem=(0,),
        scratch=[pltpu.VMEM((features, time_columns), F32)],
    )
    space_y, out_y, (time_send, grad_time) = together(space_y, out_y, [time_send, grad_time])
    time_y = [dp_swap(time_send, 1)]
    late_shards = z_swaps(y_sums("sum_late", [(out_keep, out_y), (space_keep, space_y)]))
    first_own, first_send, vector_sum = local_call(
        "time_back",
        time_back_kernel,
        [wide(features, BF16), wide(features, BF16), shaped((16, features), F32)],
        grad_time, time_maps, tokens_sorted, back, bias_grad, sums_one, sums_two,
        scratch=[pltpu.VMEM((count, features), BF16)],
    )
    time_y, late_shards, (first_send,) = together(time_y, late_shards, [first_send])
    first_part = (first_own.astype(F32) + core_swap(first_send).astype(F32)).astype(BF16)
    first_part_got = x_swap(first_part)
    time_shards = y_sums("sum_time", [(time_keep, time_y)])
    time_shards = z_swaps(time_shards)

    out_width = 2 * width
    out_total = sum([one[:, :out_width].astype(F32) for one in late_shards])
    mix_keep, mix_send = local_call(
        "mix_shard",
        mix_shard_kernel,
        [shaped((shard, out_width), F32), shaped((shard, out_width), BF16)],
        place, out_total[:, width:], out_map,
        smem=(0,),
    )
    mix_sum = mix_keep + core_swap(mix_send).astype(F32)
    mix_total = mix_sum[:, :width] + x_swap(mix_sum[:, width:].astype(BF16)).astype(F32)

    (grad_half,) = local_call(
        "input_grad", input_grad_kernel, [wide(features, F32)], first_part, first_part_got, tokens_own, vec, grad_one
    )
    bias_part = lax.dynamic_slice_in_dim(vec[2:3], lax.axis_index("heads") * width, width, 1)
    late = [out_width, out_width + 4 * width]
    early_grad, early_square = local_call(
        "early_grad",
        partial(early_grad_kernel, (late, [0, hidden], [0, hidden])),
        [shaped((shard, 4 * width + 2 * hidden), F32), shaped((1, features), F32)],
        *late_shards, *up_shards, *down_shards,
        staged=True,
    )
    time_shards, (mix_total, early_grad) = together(time_shards, [mix_total, early_grad])
    weight_grad, sums = local_call(
        "whole_grad",
        whole_grad_kernel,
        [shaped(weights.shape, F32), shaped((16, features), F32)],
        early_grad, early_square, vector_sum, bias_part, out_total, mix_total, *time_shards,
        staged=True,
    )
    sums, grad_half = lax.optimization_barrier((sums, grad_half))
    grad_rows = whole("grad_rows", grad_half)
    sums = all_sum(sums)
    vector_all = sums[:VECTORS]
    vector_grad = lax.dynamic_slice_in_dim(vector_all, lax.axis_index("dp") * shard, shard, 1)
    grad_norm = jnp.sqrt(sums[VECTORS, 0] + jnp.sum(vector_all * vector_all))
    limit = 0.5 * math.sqrt(NPARAM)
    factor = limit / jnp.maximum(grad_norm, limit)
    weights_out = adam_update(
        weights, weights_m, weights_v, weights_ema, weight_grad, factor, MATRIX_RATE, MATRIX_DECAY
    )
    vectors_out = adam_update(vectors, vectors_m, vectors_v, vectors_ema, vector_grad, factor, VECTOR_RATE, 0.0)

    return (
        layer_rows,
        grad_rows,
        weight_grad,
        vector_grad,
        grad_norm,
        *weights_out,
        *vectors_out,
    )


def solution(mesh):
    rows, square, line = P("dp", None), P("dp", "heads"), P(None, "dp")
    placed = (rows,) * 5 + (square,) * 4 + (line,) * 4
    return jax.shard_map(
        local,
        mesh=mesh,
        in_specs=placed,
        out_specs=(rows, rows, square, line, P()) + (square,) * 4 + (line,) * 4,
        check_vma=False,
    )
```

```python
import math
from functools import partial

import jax
import jax.numpy as jnp
from jax import lax
from jax.experimental import pallas as pl
from jax.experimental.pallas import tpu as pltpu
from jax.sharding import PartitionSpec as P

HEAD_DIM = 64
STEP = 5
NPARAM = 10034688
VECTORS = 10

NORM_EPS = 1e-06
BETA_FIRST = 0.5
BETA_SECOND = 0.5
AVERAGE_RATE = 0.5
MATRIX_RATE = 0.03
VECTOR_RATE = 0.3
MATRIX_DECAY = 0.05
ADAM_EPS = 1e-08
MASKED = -1e30
SCALE = HEAD_DIM ** (-0.5)
F32 = jnp.float32
BF16 = jnp.bfloat16

BLOCK = 128
WINDOW = 256
CLASSES = 16
CHUNK = 256
UNROLL = 4
SPARE = 64
LONG = 40_000_000_000

VMEM = pl.BlockSpec(memory_space=pltpu.VMEM)
SMEM = pl.BlockSpec(memory_space=pltpu.SMEM)
ANY = pl.BlockSpec(memory_space=pl.ANY)


def core_swap(value):
    return lax.ppermute(value, "heads", [(i, i ^ 1) for i in range(4)])


def x_swap(value):
    return lax.ppermute(value, "heads", [(i, i ^ 2) for i in range(4)])


def dp_swap(value, mask):
    count = lax.axis_size("dp")
    return lax.ppermute(value, "dp", [(i, i ^ mask) for i in range(count)])


def all_sum(value, early, late):
    count = lax.axis_size("dp") * lax.axis_size("heads")
    value = value + core_swap(value)
    step, made = 2, None
    while step < count:
        masks = [step, 2 * step, 3 * step] if 2 * step < count else [step]
        got = [lax.ppermute(value, ("dp", "heads"), [(i, i ^ mask) for i in range(count)]) for mask in masks]
        step *= 4
        if made is None:
            made = early(value)
            got, made = together(got, made)
        if step >= count:
            break
        value = value + got[0]
        if len(got) > 1:
            value = value + (got[1] + got[2])
    made = late(value, *made)
    got, made = together(got, made)
    return [value, *got], made


def after(value, *others):
    return lax.optimization_barrier((value, *others))[0]


def together(*groups):
    flat = lax.optimization_barrier([one for group in groups for one in group])
    split, at = [], 0
    for group in groups:
        split.append(list(flat[at : at + len(group)]))
        at += len(group)
    return split


def shaped(shape, dtype):
    return jax.ShapeDtypeStruct(shape, dtype)


def local_call(name, kernel, outs, *operands, scratch=(), smem=(), extra=6, flops=0, staged=False):
    spec = VMEM
    if staged:
        spec, inner, count = ANY, kernel, len(operands)
        moved = [i for i in range(count) if i not in smem]

        def kernel(*refs):
            ins, rest, held, sem = list(refs[:count]), refs[count : -1 - len(moved)], refs[-1 - len(moved) : -1], refs[-1]
            copies = [pltpu.make_async_copy(ins[i], ref, sem.at[j]) for j, (i, ref) in enumerate(zip(moved, held))]
            for copy in copies:
                copy.start()
            for copy, i, ref in zip(copies, moved, held):
                copy.wait()
                ins[i] = ref
            inner(*ins, *rest)

        scratch = [*scratch, *[pltpu.VMEM(operands[i].shape, operands[i].dtype) for i in moved]]
    held = sum(math.prod(one.shape) * jnp.dtype(one.dtype).itemsize for one in scratch)
    return pl.pallas_call(
        kernel,
        name=name,
        out_shape=list(outs),
        in_specs=[SMEM if i in smem else spec for i in range(len(operands))],
        out_specs=[VMEM] * len(outs),
        scratch_shapes=[*scratch, *([pltpu.SemaphoreType.DMA((len(moved),))] if staged else [])],
        compiler_params=pltpu.CompilerParams(
            vmem_limit_bytes=held + extra * 2**20
        ),
        cost_estimate=pl.CostEstimate(flops=flops, bytes_accessed=0, transcendentals=0),
    )(*operands)


def dot(left, right):
    return jnp.dot(left, right, preferred_element_type=F32)


def dot_nt(left, right):
    return lax.dot_general(left, right, (((1,), (1,)), ((), ())), preferred_element_type=F32)


def dot_tn(left, right):
    return lax.dot_general(left, right, (((0,), (0,)), ((), ())), preferred_element_type=F32)


def chunk_loop(rows, body, size=CHUNK):
    def step(i, carry):
        body(pl.ds(pl.multiple_of(i * size, size), size))
        return carry

    lax.fori_loop(0, rows // size, step, 0)


def normed(stream):
    center = stream - jnp.mean(stream, -1, keepdims=True)
    factor = lax.rsqrt(jnp.mean(center * center, -1, keepdims=True) + NORM_EPS)
    return center * factor, factor


def norm_grad(hat, factor, gain, grad):
    scaled = grad * gain
    return factor * (
        scaled - jnp.mean(scaled, -1, keepdims=True) - hat * jnp.mean(scaled * hat, -1, keepdims=True)
    )


def column_sum(value):
    return jnp.sum(value, 0, keepdims=True)


def z_blocks(piece):
    return [piece] + [dp_swap(piece, 2 * k) for k in range(1, lax.axis_size("dp") // 2)]


def y_blocks(mine, fine=False):
    return [dp_swap(one, 1) for one in mine] if fine else [dp_swap(jnp.stack(mine), 1)]


def assemble(name, mine, other, cuts=()):
    half, count, fine = len(mine), lax.axis_size("dp"), len(other) > 1
    rows, columns = mine[0].shape
    bounds = [0, *cuts, columns]
    parts = [slice(start, stop) for start, stop in zip(bounds, bounds[1:])]

    def kernel(place_ref, *refs):
        z, y = place_ref[0], place_ref[1]
        for out_ref, part in zip(refs[half + len(other) :], parts):
            for k in range(half):
                out_ref[(z ^ k) * 2 + y] = refs[k][:, part]
                out_ref[(z ^ k) * 2 + (1 - y)] = refs[half + k][:, part] if fine else refs[half][k, :, part]

    outs = local_call(
        name,
        kernel,
        [shaped((count, rows, part.stop - part.start), mine[0].dtype) for part in parts],
        places(), *mine, *other,
        smem=(0,),
    )
    outs = [one.reshape(count * rows, -1) for one in outs]
    return outs if cuts else outs[0]


def places():
    dp, heads = lax.axis_index("dp"), lax.axis_index("heads")
    return jnp.stack([dp // 2, dp % 2, heads, heads % 2, dp]).astype(jnp.int32)


def split_rows(name, totals, cuts=()):
    count = lax.axis_size("dp")
    half = count // 2
    operands, columns = [], 0
    for own, received in totals:
        rows = own.shape[0] // count
        operands += [one.reshape(count, rows, own.shape[1]) for one in (own, received) if one is not None]
        columns += own.shape[1]
    bounds = [0, *cuts, columns]
    parts = list(zip(bounds, bounds[1:]))

    def kernel(place_ref, *refs):
        ins, outs = refs[: len(operands)], refs[len(operands) :]
        z, y = place_ref[0], place_ref[1]
        for k in range(half):
            for side in range(2):
                block = (z ^ k) * 2 + (1 - y if side == 0 else y)
                at, column = 0, 0
                for own, received in totals:
                    value = ins[at][block].astype(F32)
                    at += 1
                    if received is not None:
                        value = value + ins[at][block].astype(F32)
                        at += 1
                    for i, (start, stop) in enumerate(parts):
                        first, last = max(start, column), min(stop, column + own.shape[1])
                        if first < last:
                            ref = outs[2 * i + side]
                            ref[k, :, first - start : last - start] = value[:, first - column : last - column].astype(
                                ref.dtype
                            )
                    column += own.shape[1]

    outs = []
    for start, stop in parts:
        outs += [shaped((half, rows, stop - start), BF16), shaped((half, rows, stop - start), F32)]
    outs = local_call(name, kernel, outs, places(), *operands, smem=(0,))
    return list(zip(outs[::2], outs[1::2]))


def y_sums(name, pieces, flops=0):
    half, rows, _ = pieces[0][0].shape
    columns = [keep.shape[2] for keep, _ in pieces]
    fine = len(pieces[0][1]) > 1
    operands = [one for keep, arrived in pieces for one in (keep, *arrived)]
    step = 1 + len(pieces[0][1])

    def kernel(*refs):
        ins, outs = refs[: len(operands)], refs[len(operands) :]
        column = 0
        for i, width in enumerate(columns):
            part = slice(column, column + width)
            column += width
            for k in range(half):
                there = ins[i * step + 1 + k][...] if fine else ins[i * step + 1][k]
                value = ins[i * step][k] + there.astype(F32)
                outs[k][:, part] = value.astype(outs[k].dtype)

    outs = [shaped((rows, sum(columns)), F32)] + [shaped((rows, sum(columns)), BF16)] * (half - 1)
    return local_call(name, kernel, outs, *operands, flops=flops)


def z_swaps(summed):
    return [summed[0]] + [dp_swap(summed[k], 2 * k) for k in range(1, len(summed))]


def head_pairs(width):
    pair = 2 * HEAD_DIM
    return [(at, min(at + pair, width), min(2, (width - at) // HEAD_DIM)) for at in range(0, width, pair)]


def by_head(value, heads):
    if heads == 1:
        return value
    lane = lax.broadcasted_iota(jnp.int32, value.shape, 1)
    zero = jnp.zeros_like(value)
    return jnp.concatenate(
        [jnp.where(lane < HEAD_DIM, value, zero), jnp.where(lane < HEAD_DIM, zero, value)], 0
    )


def own_columns(value, heads):
    if heads == 1:
        return value
    count = value.shape[1] // 2
    return jnp.concatenate([value[:HEAD_DIM, :count], value[HEAD_DIM:, count:]], 0)


def own_rows(value, heads):
    if heads == 1:
        return value
    count = value.shape[0] // 2
    lane = lax.broadcasted_iota(jnp.int32, (count, value.shape[1]), 1)
    return jnp.where(lane < HEAD_DIM, value[:count], value[count:])


def masked_bias(allowed):
    return jnp.where(allowed, 0.0, MASKED).astype(F32)


def pair_forward(q, keys, values, bias, heads):
    scores = dot_nt(keys, by_head(q, heads)) + (bias if heads == 1 else jnp.concatenate([bias, bias], 1))
    top = jnp.max(scores, 0, keepdims=True)
    exps = jnp.exp(scores - top)
    total = jnp.sum(exps, 0, keepdims=True)
    out = dot_tn(values, exps.astype(BF16)) / total
    log = top + jnp.log(total)
    count = q.shape[0]
    return own_columns(out, heads), [log[:, h * count : (h + 1) * count] for h in range(heads)]


def pair_backward(q, grad, keys, values, bias, logs, heads):
    q, grad = by_head(q, heads), by_head(grad, heads)
    if heads > 1:
        bias, logs = jnp.concatenate([bias, bias], 1), [jnp.concatenate(logs, 1)]
    probs = jnp.exp(dot_nt(keys, q) + bias - logs[0])
    grad_probs = dot_nt(values, grad)
    delta = jnp.sum(probs * grad_probs, 0, keepdims=True)
    grad_scores = (probs * (grad_probs - delta)).astype(BF16)
    grad_q = own_columns(dot_tn(keys, grad_scores), heads) * SCALE
    return grad_q, dot(grad_scores, q), dot(probs.astype(BF16), grad)


def sort_kernel(
    place_ref, clip_ref, frame_ref, patch_ref, tokens_ref, dy_ref,
    sorted_ref, order_ref, back_ref, col_ref, row_ref, space_col_ref, space_row_ref, own_ref, own_dy_ref,
    all_ref,
):
    count = tokens_ref.shape[0]
    rows = count // 2
    core = place_ref[3]
    own = pl.ds(pl.multiple_of(core * rows, rows), rows)
    far = pl.ds(pl.multiple_of((1 - core) * rows, rows), rows)
    own_ref[...] = tokens_ref[own, :]
    own_dy_ref[...] = dy_ref[own, :]
    all_ref[:rows, :] = tokens_ref[own, :]
    all_ref[rows:, :] = tokens_ref[far, :]
    ids = [clip_ref, frame_ref, patch_ref]
    spare = jnp.zeros((5, count), jnp.int32)
    natural = jnp.concatenate([ref[...] for ref in ids] + [spare], 0)
    space_row_ref[...] = natural
    space_col_ref[...] = natural.astype(F32).T.astype(jnp.int32)
    ordered = jnp.concatenate(
        [jnp.concatenate([ref[:, own], ref[:, far]], 1) for ref in ids] + [spare], 0
    )
    ordered_col = ordered.astype(F32).T.astype(jnp.int32)
    key_row = (ordered[0:1] * 128 + ordered[2:3] + 1) * 64 + ordered[1:2] + 1
    key_col = (ordered_col[:, 0:1] * 128 + ordered_col[:, 2:3] + 1) * 64 + ordered_col[:, 1:2] + 1
    rank_row = jnp.zeros((1, count), jnp.int32)
    for i in range(0, count, CHUNK):
        smaller = key_col[i : i + CHUNK] < key_row
        rank_row = rank_row + jnp.sum(smaller.astype(jnp.int32), 0, keepdims=True)
    for i in range(0, count, CHUNK):
        at = slice(i, i + CHUNK)
        place = lax.broadcasted_iota(jnp.int32, (CHUNK, count), 0) + i
        order = (place == rank_row).astype(F32).astype(BF16)
        order_ref[at, :] = order
        rank_col = jnp.sum((key_row < key_col[at]).astype(jnp.int32), 1, keepdims=True)
        place = lax.broadcasted_iota(jnp.int32, (CHUNK, count), 1)
        back_ref[at, :] = (place == rank_col).astype(F32).astype(BF16)
        sorted_ref[at, :] = dot(order, all_ref[...]).astype(BF16)
        col_ref[at, :] = dot(order, ordered_col.astype(F32).astype(BF16))
        row_ref[:, at] = dot_nt(ordered.astype(F32).astype(BF16), order)


def pack_kernel(weights_ref, vectors_ref, head_ref, space_ref, up_ref, down_ref):
    width, hidden = space_ref.shape[1] // 4, up_ref.shape[1]
    rows = weights_ref.shape[0]
    start = head_ref.shape[1] - 2 * width
    unit = lax.broadcasted_iota(jnp.int32, (rows, rows), 0) == lax.broadcasted_iota(jnp.int32, (rows, rows), 1)
    vectors = jnp.concatenate([vectors_ref[...], jnp.zeros((16 - VECTORS, rows), F32)], 0).astype(BF16)
    head_ref[:, : 3 * width] = weights_ref[:, : 3 * width].astype(BF16)
    head_ref[:, 3 * width : start] = jnp.zeros((rows, start - 3 * width), BF16)
    head_ref[:, 3 * width : 3 * width + 16] = dot_nt(unit.astype(F32).astype(BF16), vectors).astype(BF16)
    head_ref[:, start : start + width] = weights_ref[:, 4 * width : 5 * width].astype(BF16)
    head_ref[:, start + width :] = weights_ref[:, 3 * width : 4 * width].astype(BF16)
    space_ref[...] = weights_ref[:, 5 * width : 9 * width].astype(BF16)
    up_ref[...] = weights_ref[:, 9 * width : 9 * width + hidden].astype(BF16)
    down_ref[...] = weights_ref[:, 9 * width + hidden :].astype(BF16)


def same_clip_patch(col_ref, row_ref, keys, queries):
    key = col_ref[keys, :]
    query = row_ref[:, queries]
    return (key[:, 0:1] * 128 + key[:, 2:3]) == (query[0:1] * 128 + query[2:3])


def temporal_window(i, count):
    first = i * BLOCK
    start = jnp.clip(first - (WINDOW - BLOCK) // 2, 0, count - WINDOW)
    return (
        pl.ds(pl.multiple_of(first, BLOCK), BLOCK),
        pl.ds(pl.multiple_of(start, (WINDOW - BLOCK) // 2), WINDOW),
    )


def time_forward_kernel(
    maps_ref, tokens_ref, back_ref, col_ref, row_ref,
    vec_ref, first_ref, inputs_ref, own_ref, far_ref, log_ref, heads_ref,
):
    count, width = tokens_ref.shape[0], own_ref.shape[1]
    columns = maps_ref.shape[1]
    lanes = maps_ref[:, columns - 128 :].astype(F32).T
    offset = 3 * width - (columns - 128)
    vec_ref[...] = lanes[offset : offset + 16]
    gain, shift = vec_ref[0:1], vec_ref[1:2]

    def project(at):
        hat, _ = normed(tokens_ref[at, :].astype(F32))
        first = (hat * gain + shift).astype(BF16)
        first_ref[at, :] = first
        inputs_ref[at, :] = dot(first, maps_ref[:, : 3 * width]).astype(BF16)

    chunk_loop(count, project)

    def step(i, carry):
        queries, keys = temporal_window(i, count)
        bias = masked_bias(same_clip_patch(col_ref, row_ref, keys, queries))
        outs, logs = [], []
        for start, stop, heads in head_pairs(width):
            out, log = pair_forward(
                inputs_ref[queries, start:stop] * BF16(SCALE),
                inputs_ref[keys, width + start : width + stop],
                inputs_ref[keys, 2 * width + start : 2 * width + stop],
                bias,
                heads,
            )
            outs.append(out)
            logs += log
        heads_ref[queries, :] = jnp.concatenate(outs, 0).T.astype(BF16)
        log_ref[:, queries] = jnp.concatenate(logs + [logs[0]] * (8 - len(logs)), 0)
        return carry

    lax.fori_loop(0, count // BLOCK, step, 0, unroll=8)
    rows = count // 2
    for i in range(0, rows, CHUNK):
        own_ref[i : i + CHUNK, :] = dot(back_ref[i : i + CHUNK, :], heads_ref[...]).astype(BF16)
        far_ref[i : i + CHUNK, :] = dot(back_ref[rows + i : rows + i + CHUNK, :], heads_ref[...]).astype(BF16)


def time_backward_kernel(
    own_ref, far_ref, order_ref, inputs_ref, log_ref, col_ref, row_ref,
    out_ref, grad_ref, sum_ref,
):
    count, width = inputs_ref.shape[0], own_ref.shape[1]
    rows = count // 2
    for i in range(0, count, CHUNK):
        grad_ref[i : i + CHUNK, :] = (
            dot(order_ref[i : i + CHUNK, :rows], own_ref[...]) + dot(order_ref[i : i + CHUNK, rows:], far_ref[...])
        ).astype(BF16)
    sum_ref[...] = jnp.zeros_like(sum_ref)

    def step(i, carry):
        queries, keys = temporal_window(i, count)
        bias = masked_bias(same_clip_patch(col_ref, row_ref, keys, queries))
        grad_qs, head = [], 0
        for start, stop, heads in head_pairs(width):
            grad_q, grad_k, grad_v = pair_backward(
                inputs_ref[queries, start:stop] * BF16(SCALE),
                grad_ref[queries, start:stop],
                inputs_ref[keys, width + start : width + stop],
                inputs_ref[keys, 2 * width + start : 2 * width + stop],
                bias,
                [log_ref[h : h + 1, queries] for h in range(head, head + heads)],
                heads,
            )
            head += heads
            grad_qs.append(grad_q)
            sum_ref[keys, start:stop] += grad_k
            sum_ref[keys, width + start : width + stop] += grad_v
        out_ref[queries, :width] = jnp.concatenate(grad_qs, 0).T.astype(BF16)
        return carry

    lax.fori_loop(0, count // BLOCK, step, 0, unroll=8)

    def store(at):
        out_ref[at, width:] = sum_ref[at, :].astype(BF16)

    chunk_loop(count, store)


def space_window(i, core, rows):
    first = core * rows + i * BLOCK
    start = jnp.clip(first - (WINDOW - BLOCK) // 2, 0, 2 * rows - WINDOW)
    return (
        pl.ds(pl.multiple_of(i * BLOCK, BLOCK), BLOCK),
        pl.ds(pl.multiple_of(first, BLOCK), BLOCK),
        pl.ds(pl.multiple_of(start, (WINDOW - BLOCK) // 2), WINDOW),
    )


def whole_pairs(core, pairs_ref, got_ref, whole_ref):
    rows, width = pairs_ref.shape[0], pairs_ref.shape[1] // 4
    whole_ref[pl.ds(pl.multiple_of(core * rows, rows), rows), :] = pairs_ref[...]
    there = pl.ds(pl.multiple_of((1 - core) * rows, rows), rows)
    for i, j in enumerate((1, 0, 3, 2)):
        whole_ref[there, i * width : (i + 1) * width] = got_ref[:, j * width : (j + 1) * width]


def class_rows(row):
    number = lax.broadcasted_iota(jnp.int32, (CLASSES, row.shape[1]), 0)
    return (row[0:1] == number) & (row[1:2] < 0)


def space_bias(col_ref, row_ref, queries, keys):
    key, query = col_ref[keys, :], row_ref[:, queries]
    frame = jnp.where(key[:, 1:2] < 0, -1, key[:, 0:1] * 128 + key[:, 1:2]) == query[0:1] * 128 + query[1:2]
    number = lax.broadcasted_iota(jnp.int32, (CLASSES, BLOCK), 0)
    return masked_bias(jnp.concatenate([frame & (query[1:2] >= 0), number == query[0:1]], 0))


def class_allowed(row_ref):
    number = lax.broadcasted_iota(jnp.int32, (CLASSES, row_ref.shape[1]), 0)
    return row_ref[0:1] == number


def space_forward_kernel(
    place_ref, q_ref, pairs_ref, got_ref, col_ref, row_ref, out_own_ref, out_far_ref,
    heads_ref, log_ref, class_log_ref, part_ref, whole_ref, class_ref,
):
    core = place_ref[3]
    rows, width = q_ref.shape
    whole_pairs(core, pairs_ref, got_ref, whole_ref)
    here = pl.ds(pl.multiple_of(core * rows, rows), rows)
    classes = class_rows(row_ref[...]).astype(F32).astype(BF16)
    own_classes = class_rows(row_ref[:, here]).astype(F32).astype(BF16)
    class_ref[...] = dot(classes, whole_ref[...]).astype(BF16)
    def both(keys, part):
        return jnp.concatenate([whole_ref[keys, part], class_ref[:, part]], 0)

    def step(i, carry):
        local, queries, keys = space_window(i, core, rows)
        bias = space_bias(col_ref, row_ref, queries, keys)
        outs, logs = [], []
        for start, stop, heads in head_pairs(width):
            out, log = pair_forward(
                q_ref[local, start:stop] * BF16(SCALE),
                both(keys, slice(start, stop)),
                both(keys, slice(width + start, width + stop)),
                bias,
                heads,
            )
            outs.append(out)
            logs += log
        heads_ref[local, :] = jnp.concatenate(outs, 0).T.astype(BF16)
        log_ref[:, local] = jnp.concatenate(logs + [logs[0]] * (8 - len(logs)), 0)
        return carry

    lax.fori_loop(0, rows // BLOCK, step, 0, unroll=UNROLL)

    bias = masked_bias(class_allowed(row_ref))
    class_q = dot(own_classes, q_ref[...]).astype(BF16) * BF16(SCALE)
    outs, logs = [], []
    for start, stop, heads in head_pairs(width):
        scores = dot_nt(by_head(class_q[:, start:stop], heads), whole_ref[:, start:stop])
        scores = scores + (bias if heads == 1 else jnp.concatenate([bias, bias], 0))
        top = jnp.max(scores, 1, keepdims=True)
        exps = jnp.exp(scores - top)
        total = jnp.sum(exps, 1, keepdims=True)
        outs.append(own_rows(dot(exps.astype(BF16), whole_ref[:, width + start : width + stop]) / total, heads))
        log = top + jnp.log(total)
        logs += [log[h * CLASSES : (h + 1) * CLASSES] for h in range(heads)]
    class_log_ref[...] = jnp.concatenate(logs + [logs[0]] * (8 - len(logs)), 1)
    class_out = jnp.concatenate(outs, 1).astype(BF16)
    is_class = col_ref[here, 1:2] < 0

    def replace(at):
        back = dot_tn(own_classes, class_out).astype(BF16)
        heads_ref[...] = jnp.where(is_class, back, heads_ref[...])

    replace(None)
    group = width // 2

    def project(at):
        part_ref[at, :] = (
            dot_nt(heads_ref[at, :group], out_own_ref[:, 3 * group :])
            + dot_nt(heads_ref[at, group:], out_far_ref[:, 3 * group :])
        ).astype(BF16)

    chunk_loop(rows, project)


def space_back_in_kernel(
    part_ref, got_ref, stream_ref, vec_ref, dy_ref, out_own_ref, out_far_ref,
    grad_ref, low_ref, sums_ref, heads_ref,
):
    group = heads_ref.shape[1] // 2
    gain = vec_ref[7:8]
    sums_ref[...] = jnp.zeros_like(sums_ref)

    def through_norm(at):
        grad = part_ref[at, :].astype(F32) + got_ref[at, :].astype(F32)
        hat, factor = normed(stream_ref[at, :])
        dy = dy_ref[at, :].astype(F32)
        dx = dy + norm_grad(hat, factor, gain, grad)
        grad_ref[at, :] = dx
        low = dx.astype(BF16)
        low_ref[at, :] = low
        heads_ref[at, :group] = dot(low, out_own_ref[:, 3 * group :]).astype(BF16)
        heads_ref[at, group:] = dot(low, out_far_ref[:, 3 * group :]).astype(BF16)
        sums_ref[0:4] += jnp.concatenate(
            [column_sum(dx), column_sum(grad * hat), column_sum(grad), column_sum(dy)], 0
        )

    chunk_loop(grad_ref.shape[0], through_norm)


def space_backward_kernel(
    place_ref, heads_ref, q_ref, pairs_ref, got_ref, log_ref, class_log_ref, col_ref, row_ref,
    dq_ref, keep_ref, send_ref,
    whole_ref, class_ref, total_ref, class_total_ref, class_dq_ref,
):
    core = place_ref[3]
    rows, width = q_ref.shape
    whole_pairs(core, pairs_ref, got_ref, whole_ref)
    here = pl.ds(pl.multiple_of(core * rows, rows), rows)
    there = pl.ds(pl.multiple_of((1 - core) * rows, rows), rows)
    classes = class_rows(row_ref[...]).astype(F32)
    own_classes = class_rows(row_ref[:, here]).astype(F32).astype(BF16)
    class_ref[...] = dot(classes.astype(BF16), whole_ref[...]).astype(BF16)
    class_total_ref[...] = jnp.zeros_like(class_total_ref)
    bias = masked_bias(class_allowed(row_ref))
    class_q = dot(own_classes, q_ref[...]).astype(BF16) * BF16(SCALE)
    class_g = dot(own_classes, heads_ref[...]).astype(BF16)
    head = 0
    for start, stop, heads in head_pairs(width):
        keys, values = whole_ref[:, start:stop], whole_ref[:, width + start : width + stop]
        q, grad = by_head(class_q[:, start:stop], heads), by_head(class_g[:, start:stop], heads)
        logs = [class_log_ref[:, h : h + 1] for h in range(head, head + heads)]
        head += heads
        scores = dot_nt(q, keys) + (bias if heads == 1 else jnp.concatenate([bias, bias], 0))
        probs = jnp.exp(scores - jnp.concatenate(logs, 0))
        grad_probs = dot_nt(grad, values)
        grad_scores = (probs * (grad_probs - jnp.sum(probs * grad_probs, 1, keepdims=True))).astype(BF16)
        class_dq_ref[:, start:stop] = own_rows(dot(grad_scores, keys) * SCALE, heads).astype(BF16)
        total_ref[:, start:stop] = dot_tn(grad_scores, q)
        total_ref[:, width + start : width + stop] = dot_tn(probs.astype(BF16), grad)

    def both(keys, part):
        return jnp.concatenate([whole_ref[keys, part], class_ref[:, part]], 0)

    def step(i, carry):
        local, queries, keys = space_window(i, core, rows)
        bias = space_bias(col_ref, row_ref, queries, keys)
        is_class = row_ref[1:2, queries] < 0
        grad_qs, head = [], 0
        for start, stop, heads in head_pairs(width):
            key_part, value_part = slice(start, stop), slice(width + start, width + stop)
            grad_q, grad_k, grad_v = pair_backward(
                q_ref[local, start:stop] * BF16(SCALE),
                heads_ref[local, start:stop],
                both(keys, key_part),
                both(keys, value_part),
                bias,
                [jnp.where(is_class, -MASKED, log_ref[h : h + 1, local]) for h in range(head, head + heads)],
                heads,
            )
            head += heads
            grad_qs.append(grad_q)
            total_ref[keys, key_part] += grad_k[:WINDOW]
            total_ref[keys, value_part] += grad_v[:WINDOW]
            class_total_ref[:, key_part] += grad_k[WINDOW:]
            class_total_ref[:, value_part] += grad_v[WINDOW:]
        dq_ref[local, :] = jnp.concatenate(grad_qs, 0).T.astype(BF16)
        return carry

    lax.fori_loop(0, rows // BLOCK, step, 0, unroll=UNROLL)
    dq_ref[...] = jnp.where(
        col_ref[here, 1:2] < 0, dot_tn(own_classes, class_dq_ref[...]).astype(BF16), dq_ref[...]
    )
    high = class_total_ref[...].astype(BF16)
    rest = (class_total_ref[...] - high.astype(F32)).astype(BF16)
    classes = classes.astype(BF16)
    total_ref[...] += dot_tn(jnp.concatenate([classes, classes], 0), jnp.concatenate([high, rest], 0))
    keep_ref[...] = total_ref[here, :]
    send_ref[...] = total_ref[there, :].astype(BF16)


def mix_kernel(place_ref, out_ref, own_ref, x_ref, core_ref, vec_ref, mix_ref, fused_ref, bias_ref):
    place = place_ref[2]
    width = out_ref.shape[1]
    mix_ref[0] = own_ref[...]
    mix_ref[1] = core_ref[:, :width]
    mix_ref[2] = x_ref[...]
    mix_ref[3] = core_ref[:, width:]
    total, bias = 0.0, 0.0
    low = vec_ref[...].astype(BF16)
    for j in range(4):
        block = mix_ref[place ^ j]
        total = total + dot(block, out_ref[j * width : (j + 1) * width, :])
        bias = bias + dot_nt(low[:, j * width : (j + 1) * width], block)
    fused_ref[...] = total.astype(BF16)
    bias_ref[...] = bias[2:3] + vec_ref[3:4]


def time_out_kernel(own_ref, got_ref, fused_ref, far_ref, part_ref):
    def project(at):
        part_ref[at, :] = (dot_nt(own_ref[at, :], fused_ref[...]) + dot_nt(got_ref[at, :], far_ref[...])).astype(BF16)

    chunk_loop(part_ref.shape[0], project)


def norm_in_kernel(gain_row, before_ref, part_ref, got_ref, shift_ref, vec_ref, stream_ref, normed_ref):
    gain, shift = vec_ref[gain_row : gain_row + 1], vec_ref[gain_row + 1 : gain_row + 2]

    def body(at):
        stream = (
            before_ref[at, :].astype(F32)
            + (part_ref[at, :].astype(F32) + got_ref[at, :].astype(F32))
            + shift_ref[0:1]
        )
        stream_ref[at, :] = stream
        hat, _ = normed(stream)
        normed_ref[at, :] = (hat * gain + shift).astype(BF16)

    chunk_loop(stream_ref.shape[0], body)


def space_in_kernel(second_ref, own_ref, far_ref, q_ref, pairs_ref):
    width = q_ref.shape[1] // 2

    def project(at):
        for g, maps_ref in enumerate((own_ref, far_ref)):
            inputs = dot(second_ref[at, :], maps_ref[:, : 3 * width]).astype(BF16)
            q_ref[at, g * width : (g + 1) * width] = inputs[:, :width]
            pairs_ref[at, g * width : (g + 1) * width] = inputs[:, width : 2 * width]
            pairs_ref[at, (2 + g) * width : (3 + g) * width] = inputs[:, 2 * width :]

    chunk_loop(q_ref.shape[0], project)


def gelu_parts(pre):
    cdf = 0.5 * (1.0 + lax.erf(pre * (0.5**0.5)))
    slope = cdf + pre * jnp.exp(-0.5 * pre * pre) * (1.0 / math.sqrt(2.0 * math.pi))
    return pre * cdf, slope


def feed_kernel(
    third_ref, dy_ref, up_ref, up_far_ref, down_ref, down_far_ref, activ_ref, grad_ref, back_ref
):
    hidden = activ_ref.shape[1] // 2

    def project(at):
        back = 0.0
        for g, (ups_ref, downs_ref) in enumerate(((up_ref, down_ref), (up_far_ref, down_far_ref))):
            act, slope = gelu_parts(dot(third_ref[at, :], ups_ref[...]))
            part = slice(g * hidden, (g + 1) * hidden)
            activ_ref[at, part] = act.astype(BF16)
            grad = (dot(dy_ref[at, :], downs_ref[...]) * slope).astype(BF16)
            grad_ref[at, part] = grad
            back = back + dot_nt(grad, ups_ref[...])
        back_ref[at, :] = back.astype(BF16)

    chunk_loop(third_ref.shape[0], project)


def feed_out_kernel(activ_ref, own_ref, far_ref, part_ref):
    hidden = activ_ref.shape[1] // 2

    def project(at):
        part_ref[at, :] = (
            dot_nt(activ_ref[at, :hidden], own_ref[...]) + dot_nt(activ_ref[at, hidden:], far_ref[...])
        ).astype(BF16)

    chunk_loop(part_ref.shape[0], project)


def feed_grads_kernel(group, third_ref, grad_ref, dy_ref, activ_ref, out_ref):
    hidden = out_ref.shape[1] // 2
    part = slice(group * hidden, (group + 1) * hidden)
    out_ref[:, :hidden] = dot_tn(third_ref[...], grad_ref[:, part]).astype(BF16)
    out_ref[:, hidden:] = dot_tn(dy_ref[...], activ_ref[:, part]).astype(BF16)


def space_back_kernel(
    dq_ref, keep_ref, got_ref, own_ref, far_ref, grad_own_ref, grad_far_ref, part_ref
):
    width = dq_ref.shape[1] // 2

    def project(at):
        total = 0.0
        for g, (maps_ref, grad_ref) in enumerate(((own_ref, grad_own_ref), (far_ref, grad_far_ref))):
            grad_ref[at, :width] = dq_ref[at, g * width : (g + 1) * width]
            for i in (1, 2):
                mine = slice((2 * i - 2 + g) * width, (2 * i - 1 + g) * width)
                theirs = slice((2 * i - 1 - g) * width, (2 * i - g) * width)
                grad_ref[at, i * width : (i + 1) * width] = (
                    keep_ref[at, mine] + got_ref[at, theirs].astype(F32)
                ).astype(BF16)
            total = total + dot_nt(grad_ref[at, :], maps_ref[:, : 3 * width])
        part_ref[at, :] = total.astype(BF16)

    chunk_loop(part_ref.shape[0], project)


def space_grads_kernel(group, second_ref, grad_ref, low_ref, heads_ref, out_ref):
    width = heads_ref.shape[1] // 2
    out_ref[:, : 3 * width] = dot_tn(second_ref[...], grad_ref[...]).astype(BF16)
    out_ref[:, 3 * width :] = dot_tn(low_ref[...], heads_ref[:, group * width : (group + 1) * width]).astype(BF16)


def time_back_in_kernel(
    part_ref, got_ref, stream_ref, vec_ref, before_ref, fused_ref, far_ref,
    grad_ref, low_ref, sums_ref, own_ref, send_ref,
):
    gain = vec_ref[4:5]
    sums_ref[...] = jnp.zeros_like(sums_ref)

    def through_norm(at):
        grad = part_ref[at, :].astype(F32) + got_ref[at, :].astype(F32)
        hat, factor = normed(stream_ref[at, :])
        dx = before_ref[at, :] + norm_grad(hat, factor, gain, grad)
        grad_ref[at, :] = dx
        low = dx.astype(BF16)
        low_ref[at, :] = low
        own_ref[at, :] = dot(low, fused_ref[...]).astype(BF16)
        send_ref[at, :] = dot(low, far_ref[...]).astype(BF16)
        sums_ref[0:4] += jnp.concatenate(
            [column_sum(low.astype(F32)), column_sum(dx), column_sum(grad * hat), column_sum(grad)], 0
        )

    chunk_loop(grad_ref.shape[0], through_norm)


def time_grads_kernel(place_ref, first_ref, grad_ref, row_sum_ref, send_ref, keep_ref, total_ref):
    half, rows, columns = keep_ref.shape
    width = columns - row_sum_ref.shape[1]
    z, y = place_ref[0], place_ref[1]
    total_ref[:, :width] = dot_tn(first_ref[...], grad_ref[...])
    total_ref[:, width:] = row_sum_ref[...]
    for k in range(half):
        mine = pl.ds(pl.multiple_of(((z ^ k) * 2 + y) * rows, 8), rows)
        theirs = pl.ds(pl.multiple_of(((z ^ k) * 2 + (1 - y)) * rows, 8), rows)
        send_ref[k] = total_ref[theirs, :].astype(BF16)
        keep_ref[k] = total_ref[mine, :]


def time_back_kernel(
    grad_ref, maps_ref, tokens_ref, back_ref, bias_ref, one_ref, two_ref, own_ref, far_ref, sums_ref, sorted_ref
):
    count, width = tokens_ref.shape[0], grad_ref.shape[1] // 3
    sums_ref[...] = jnp.zeros_like(sums_ref)
    sums_ref[2:3] = 0.5 * bias_ref[0:1]
    sums_ref[3:6] = 0.5 * one_ref[1:4]
    sums_ref[6:10] = 0.5 * two_ref[0:4]

    def project(at):
        grad = dot_nt(grad_ref[at, :], maps_ref[:, : 3 * width])
        hat, _ = normed(tokens_ref[at, :].astype(F32))
        sums_ref[0:2] += jnp.concatenate([column_sum(grad * hat), column_sum(grad)], 0)
        sorted_ref[at, :] = grad.astype(BF16)

    chunk_loop(count, project)
    rows = count // 2
    for i in range(0, rows, CHUNK):
        far_ref[i : i + CHUNK, :] = dot(back_ref[rows + i : rows + i + CHUNK, :], sorted_ref[...]).astype(BF16)
    for i in range(0, rows, CHUNK):
        own_ref[i : i + CHUNK, :] = dot(back_ref[i : i + CHUNK, :], sorted_ref[...]).astype(BF16)


def input_grad_kernel(part_ref, got_ref, tokens_ref, vec_ref, before_ref, out_ref):
    gain = vec_ref[0:1]

    def through_norm(at):
        grad = part_ref[at, :].astype(F32) + got_ref[at, :].astype(F32)
        hat, factor = normed(tokens_ref[at, :].astype(F32))
        out_ref[at, :] = before_ref[at, :] + norm_grad(hat, factor, gain, grad)

    chunk_loop(out_ref.shape[0], through_norm)


def layer_out_kernel(stream_ref, part_ref, got_ref, vec_ref, out_ref):
    out_ref[...] = stream_ref[...] + (part_ref[...].astype(F32) + got_ref[...].astype(F32)) + vec_ref[9:10]


def whole_rows_kernel(place_ref, own_ref, got_ref, out_ref, sem):
    core = place_ref[3]
    rows = own_ref.shape[0]
    copies = [
        pltpu.make_async_copy(ref, out_ref.at[pl.ds(pl.multiple_of(at * rows, rows), rows)], sem.at[i])
        for i, (ref, at) in enumerate(((own_ref, core), (got_ref, 1 - core)))
    ]
    for copy in copies:
        copy.start()
    for copy in copies:
        copy.wait()


def fused_grads_kernel(low_ref, heads_ref, got_heads_ref, own_ref, far_ref):
    ones = jnp.ones((low_ref.shape[0], own_ref.shape[1] - heads_ref.shape[1]), BF16)
    far_ref[...] = dot_tn(low_ref[...], jnp.concatenate([got_heads_ref[...], ones], 1)).astype(BF16)
    own_ref[...] = dot_tn(low_ref[...], jnp.concatenate([heads_ref[...], ones], 1))


def mix_grads_kernel(
    place_ref, fused_ref, got_ref, mix_ref, sums_ref, grad_out_ref, total_ref, row_sum_ref, bias_ref
):
    place = place_ref[2]
    width = total_ref.shape[1]
    both = fused_ref[...] + got_ref[...].astype(F32)
    row_sum_ref[...] = both[:, width:]
    fused = both[:, :width].astype(BF16)
    total_ref[...] = fused
    for j in range(4):
        block = mix_ref[place ^ j]
        grad_out_ref[j * width : (j + 1) * width, :] = dot_tn(block, fused).astype(BF16)
        bias_ref[:, j * width : (j + 1) * width] = dot(sums_ref[...].astype(BF16), block)


def mix_shard_kernel(place_ref, out_ref, *refs):
    ins, (grad_ref, keep_ref, send_ref) = refs[:-3], refs[-3:]
    place = place_ref[2]
    width = out_ref.shape[1]
    total = sum(ref[:, : 2 * width].astype(F32) for ref in ins)
    grad_ref[...] = total[:, :width]
    fused = total[:, width:].astype(BF16)
    for m in range(4):
        rows = out_ref[pl.ds(pl.multiple_of((place ^ m) * width, width), width), :]
        part = dot_nt(fused, rows)
        ref = send_ref if m % 2 else keep_ref
        ref[:, m // 2 * width : (m // 2 + 1) * width] = part.astype(ref.dtype)


def mix_sum_kernel(keep_ref, got_ref, own_ref, send_ref):
    width = own_ref.shape[1]
    total = keep_ref[...] + got_ref[...].astype(F32)
    own_ref[...] = total[:, :width]
    send_ref[...] = total[:, width:].astype(BF16)


def add_kernel(own_ref, got_ref, out_ref):
    out_ref[...] = (own_ref[...].astype(F32) + got_ref[...].astype(F32)).astype(BF16)


def whole_grad_kernel(head_ref, early_ref, grad_ref):
    columns = head_ref.shape[1]
    grad_ref[:, :columns] = head_ref[...]
    grad_ref[:, columns:] = early_ref[...]


def update_kernel(terms, shards, steps, place_ref, *refs):
    sums, refs = refs[:terms], refs[terms:]
    grad_ref, *matrix = refs[:5]
    vectors, refs = refs[5:9], refs[9:]
    new, (vector_grad_ref, norm_ref, *vectors_new) = refs[:4], refs[4:10]
    held_in, held_out, sem_in, sem_out = refs[10:14], refs[14:18], refs[18], refs[19]
    count = grad_ref.shape[0] // steps
    cuts = [pl.ds(i * count, count) for i in range(steps)]
    loads = [
        [pltpu.make_async_copy(a.at[cut], b.at[cut], sem_in.at[i, j]) for j, (a, b) in enumerate(zip(matrix, held_in))]
        for i, cut in enumerate(cuts)
    ]
    stores = [
        [
            pltpu.make_async_copy(a.at[cut], b.at[cut], sem_out.at[i, j])
            for j, (a, b) in enumerate(zip(held_out, new))
        ]
        for i, cut in enumerate(cuts)
    ]
    for step in loads:
        for copy in step:
            copy.start()
    total = sums[0][...]
    if terms > 1:
        total = total + sums[1][...]
    if terms > 2:
        total = total + (sums[2][...] + sums[3][...])
    rows = total[:VECTORS]
    norm = jnp.sqrt(total[VECTORS : VECTORS + 1, 0:1] + jnp.sum(rows * rows))
    norm_ref[...] = norm
    limit = 0.5 * math.sqrt(NPARAM)
    factor = limit / jnp.maximum(norm, limit)
    for i, cut in enumerate(cuts):
        for copy in loads[i]:
            copy.wait()
        states = [ref[cut, :] for ref in held_in]
        updated = adam_update(*states, grad_ref[cut, :], factor, MATRIX_RATE, MATRIX_DECAY)
        for ref, value in zip(held_out, updated):
            ref[cut, :] = value
        for copy in stores[i]:
            copy.start()
    width = vector_grad_ref.shape[1]
    vector_grad = 0.0
    for j in range(shards):
        part = rows[:, j * width : (j + 1) * width]
        vector_grad = vector_grad + jnp.where(place_ref[4] == j, part, 0.0)
    vector_grad_ref[...] = vector_grad
    updated = adam_update(*[ref[...] for ref in vectors], vector_grad, factor, VECTOR_RATE, 0.0)
    for ref, value in zip(vectors_new, updated):
        ref[...] = value
    for step in stores:
        for copy in step:
            copy.wait()


def adam_update(master, first_moment, second_moment, average, gradient, factor, rate, decay):
    clipped = gradient * factor
    first_new = BETA_FIRST * first_moment + (1.0 - BETA_FIRST) * clipped
    second_new = BETA_SECOND * second_moment + (1.0 - BETA_SECOND) * clipped * clipped
    first_hat = first_new / (1.0 - BETA_FIRST**STEP)
    second_hat = second_new / (1.0 - BETA_SECOND**STEP)
    master_new = master - rate * (first_hat / (jnp.sqrt(second_hat) + ADAM_EPS) + decay * master)
    average_new = AVERAGE_RATE * average + (1.0 - AVERAGE_RATE) * master_new
    return (master_new, first_new, second_new, average_new)


def local(
    tokens,
    cotangent,
    clip_ids,
    frame_ids,
    patch_ids,
    weights,
    weights_m,
    weights_v,
    weights_ema,
    vectors,
    vectors_m,
    vectors_v,
    vectors_ema,
):
    group_count = lax.axis_size("heads")
    core = lax.axis_index("heads") % 2
    place = places()
    count, features = tokens.shape
    width = features // group_count
    hidden = (weights.shape[1] - 9 * width) // 2
    rows = count // 2
    half = lax.axis_size("dp") // 2
    shard = weights.shape[0]

    wide = lambda n, dtype: shaped((rows, n), dtype)

    head_start = -(-(3 * width + 16) // 128) * 128
    head_piece, space_piece, up_piece, down_piece = local_call(
        "pack",
        pack_kernel,
        [shaped((shard, n), BF16) for n in (head_start + 2 * width, 4 * width, hidden, hidden)],
        weights, vectors,
    )
    head_z = z_blocks(head_piece)
    tokens_sorted, order, back, time_col, time_row, space_col, space_row, tokens_own, dy = local_call(
        "sort_rows",
        sort_kernel,
        [
            shaped((count, features), BF16),
            shaped((count, count), BF16),
            shaped((count, count), BF16),
            shaped((count, 8), F32),
            shaped((8, count), F32),
            shaped((count, 8), jnp.int32),
            shaped((8, count), jnp.int32),
            wide(features, BF16),
            wide(features, BF16),
        ],
        place, clip_ids, frame_ids, patch_ids, tokens, cotangent,
        smem=(0,),
        scratch=[pltpu.VMEM((count, features), BF16)],
    )
    head_y = [dp_swap(head_piece, 1)]
    before = tokens_sorted
    for k in range(1, half):
        head_z[k] = after(head_z[k], before)
        before = head_z[k]
        head_y.append(dp_swap(head_z[k], 1))
    space_z = z_blocks(after(space_piece, *head_z))
    (head_y,) = together(head_y)
    time_maps, mix_map, out_map = assemble(
        "gather_head", head_z, head_y, (head_start, head_start + width)
    )
    mix_x = x_swap(mix_map)

    vec, first, time_inputs, time_own, time_send, time_logs = local_call(
        "time_forward",
        time_forward_kernel,
        [
            shaped((16, features), F32),
            shaped((count, features), BF16),
            shaped((count, 3 * width), BF16),
            wide(width, BF16),
            wide(width, BF16),
            shaped((8, count), F32),
        ],
        time_maps, tokens_sorted, back, time_col, time_row,
        scratch=[pltpu.VMEM((count, width), BF16)],
    )
    space_z, (mix_x, time_send) = together(space_z, [mix_x, time_send])
    mix_core = core_swap(jnp.concatenate([mix_map, mix_x], 1))
    time_got = core_swap(time_send)

    mix_blocks, fused, mix_bias = local_call(
        "mix_maps",
        mix_kernel,
        [
            shaped((group_count, features, width), BF16),
            shaped((features, width), BF16),
            shaped((1, features), F32),
        ],
        place, out_map, mix_map, mix_x, mix_core, vec,
        smem=(0,),
    )
    fused_far = core_swap(fused)
    space_y = y_blocks(space_z)
    up_z = z_blocks(after(up_piece, *space_z))
    (time_part,) = local_call("time_out", time_out_kernel, [wide(features, BF16)], time_own, time_got, fused, fused_far)
    stream_one, second = local_call(
        "space_norm",
        partial(norm_in_kernel, 4),
        [wide(features, F32), wide(features, BF16)],
        tokens_own, time_part, x_swap(time_part), mix_bias, vec,
        flops=LONG,
    )

    space_own = assemble("gather_space", space_z, space_y)
    space_far = core_swap(space_own)
    space_q, space_pairs = local_call(
        "space_in",
        space_in_kernel,
        [wide(2 * width, BF16), wide(4 * width, BF16)],
        second, space_own, space_far,
    )
    up_z, (space_q, space_pairs) = together(up_z, [space_q, space_pairs])
    up_y = y_blocks(up_z)
    down_z = z_blocks(after(down_piece, *up_z))
    space_got = core_swap(space_pairs)
    space_heads, space_logs, class_logs, space_part = local_call(
        "space_forward",
        space_forward_kernel,
        [wide(2 * width, BF16), shaped((8, rows), F32), shaped((CLASSES, 8), F32), wide(features, BF16)],
        place, space_q, space_pairs, space_got, space_col, space_row, space_own, space_far,
        smem=(0,),
        scratch=[pltpu.VMEM((count, 4 * width), BF16), pltpu.VMEM((CLASSES, 4 * width), BF16)],
    )
    up_y, down_z, (space_part,) = together(up_y, down_z, [space_part])
    stream_two, third = local_call(
        "feed_norm",
        partial(norm_in_kernel, 7),
        [wide(features, F32), wide(features, BF16)],
        stream_one, space_part, x_swap(space_part), vec[6:8], vec,
        flops=LONG,
    )

    up_own = assemble("gather_up", up_z, up_y)
    up_far = core_swap(up_own)
    down_own = assemble("gather_down", down_z, y_blocks(down_z))
    down_far = core_swap(down_own)
    activ, grad_pre, third_part = local_call(
        "feed",
        feed_kernel,
        [wide(2 * hidden, BF16), wide(2 * hidden, BF16), wide(features, BF16)],
        third, dy, up_own, up_far, down_own, down_far,
    )
    third_got = x_swap(third_part)
    feed_grad_far, feed_grad_own = [
        local_call(
            name,
            partial(feed_grads_kernel, group),
            [shaped((features, 2 * hidden), BF16)],
            third, grad_pre, dy, activ,
        )[0]
        for name, group in (("feed_grads_far", 1), ("feed_grads_own", 0))
    ]
    (feed_part,) = local_call("feed_out", feed_out_kernel, [wide(features, BF16)], activ, down_own, down_far)
    (up_send, up_keep), (down_send, down_keep) = split_rows(
        "split_feed", [(feed_grad_own, core_swap(feed_grad_far))], (hidden,)
    )
    up_y = [dp_swap(up_send, 1)]
    third_got, feed_part = lax.optimization_barrier((third_got, feed_part))

    grad_two, grad_two_low, sums_two, space_grad_heads = local_call(
        "space_back_in",
        space_back_in_kernel,
        [wide(features, F32), wide(features, BF16), shaped((8, features), F32), wide(2 * width, BF16)],
        third_part, third_got, stream_two, vec, dy, space_own, space_far,
    )
    space_dq, space_keep, space_send = local_call(
        "space_backward",
        space_backward_kernel,
        [wide(2 * width, BF16), wide(4 * width, F32), wide(4 * width, BF16)],
        place, space_grad_heads, space_q, space_pairs, space_got, space_logs, class_logs, space_col, space_row,
        smem=(0,),
        scratch=[
            pltpu.VMEM((count, 4 * width), BF16),
            pltpu.VMEM((CLASSES, 4 * width), BF16),
            pltpu.VMEM((count, 4 * width), F32),
            pltpu.VMEM((CLASSES, 4 * width), F32),
            pltpu.VMEM((CLASSES, 2 * width), BF16),
        ],
    )
    up_y, (space_send,) = together(up_y, [space_send])
    up_shards = z_swaps(y_sums("sum_up", [(up_keep, up_y)]))
    space_got_grads = core_swap(space_send)
    down_y = [dp_swap(after(down_send, *up_y), 1)]
    grad_space, grad_space_far, second_part = local_call(
        "space_back",
        space_back_kernel,
        [wide(3 * width, BF16), wide(3 * width, BF16), wide(features, BF16)],
        space_dq, space_keep, space_got_grads, space_own, space_far,
    )
    second_got = x_swap(second_part)
    space_grad_far, space_grad_own = [
        local_call(
            name,
            partial(space_grads_kernel, group),
            [shaped((features, 4 * width), BF16)],
            second, grad, grad_two_low, space_heads,
        )[0]
        for name, group, grad in (("space_grads_far", 1, grad_space_far), ("space_grads_own", 0, grad_space))
    ]

    def whole(name, value, got):
        return pl.pallas_call(
            whole_rows_kernel,
            name=name,
            out_shape=shaped((count, features), F32),
            in_specs=[SMEM, VMEM, VMEM],
            out_specs=ANY,
            scratch_shapes=[pltpu.SemaphoreType.DMA((2,))],
            compiler_params=pltpu.CompilerParams(vmem_limit_bytes=2**21),
            cost_estimate=pl.CostEstimate(flops=0, bytes_accessed=0, transcendentals=0),
        )(place, value, got)

    ((space_y_send, space_keep),) = split_rows("split_space", [(space_grad_own, core_swap(space_grad_far))])
    space_y = [dp_swap(space_y_send, 1)]
    up_shards, (second_got, space_y_send) = together(up_shards, [second_got, space_y_send])
    grad_one, grad_one_low, sums_one, time_grad_own, time_grad_send = local_call(
        "time_back_in",
        time_back_in_kernel,
        [
            wide(features, F32),
            wide(features, BF16),
            shaped((8, features), F32),
            wide(width, BF16),
            wide(width, BF16),
        ],
        second_part, second_got, stream_one, vec, grad_two, fused, fused_far,
    )
    down_y, (time_grad_own, time_grad_send, grad_one_low) = together(
        down_y, [time_grad_own, time_grad_send, grad_one_low]
    )
    down_shards = z_swaps(y_sums("sum_down", [(down_keep, down_y)]))
    time_grad_got = core_swap(time_grad_send)
    fused_grad, fused_grad_far = local_call(
        "fused_grads",
        fused_grads_kernel,
        [shaped((features, width + SPARE), F32), shaped((features, width + SPARE), BF16)],
        grad_one_low, time_own, time_got,
    )
    fused_grad_got = core_swap(fused_grad_far)
    grad_time_out, fused_total, row_sum, bias_grad = local_call(
        "mix_grads",
        mix_grads_kernel,
        [
            shaped((features, width), BF16),
            shaped((features, width), BF16),
            shaped((features, SPARE), F32),
            shaped((8, features), F32),
        ],
        place, fused_grad, fused_grad_got, mix_blocks, sums_one,
        smem=(0,),
    )
    ((out_send, out_keep),) = split_rows("split_out", [(grad_time_out, None), (fused_total, None)])
    out_send, time_grad_own, time_grad_got = lax.optimization_barrier((out_send, time_grad_own, time_grad_got))
    out_y = [dp_swap(out_send, 1)]
    (grad_time,) = local_call(
        "time_backward",
        time_backward_kernel,
        [shaped((count, 3 * width), BF16)],
        time_grad_own, time_grad_got, order, time_inputs, time_logs, time_col, time_row,
        scratch=[pltpu.VMEM((count, width), BF16), pltpu.VMEM((count, 2 * width), F32)],
    )
    down_shards, space_y, out_y, (grad_time,) = together(down_shards, space_y, out_y, [grad_time])
    time_columns = 3 * width + SPARE
    time_send, time_keep = local_call(
        "time_grads",
        time_grads_kernel,
        [shaped((half, shard, time_columns), BF16), shaped((half, shard, time_columns), F32)],
        place, first, grad_time, row_sum,
        smem=(0,),
        scratch=[pltpu.VMEM((features, time_columns), F32)],
    )
    space_y, out_y, (time_send, grad_time) = together(space_y, out_y, [time_send, grad_time])
    time_y = [dp_swap(time_send, 1)]
    late_shards = z_swaps(y_sums("sum_late", [(out_keep, out_y), (space_keep, space_y)]))
    first_own, first_send, vector_sum = local_call(
        "time_back",
        time_back_kernel,
        [wide(features, BF16), wide(features, BF16), shaped((16, features), F32)],
        grad_time, time_maps, tokens_sorted, back, bias_grad, sums_one, sums_two,
        scratch=[pltpu.VMEM((count, features), BF16)],
    )
    feed_part_got = x_swap(after(feed_part, time_send))
    time_y, late_shards, (first_send, feed_part_got) = together(time_y, late_shards, [first_send, feed_part_got])
    first_got = core_swap(first_send)

    out_width = 2 * width
    out_grad, mix_keep, mix_send = local_call(
        "mix_shard",
        mix_shard_kernel,
        [shaped((shard, width), F32), shaped((shard, out_width), F32), shaped((shard, out_width), BF16)],
        place, out_map, *late_shards,
        smem=(0,),
    )
    (first_part,) = local_call("first_part", add_kernel, [wide(features, BF16)], first_own, first_got)
    mix_own, mix_send = local_call(
        "mix_sum",
        mix_sum_kernel,
        [shaped((shard, width), F32), shaped((shard, width), BF16)],
        mix_keep, core_swap(mix_send),
    )
    mix_got = x_swap(mix_send)
    first_part = after(first_part, mix_send)
    first_part_got = x_swap(first_part)
    (layer_half,) = local_call(
        "layer_out", layer_out_kernel, [wide(features, F32)], stream_two, feed_part, feed_part_got, vec
    )
    layer_got = core_swap(after(layer_half, first_got))
    time_shards = y_sums("sum_time", [(time_keep, time_y)])
    time_shards, (mix_got, layer_got) = together(time_shards, [mix_got, layer_got])
    time_shards = z_swaps(time_shards)
    layer_rows = whole("layer_rows", layer_half, layer_got)

    bias_part = lax.dynamic_slice_in_dim(vec[2:3], lax.axis_index("heads") * width, width, 1)
    late = [out_width, out_width + 4 * width]
    total = lambda shards: sum([one.astype(F32) for one in shards])
    up_shards, down_shards, _ = together(up_shards, down_shards, [first_part])
    early_grad = jnp.concatenate([total(late_shards)[:, out_width:], total(up_shards), total(down_shards)], 1)
    early_square = jnp.sum(early_grad * early_grad)
    time_shards, (early_grad, early_square, layer_rows) = together(time_shards, [early_grad, early_square, layer_rows])
    time_total = total(time_shards)
    mix_grad = mix_own + mix_got.astype(F32) + time_total[:, 3 * width : 3 * width + 1] * bias_part
    head_grad = jnp.concatenate([time_total[:, : 3 * width], out_grad, mix_grad], 1)
    square = early_square + jnp.sum(head_grad * head_grad)
    row = lax.broadcasted_iota(jnp.int32, vector_sum.shape, 0)
    sums = jnp.where(row == VECTORS, square, vector_sum)

    def input_half(ready):
        return local_call(
            "input_grad",
            input_grad_kernel,
            [wide(features, F32)],
            first_part, after(first_part_got, ready), tokens_own, vec, grad_one,
        )

    def last_results(ready, grad_half):
        grad_rows = whole("grad_rows", grad_half, core_swap(grad_half))
        (weight_grad,) = local_call(
            "whole_grad", whole_grad_kernel, [shaped(weights.shape, F32)], after(head_grad, ready), early_grad
        )
        return [grad_rows, weight_grad]

    terms, (grad_rows, weight_grad) = all_sum(sums, input_half, last_results)
    steps = max(one for one in (1, 2, 3, 4) if shard % (8 * one) == 0)
    states = [weights, weights_m, weights_v, weights_ema]
    vector_states = [vectors, vectors_m, vectors_v, vectors_ema]
    outs = pl.pallas_call(
        partial(update_kernel, len(terms), lax.axis_size("dp"), steps),
        name="update",
        out_shape=[shaped(weights.shape, F32)] * 4
        + [shaped(vectors.shape, F32), shaped((1, 1), F32)]
        + [shaped(vectors.shape, F32)] * 4,
        in_specs=[SMEM] + [VMEM] * (len(terms) + 1) + [ANY] * 4 + [VMEM] * 4,
        out_specs=[ANY] * 4 + [VMEM] * 6,
        scratch_shapes=[pltpu.VMEM(weights.shape, F32)] * 8
        + [pltpu.SemaphoreType.DMA((steps, 4)), pltpu.SemaphoreType.DMA((steps, 4))],
        compiler_params=pltpu.CompilerParams(vmem_limit_bytes=14 * 2**20),
    )(place, *terms, weight_grad, *states, *vector_states)
    weights_out, (vector_grad, grad_norm, *vectors_out) = outs[:4], outs[4:]
    return (
        layer_rows,
        grad_rows,
        weight_grad,
        vector_grad,
        grad_norm[0, 0],
        *weights_out,
        *vectors_out,
    )


def solution(mesh):
    rows, square, line = P("dp", None), P("dp", "heads"), P(None, "dp")
    placed = (rows,) * 5 + (square,) * 4 + (line,) * 4
    return jax.shard_map(
        local,
        mesh=mesh,
        in_specs=placed,
        out_specs=(rows, rows, square, line, P()) + (square,) * 4 + (line,) * 4,
        check_vma=False,
    )
```

```python
import math
from functools import partial

import jax
import jax.numpy as jnp
from jax import lax
from jax.experimental import pallas as pl
from jax.experimental.pallas import tpu as pltpu
from jax.sharding import PartitionSpec as P

HEAD_DIM = 64
STEP = 5
NPARAM = 10034688
VECTORS = 10

NORM_EPS = 1e-06
BETA_FIRST = 0.5
BETA_SECOND = 0.5
AVERAGE_RATE = 0.5
MATRIX_RATE = 0.03
VECTOR_RATE = 0.3
MATRIX_DECAY = 0.05
ADAM_EPS = 1e-08
MASKED = -1e30
SCALE = HEAD_DIM ** (-0.5)
F32 = jnp.float32
BF16 = jnp.bfloat16

BLOCK = 128
WINDOW = 256
CLASSES = 16
CHUNK = 256
UNROLL = 4
SPARE = 64
LONG = 40_000_000_000

VMEM = pl.BlockSpec(memory_space=pltpu.VMEM)
SMEM = pl.BlockSpec(memory_space=pltpu.SMEM)
ANY = pl.BlockSpec(memory_space=pl.ANY)


def core_swap(value):
    return lax.ppermute(value, "heads", [(i, i ^ 1) for i in range(4)])


def x_swap(value):
    return lax.ppermute(value, "heads", [(i, i ^ 2) for i in range(4)])


def dp_swap(value, mask):
    count = lax.axis_size("dp")
    return lax.ppermute(value, "dp", [(i, i ^ mask) for i in range(count)])


def all_sum(value, early, late):
    count = lax.axis_size("dp") * lax.axis_size("heads")
    value = value + core_swap(value)
    step, made = 2, None
    while step < count:
        masks = [step, 2 * step, 3 * step] if 2 * step < count else [step]
        got = [lax.ppermute(value, ("dp", "heads"), [(i, i ^ mask) for i in range(count)]) for mask in masks]
        step *= 4
        if made is None:
            made = early(value)
            got, made = together(got, made)
        if step >= count:
            break
        value = value + got[0]
        if len(got) > 1:
            value = value + (got[1] + got[2])
    made = late(value, *made)
    got, made = together(got, made)
    return [value, *got], made


def after(value, *others):
    return lax.optimization_barrier((value, *others))[0]


def together(*groups):
    flat = lax.optimization_barrier([one for group in groups for one in group])
    split, at = [], 0
    for group in groups:
        split.append(list(flat[at : at + len(group)]))
        at += len(group)
    return split


def shaped(shape, dtype):
    return jax.ShapeDtypeStruct(shape, dtype)


def local_call(name, kernel, outs, *operands, scratch=(), smem=(), extra=6, flops=0, staged=False):
    spec = VMEM
    if staged:
        spec, inner, count = ANY, kernel, len(operands)
        moved = [i for i in range(count) if i not in smem]

        def kernel(*refs):
            ins, rest, held, sem = list(refs[:count]), refs[count : -1 - len(moved)], refs[-1 - len(moved) : -1], refs[-1]
            copies = [pltpu.make_async_copy(ins[i], ref, sem.at[j]) for j, (i, ref) in enumerate(zip(moved, held))]
            for copy in copies:
                copy.start()
            for copy, i, ref in zip(copies, moved, held):
                copy.wait()
                ins[i] = ref
            inner(*ins, *rest)

        scratch = [*scratch, *[pltpu.VMEM(operands[i].shape, operands[i].dtype) for i in moved]]
    held = sum(math.prod(one.shape) * jnp.dtype(one.dtype).itemsize for one in scratch)
    return pl.pallas_call(
        kernel,
        name=name,
        out_shape=list(outs),
        in_specs=[SMEM if i in smem else spec for i in range(len(operands))],
        out_specs=[VMEM] * len(outs),
        scratch_shapes=[*scratch, *([pltpu.SemaphoreType.DMA((len(moved),))] if staged else [])],
        compiler_params=pltpu.CompilerParams(
            vmem_limit_bytes=held + extra * 2**20
        ),
        cost_estimate=pl.CostEstimate(flops=flops, bytes_accessed=0, transcendentals=0),
    )(*operands)


def dot(left, right):
    return jnp.dot(left, right, preferred_element_type=F32)


def dot_nt(left, right):
    return lax.dot_general(left, right, (((1,), (1,)), ((), ())), preferred_element_type=F32)


def dot_tn(left, right):
    return lax.dot_general(left, right, (((0,), (0,)), ((), ())), preferred_element_type=F32)


def chunk_loop(rows, body, size=CHUNK):
    def step(i, carry):
        body(pl.ds(pl.multiple_of(i * size, size), size))
        return carry

    lax.fori_loop(0, rows // size, step, 0)


def normed(stream):
    center = stream - jnp.mean(stream, -1, keepdims=True)
    factor = lax.rsqrt(jnp.mean(center * center, -1, keepdims=True) + NORM_EPS)
    return center * factor, factor


def norm_grad(hat, factor, gain, grad):
    scaled = grad * gain
    return factor * (
        scaled - jnp.mean(scaled, -1, keepdims=True) - hat * jnp.mean(scaled * hat, -1, keepdims=True)
    )


def column_sum(value):
    return jnp.sum(value, 0, keepdims=True)


def z_blocks(piece):
    return [piece] + [dp_swap(piece, 2 * k) for k in range(1, lax.axis_size("dp") // 2)]


def y_blocks(mine, fine=False):
    return [dp_swap(one, 1) for one in mine] if fine else [dp_swap(jnp.stack(mine), 1)]


def assemble(name, mine, other, cuts=()):
    half, count, fine = len(mine), lax.axis_size("dp"), len(other) > 1
    rows, columns = mine[0].shape
    bounds = [0, *cuts, columns]
    parts = [slice(start, stop) for start, stop in zip(bounds, bounds[1:])]

    def kernel(place_ref, *refs):
        z, y = place_ref[0], place_ref[1]
        for out_ref, part in zip(refs[half + len(other) :], parts):
            for k in range(half):
                out_ref[(z ^ k) * 2 + y] = refs[k][:, part]
                out_ref[(z ^ k) * 2 + (1 - y)] = refs[half + k][:, part] if fine else refs[half][k, :, part]

    outs = local_call(
        name,
        kernel,
        [shaped((count, rows, part.stop - part.start), mine[0].dtype) for part in parts],
        places(), *mine, *other,
        smem=(0,),
    )
    outs = [one.reshape(count * rows, -1) for one in outs]
    return outs if cuts else outs[0]


def places():
    dp, heads = lax.axis_index("dp"), lax.axis_index("heads")
    return jnp.stack([dp // 2, dp % 2, heads, heads % 2, dp]).astype(jnp.int32)


def split_rows(name, totals, cuts=()):
    count = lax.axis_size("dp")
    half = count // 2
    operands, columns = [], 0
    for own, received in totals:
        rows = own.shape[0] // count
        operands += [one.reshape(count, rows, own.shape[1]) for one in (own, received) if one is not None]
        columns += own.shape[1]
    bounds = [0, *cuts, columns]
    parts = list(zip(bounds, bounds[1:]))

    def kernel(place_ref, *refs):
        ins, outs = refs[: len(operands)], refs[len(operands) :]
        z, y = place_ref[0], place_ref[1]
        for k in range(half):
            for side in range(2):
                block = (z ^ k) * 2 + (1 - y if side == 0 else y)
                at, column = 0, 0
                for own, received in totals:
                    value = ins[at][block].astype(F32)
                    at += 1
                    if received is not None:
                        value = value + ins[at][block].astype(F32)
                        at += 1
                    for i, (start, stop) in enumerate(parts):
                        first, last = max(start, column), min(stop, column + own.shape[1])
                        if first < last:
                            ref = outs[2 * i + side]
                            ref[k, :, first - start : last - start] = value[:, first - column : last - column].astype(
                                ref.dtype
                            )
                    column += own.shape[1]

    outs = []
    for start, stop in parts:
        outs += [shaped((half, rows, stop - start), BF16), shaped((half, rows, stop - start), F32)]
    outs = local_call(name, kernel, outs, places(), *operands, smem=(0,))
    return list(zip(outs[::2], outs[1::2]))


def y_sums(name, pieces, flops=0):
    half, rows, _ = pieces[0][0].shape
    columns = [keep.shape[2] for keep, _ in pieces]
    fine = len(pieces[0][1]) > 1
    operands = [one for keep, arrived in pieces for one in (keep, *arrived)]
    step = 1 + len(pieces[0][1])

    def kernel(*refs):
        ins, outs = refs[: len(operands)], refs[len(operands) :]
        column = 0
        for i, width in enumerate(columns):
            part = slice(column, column + width)
            column += width
            for k in range(half):
                there = ins[i * step + 1 + k][...] if fine else ins[i * step + 1][k]
                value = ins[i * step][k] + there.astype(F32)
                outs[k][:, part] = value.astype(outs[k].dtype)

    outs = [shaped((rows, sum(columns)), F32)] + [shaped((rows, sum(columns)), BF16)] * (half - 1)
    return local_call(name, kernel, outs, *operands, flops=flops)


def z_swaps(summed):
    return [summed[0]] + [dp_swap(summed[k], 2 * k) for k in range(1, len(summed))]


def head_pairs(width):
    pair = 2 * HEAD_DIM
    return [(at, min(at + pair, width), min(2, (width - at) // HEAD_DIM)) for at in range(0, width, pair)]


def by_head(value, heads):
    if heads == 1:
        return value
    lane = lax.broadcasted_iota(jnp.int32, value.shape, 1)
    zero = jnp.zeros_like(value)
    return jnp.concatenate(
        [jnp.where(lane < HEAD_DIM, value, zero), jnp.where(lane < HEAD_DIM, zero, value)], 0
    )


def own_columns(value, heads):
    if heads == 1:
        return value
    count = value.shape[1] // 2
    return jnp.concatenate([value[:HEAD_DIM, :count], value[HEAD_DIM:, count:]], 0)


def own_rows(value, heads):
    if heads == 1:
        return value
    count = value.shape[0] // 2
    lane = lax.broadcasted_iota(jnp.int32, (count, value.shape[1]), 1)
    return jnp.where(lane < HEAD_DIM, value[:count], value[count:])


def masked_bias(allowed):
    return jnp.where(allowed, 0.0, MASKED).astype(F32)


def pair_forward(q, keys, values, bias, heads):
    scores = dot_nt(keys, by_head(q, heads)) + (bias if heads == 1 else jnp.concatenate([bias, bias], 1))
    top = jnp.max(scores, 0, keepdims=True)
    exps = jnp.exp(scores - top)
    total = jnp.sum(exps, 0, keepdims=True)
    out = dot_tn(values, exps.astype(BF16)) / total
    log = top + jnp.log(total)
    count = q.shape[0]
    return own_columns(out, heads), [log[:, h * count : (h + 1) * count] for h in range(heads)]


def pair_backward(q, grad, keys, values, bias, logs, heads):
    q, grad = by_head(q, heads), by_head(grad, heads)
    if heads > 1:
        bias, logs = jnp.concatenate([bias, bias], 1), [jnp.concatenate(logs, 1)]
    probs = jnp.exp(dot_nt(keys, q) + bias - logs[0])
    grad_probs = dot_nt(values, grad)
    delta = jnp.sum(probs * grad_probs, 0, keepdims=True)
    grad_scores = (probs * (grad_probs - delta)).astype(BF16)
    grad_q = own_columns(dot_tn(keys, grad_scores), heads) * SCALE
    return grad_q, dot(grad_scores, q), dot(probs.astype(BF16), grad)


def sort_kernel(
    place_ref, clip_ref, frame_ref, patch_ref, tokens_ref, dy_ref,
    sorted_ref, order_ref, back_ref, col_ref, row_ref, space_col_ref, space_row_ref, own_ref, own_dy_ref,
    all_ref,
):
    count = tokens_ref.shape[0]
    rows = count // 2
    core = place_ref[3]
    own = pl.ds(pl.multiple_of(core * rows, rows), rows)
    far = pl.ds(pl.multiple_of((1 - core) * rows, rows), rows)
    own_ref[...] = tokens_ref[own, :]
    own_dy_ref[...] = dy_ref[own, :]
    all_ref[:rows, :] = tokens_ref[own, :]
    all_ref[rows:, :] = tokens_ref[far, :]
    ids = [clip_ref, frame_ref, patch_ref]
    spare = jnp.zeros((5, count), jnp.int32)
    natural = jnp.concatenate([ref[...] for ref in ids] + [spare], 0)
    space_row_ref[...] = natural
    space_col_ref[...] = natural.astype(F32).T.astype(jnp.int32)
    ordered = jnp.concatenate(
        [jnp.concatenate([ref[:, own], ref[:, far]], 1) for ref in ids] + [spare], 0
    )
    ordered_col = ordered.astype(F32).T.astype(jnp.int32)
    key_row = (ordered[0:1] * 128 + ordered[2:3] + 1) * 64 + ordered[1:2] + 1
    key_col = (ordered_col[:, 0:1] * 128 + ordered_col[:, 2:3] + 1) * 64 + ordered_col[:, 1:2] + 1
    rank_row = jnp.zeros((1, count), jnp.int32)
    for i in range(0, count, CHUNK):
        smaller = key_col[i : i + CHUNK] < key_row
        rank_row = rank_row + jnp.sum(smaller.astype(jnp.int32), 0, keepdims=True)
    for i in range(0, count, CHUNK):
        at = slice(i, i + CHUNK)
        place = lax.broadcasted_iota(jnp.int32, (CHUNK, count), 0) + i
        order = (place == rank_row).astype(F32).astype(BF16)
        order_ref[at, :] = order
        rank_col = jnp.sum((key_row < key_col[at]).astype(jnp.int32), 1, keepdims=True)
        place = lax.broadcasted_iota(jnp.int32, (CHUNK, count), 1)
        back_ref[at, :] = (place == rank_col).astype(F32).astype(BF16)
        sorted_ref[at, :] = dot(order, all_ref[...]).astype(BF16)
        col_ref[at, :] = dot(order, ordered_col.astype(F32).astype(BF16))
        row_ref[:, at] = dot_nt(ordered.astype(F32).astype(BF16), order)


def pack_kernel(weights_ref, vectors_ref, head_ref, space_ref, up_ref, down_ref):
    width, hidden = space_ref.shape[1] // 4, up_ref.shape[1]
    rows = weights_ref.shape[0]
    start = head_ref.shape[1] - 2 * width
    unit = lax.broadcasted_iota(jnp.int32, (rows, rows), 0) == lax.broadcasted_iota(jnp.int32, (rows, rows), 1)
    vectors = jnp.concatenate([vectors_ref[...], jnp.zeros((16 - VECTORS, rows), F32)], 0).astype(BF16)
    head_ref[:, : 3 * width] = weights_ref[:, : 3 * width].astype(BF16)
    head_ref[:, 3 * width : start] = jnp.zeros((rows, start - 3 * width), BF16)
    head_ref[:, 3 * width : 3 * width + 16] = dot_nt(unit.astype(F32).astype(BF16), vectors).astype(BF16)
    head_ref[:, start : start + width] = weights_ref[:, 4 * width : 5 * width].astype(BF16)
    head_ref[:, start + width :] = weights_ref[:, 3 * width : 4 * width].astype(BF16)
    space_ref[...] = weights_ref[:, 5 * width : 9 * width].astype(BF16)
    up_ref[...] = weights_ref[:, 9 * width : 9 * width + hidden].astype(BF16)
    down_ref[...] = weights_ref[:, 9 * width + hidden :].astype(BF16)


def same_clip_patch(col_ref, row_ref, keys, queries):
    key = col_ref[keys, :]
    query = row_ref[:, queries]
    return (key[:, 0:1] * 128 + key[:, 2:3]) == (query[0:1] * 128 + query[2:3])


def temporal_window(i, count):
    first = i * BLOCK
    start = jnp.clip(first - (WINDOW - BLOCK) // 2, 0, count - WINDOW)
    return (
        pl.ds(pl.multiple_of(first, BLOCK), BLOCK),
        pl.ds(pl.multiple_of(start, (WINDOW - BLOCK) // 2), WINDOW),
    )


def time_forward_kernel(
    maps_ref, tokens_ref, back_ref, col_ref, row_ref,
    vec_ref, first_ref, inputs_ref, own_ref, far_ref, log_ref, heads_ref,
):
    count, width = tokens_ref.shape[0], own_ref.shape[1]
    columns = maps_ref.shape[1]
    lanes = maps_ref[:, columns - 128 :].astype(F32).T
    offset = 3 * width - (columns - 128)
    vec_ref[...] = lanes[offset : offset + 16]
    gain, shift = vec_ref[0:1], vec_ref[1:2]

    def project(at):
        hat, _ = normed(tokens_ref[at, :].astype(F32))
        first = (hat * gain + shift).astype(BF16)
        first_ref[at, :] = first
        inputs_ref[at, :] = dot(first, maps_ref[:, : 3 * width]).astype(BF16)

    chunk_loop(count, project)

    def step(i, carry):
        queries, keys = temporal_window(i, count)
        bias = masked_bias(same_clip_patch(col_ref, row_ref, keys, queries))
        outs, logs = [], []
        for start, stop, heads in head_pairs(width):
            out, log = pair_forward(
                inputs_ref[queries, start:stop] * BF16(SCALE),
                inputs_ref[keys, width + start : width + stop],
                inputs_ref[keys, 2 * width + start : 2 * width + stop],
                bias,
                heads,
            )
            outs.append(out)
            logs += log
        heads_ref[queries, :] = jnp.concatenate(outs, 0).T.astype(BF16)
        log_ref[:, queries] = jnp.concatenate(logs + [logs[0]] * (8 - len(logs)), 0)
        return carry

    lax.fori_loop(0, count // BLOCK, step, 0, unroll=8)
    rows = count // 2
    for i in range(0, rows, CHUNK):
        own_ref[i : i + CHUNK, :] = dot(back_ref[i : i + CHUNK, :], heads_ref[...]).astype(BF16)
        far_ref[i : i + CHUNK, :] = dot(back_ref[rows + i : rows + i + CHUNK, :], heads_ref[...]).astype(BF16)


def time_backward_kernel(
    own_ref, far_ref, order_ref, inputs_ref, log_ref, col_ref, row_ref,
    out_ref, grad_ref, sum_ref,
):
    count, width = inputs_ref.shape[0], own_ref.shape[1]
    rows = count // 2
    for i in range(0, count, CHUNK):
        grad_ref[i : i + CHUNK, :] = (
            dot(order_ref[i : i + CHUNK, :rows], own_ref[...]) + dot(order_ref[i : i + CHUNK, rows:], far_ref[...])
        ).astype(BF16)
    sum_ref[...] = jnp.zeros_like(sum_ref)

    def step(i, carry):
        queries, keys = temporal_window(i, count)
        bias = masked_bias(same_clip_patch(col_ref, row_ref, keys, queries))
        grad_qs, head = [], 0
        for start, stop, heads in head_pairs(width):
            grad_q, grad_k, grad_v = pair_backward(
                inputs_ref[queries, start:stop] * BF16(SCALE),
                grad_ref[queries, start:stop],
                inputs_ref[keys, width + start : width + stop],
                inputs_ref[keys, 2 * width + start : 2 * width + stop],
                bias,
                [log_ref[h : h + 1, queries] for h in range(head, head + heads)],
                heads,
            )
            head += heads
            grad_qs.append(grad_q)
            sum_ref[keys, start:stop] += grad_k
            sum_ref[keys, width + start : width + stop] += grad_v
        out_ref[queries, :width] = jnp.concatenate(grad_qs, 0).T.astype(BF16)
        return carry

    lax.fori_loop(0, count // BLOCK, step, 0, unroll=8)

    def store(at):
        out_ref[at, width:] = sum_ref[at, :].astype(BF16)

    chunk_loop(count, store)


def space_window(i, core, rows):
    first = core * rows + i * BLOCK
    start = jnp.clip(first - (WINDOW - BLOCK) // 2, 0, 2 * rows - WINDOW)
    return (
        pl.ds(pl.multiple_of(i * BLOCK, BLOCK), BLOCK),
        pl.ds(pl.multiple_of(first, BLOCK), BLOCK),
        pl.ds(pl.multiple_of(start, (WINDOW - BLOCK) // 2), WINDOW),
    )


def whole_pairs(core, pairs_ref, got_ref, whole_ref):
    rows, width = pairs_ref.shape[0], pairs_ref.shape[1] // 4
    whole_ref[pl.ds(pl.multiple_of(core * rows, rows), rows), :] = pairs_ref[...]
    there = pl.ds(pl.multiple_of((1 - core) * rows, rows), rows)
    for i, j in enumerate((1, 0, 3, 2)):
        whole_ref[there, i * width : (i + 1) * width] = got_ref[:, j * width : (j + 1) * width]


def class_rows(row):
    number = lax.broadcasted_iota(jnp.int32, (CLASSES, row.shape[1]), 0)
    return (row[0:1] == number) & (row[1:2] < 0)


def space_bias(col_ref, row_ref, queries, keys):
    key, query = col_ref[keys, :], row_ref[:, queries]
    frame = jnp.where(key[:, 1:2] < 0, -1, key[:, 0:1] * 128 + key[:, 1:2]) == query[0:1] * 128 + query[1:2]
    number = lax.broadcasted_iota(jnp.int32, (CLASSES, BLOCK), 0)
    return masked_bias(jnp.concatenate([frame & (query[1:2] >= 0), number == query[0:1]], 0))


def class_allowed(row_ref):
    number = lax.broadcasted_iota(jnp.int32, (CLASSES, row_ref.shape[1]), 0)
    return row_ref[0:1] == number


def space_forward_kernel(
    place_ref, q_ref, pairs_ref, got_ref, col_ref, row_ref, out_own_ref, out_far_ref,
    heads_ref, log_ref, class_log_ref, part_ref, whole_ref, class_ref,
):
    core = place_ref[3]
    rows, width = q_ref.shape
    whole_pairs(core, pairs_ref, got_ref, whole_ref)
    here = pl.ds(pl.multiple_of(core * rows, rows), rows)
    classes = class_rows(row_ref[...]).astype(F32).astype(BF16)
    own_classes = class_rows(row_ref[:, here]).astype(F32).astype(BF16)
    class_ref[...] = dot(classes, whole_ref[...]).astype(BF16)
    def both(keys, part):
        return jnp.concatenate([whole_ref[keys, part], class_ref[:, part]], 0)

    def step(i, carry):
        local, queries, keys = space_window(i, core, rows)
        bias = space_bias(col_ref, row_ref, queries, keys)
        outs, logs = [], []
        for start, stop, heads in head_pairs(width):
            out, log = pair_forward(
                q_ref[local, start:stop] * BF16(SCALE),
                both(keys, slice(start, stop)),
                both(keys, slice(width + start, width + stop)),
                bias,
                heads,
            )
            outs.append(out)
            logs += log
        heads_ref[local, :] = jnp.concatenate(outs, 0).T.astype(BF16)
        log_ref[:, local] = jnp.concatenate(logs + [logs[0]] * (8 - len(logs)), 0)
        return carry

    lax.fori_loop(0, rows // BLOCK, step, 0, unroll=UNROLL)

    bias = masked_bias(class_allowed(row_ref))
    class_q = dot(own_classes, q_ref[...]).astype(BF16) * BF16(SCALE)
    outs, logs = [], []
    for start, stop, heads in head_pairs(width):
        scores = dot_nt(by_head(class_q[:, start:stop], heads), whole_ref[:, start:stop])
        scores = scores + (bias if heads == 1 else jnp.concatenate([bias, bias], 0))
        top = jnp.max(scores, 1, keepdims=True)
        exps = jnp.exp(scores - top)
        total = jnp.sum(exps, 1, keepdims=True)
        outs.append(own_rows(dot(exps.astype(BF16), whole_ref[:, width + start : width + stop]) / total, heads))
        log = top + jnp.log(total)
        logs += [log[h * CLASSES : (h + 1) * CLASSES] for h in range(heads)]
    class_log_ref[...] = jnp.concatenate(logs + [logs[0]] * (8 - len(logs)), 1)
    class_out = jnp.concatenate(outs, 1).astype(BF16)
    is_class = col_ref[here, 1:2] < 0

    def replace(at):
        back = dot_tn(own_classes, class_out).astype(BF16)
        heads_ref[...] = jnp.where(is_class, back, heads_ref[...])

    replace(None)
    group = width // 2

    def project(at):
        part_ref[at, :] = (
            dot_nt(heads_ref[at, :group], out_own_ref[:, 3 * group :])
            + dot_nt(heads_ref[at, group:], out_far_ref[:, 3 * group :])
        ).astype(BF16)

    chunk_loop(rows, project)


def space_back_in_kernel(
    part_ref, got_ref, stream_ref, vec_ref, dy_ref, out_own_ref, out_far_ref,
    grad_ref, low_ref, sums_ref, heads_ref,
):
    group = heads_ref.shape[1] // 2
    gain = vec_ref[7:8]
    sums_ref[...] = jnp.zeros_like(sums_ref)

    def through_norm(at):
        grad = part_ref[at, :].astype(F32) + got_ref[at, :].astype(F32)
        hat, factor = normed(stream_ref[at, :])
        dy = dy_ref[at, :].astype(F32)
        dx = dy + norm_grad(hat, factor, gain, grad)
        grad_ref[at, :] = dx
        low = dx.astype(BF16)
        low_ref[at, :] = low
        heads_ref[at, :group] = dot(low, out_own_ref[:, 3 * group :]).astype(BF16)
        heads_ref[at, group:] = dot(low, out_far_ref[:, 3 * group :]).astype(BF16)
        sums_ref[0:4] += jnp.concatenate(
            [column_sum(dx), column_sum(grad * hat), column_sum(grad), column_sum(dy)], 0
        )

    chunk_loop(grad_ref.shape[0], through_norm)


def space_backward_kernel(
    place_ref, heads_ref, q_ref, pairs_ref, got_ref, log_ref, class_log_ref, col_ref, row_ref,
    dq_ref, keep_ref, send_ref,
    whole_ref, class_ref, total_ref, class_total_ref, class_dq_ref,
):
    core = place_ref[3]
    rows, width = q_ref.shape
    whole_pairs(core, pairs_ref, got_ref, whole_ref)
    here = pl.ds(pl.multiple_of(core * rows, rows), rows)
    there = pl.ds(pl.multiple_of((1 - core) * rows, rows), rows)
    classes = class_rows(row_ref[...]).astype(F32)
    own_classes = class_rows(row_ref[:, here]).astype(F32).astype(BF16)
    class_ref[...] = dot(classes.astype(BF16), whole_ref[...]).astype(BF16)
    class_total_ref[...] = jnp.zeros_like(class_total_ref)
    bias = masked_bias(class_allowed(row_ref))
    class_q = dot(own_classes, q_ref[...]).astype(BF16) * BF16(SCALE)
    class_g = dot(own_classes, heads_ref[...]).astype(BF16)
    head = 0
    for start, stop, heads in head_pairs(width):
        keys, values = whole_ref[:, start:stop], whole_ref[:, width + start : width + stop]
        q, grad = by_head(class_q[:, start:stop], heads), by_head(class_g[:, start:stop], heads)
        logs = [class_log_ref[:, h : h + 1] for h in range(head, head + heads)]
        head += heads
        scores = dot_nt(q, keys) + (bias if heads == 1 else jnp.concatenate([bias, bias], 0))
        probs = jnp.exp(scores - jnp.concatenate(logs, 0))
        grad_probs = dot_nt(grad, values)
        grad_scores = (probs * (grad_probs - jnp.sum(probs * grad_probs, 1, keepdims=True))).astype(BF16)
        class_dq_ref[:, start:stop] = own_rows(dot(grad_scores, keys) * SCALE, heads).astype(BF16)
        total_ref[:, start:stop] = dot_tn(grad_scores, q)
        total_ref[:, width + start : width + stop] = dot_tn(probs.astype(BF16), grad)

    def both(keys, part):
        return jnp.concatenate([whole_ref[keys, part], class_ref[:, part]], 0)

    def step(i, carry):
        local, queries, keys = space_window(i, core, rows)
        bias = space_bias(col_ref, row_ref, queries, keys)
        is_class = row_ref[1:2, queries] < 0
        grad_qs, head = [], 0
        for start, stop, heads in head_pairs(width):
            key_part, value_part = slice(start, stop), slice(width + start, width + stop)
            grad_q, grad_k, grad_v = pair_backward(
                q_ref[local, start:stop] * BF16(SCALE),
                heads_ref[local, start:stop],
                both(keys, key_part),
                both(keys, value_part),
                bias,
                [jnp.where(is_class, -MASKED, log_ref[h : h + 1, local]) for h in range(head, head + heads)],
                heads,
            )
            head += heads
            grad_qs.append(grad_q)
            total_ref[keys, key_part] += grad_k[:WINDOW]
            total_ref[keys, value_part] += grad_v[:WINDOW]
            class_total_ref[:, key_part] += grad_k[WINDOW:]
            class_total_ref[:, value_part] += grad_v[WINDOW:]
        dq_ref[local, :] = jnp.concatenate(grad_qs, 0).T.astype(BF16)
        return carry

    lax.fori_loop(0, rows // BLOCK, step, 0, unroll=UNROLL)
    dq_ref[...] = jnp.where(
        col_ref[here, 1:2] < 0, dot_tn(own_classes, class_dq_ref[...]).astype(BF16), dq_ref[...]
    )
    high = class_total_ref[...].astype(BF16)
    rest = (class_total_ref[...] - high.astype(F32)).astype(BF16)
    classes = classes.astype(BF16)
    total_ref[...] += dot_tn(jnp.concatenate([classes, classes], 0), jnp.concatenate([high, rest], 0))
    keep_ref[...] = total_ref[here, :]
    send_ref[...] = total_ref[there, :].astype(BF16)


def mix_kernel(place_ref, out_ref, own_ref, x_ref, core_ref, vec_ref, mix_ref, fused_ref, bias_ref):
    place = place_ref[2]
    width = out_ref.shape[1]
    mix_ref[0] = own_ref[...]
    mix_ref[1] = core_ref[:, :width]
    mix_ref[2] = x_ref[...]
    mix_ref[3] = core_ref[:, width:]
    total, bias = 0.0, 0.0
    low = vec_ref[...].astype(BF16)
    for j in range(4):
        block = mix_ref[place ^ j]
        total = total + dot(block, out_ref[j * width : (j + 1) * width, :])
        bias = bias + dot_nt(low[:, j * width : (j + 1) * width], block)
    fused_ref[...] = total.astype(BF16)
    bias_ref[...] = bias[2:3] + vec_ref[3:4]


def time_out_kernel(own_ref, got_ref, fused_ref, far_ref, part_ref):
    def project(at):
        part_ref[at, :] = (dot_nt(own_ref[at, :], fused_ref[...]) + dot_nt(got_ref[at, :], far_ref[...])).astype(BF16)

    chunk_loop(part_ref.shape[0], project)


def norm_in_kernel(gain_row, before_ref, part_ref, got_ref, shift_ref, vec_ref, stream_ref, normed_ref):
    gain, shift = vec_ref[gain_row : gain_row + 1], vec_ref[gain_row + 1 : gain_row + 2]

    def body(at):
        stream = (
            before_ref[at, :].astype(F32)
            + (part_ref[at, :].astype(F32) + got_ref[at, :].astype(F32))
            + shift_ref[0:1]
        )
        stream_ref[at, :] = stream
        hat, _ = normed(stream)
        normed_ref[at, :] = (hat * gain + shift).astype(BF16)

    chunk_loop(stream_ref.shape[0], body)


def space_in_kernel(second_ref, own_ref, far_ref, q_ref, pairs_ref):
    width = q_ref.shape[1] // 2

    def project(at):
        for g, maps_ref in enumerate((own_ref, far_ref)):
            inputs = dot(second_ref[at, :], maps_ref[:, : 3 * width]).astype(BF16)
            q_ref[at, g * width : (g + 1) * width] = inputs[:, :width]
            pairs_ref[at, g * width : (g + 1) * width] = inputs[:, width : 2 * width]
            pairs_ref[at, (2 + g) * width : (3 + g) * width] = inputs[:, 2 * width :]

    chunk_loop(q_ref.shape[0], project)


def gelu_parts(pre):
    cdf = 0.5 * (1.0 + lax.erf(pre * (0.5**0.5)))
    slope = cdf + pre * jnp.exp(-0.5 * pre * pre) * (1.0 / math.sqrt(2.0 * math.pi))
    return pre * cdf, slope


def feed_kernel(
    third_ref, dy_ref, up_ref, up_far_ref, down_ref, down_far_ref, activ_ref, grad_ref, back_ref
):
    hidden = activ_ref.shape[1] // 2

    def project(at):
        back = 0.0
        for g, (ups_ref, downs_ref) in enumerate(((up_ref, down_ref), (up_far_ref, down_far_ref))):
            act, slope = gelu_parts(dot(third_ref[at, :], ups_ref[...]))
            part = slice(g * hidden, (g + 1) * hidden)
            activ_ref[at, part] = act.astype(BF16)
            grad = (dot(dy_ref[at, :], downs_ref[...]) * slope).astype(BF16)
            grad_ref[at, part] = grad
            back = back + dot_nt(grad, ups_ref[...])
        back_ref[at, :] = back.astype(BF16)

    chunk_loop(third_ref.shape[0], project)


def feed_out_kernel(activ_ref, own_ref, far_ref, part_ref):
    hidden = activ_ref.shape[1] // 2

    def project(at):
        part_ref[at, :] = (
            dot_nt(activ_ref[at, :hidden], own_ref[...]) + dot_nt(activ_ref[at, hidden:], far_ref[...])
        ).astype(BF16)

    chunk_loop(part_ref.shape[0], project)


def feed_grads_kernel(group, third_ref, grad_ref, dy_ref, activ_ref, out_ref):
    hidden = out_ref.shape[1] // 2
    part = slice(group * hidden, (group + 1) * hidden)
    out_ref[:, :hidden] = dot_tn(third_ref[...], grad_ref[:, part]).astype(BF16)
    out_ref[:, hidden:] = dot_tn(dy_ref[...], activ_ref[:, part]).astype(BF16)


def space_back_kernel(
    dq_ref, keep_ref, got_ref, own_ref, far_ref, grad_own_ref, grad_far_ref, part_ref
):
    width = dq_ref.shape[1] // 2

    def project(at):
        total = 0.0
        for g, (maps_ref, grad_ref) in enumerate(((own_ref, grad_own_ref), (far_ref, grad_far_ref))):
            grad_ref[at, :width] = dq_ref[at, g * width : (g + 1) * width]
            for i in (1, 2):
                mine = slice((2 * i - 2 + g) * width, (2 * i - 1 + g) * width)
                theirs = slice((2 * i - 1 - g) * width, (2 * i - g) * width)
                grad_ref[at, i * width : (i + 1) * width] = (
                    keep_ref[at, mine] + got_ref[at, theirs].astype(F32)
                ).astype(BF16)
            total = total + dot_nt(grad_ref[at, :], maps_ref[:, : 3 * width])
        part_ref[at, :] = total.astype(BF16)

    chunk_loop(part_ref.shape[0], project)


def space_grads_kernel(group, second_ref, grad_ref, low_ref, heads_ref, out_ref):
    width = heads_ref.shape[1] // 2
    out_ref[:, : 3 * width] = dot_tn(second_ref[...], grad_ref[...]).astype(BF16)
    out_ref[:, 3 * width :] = dot_tn(low_ref[...], heads_ref[:, group * width : (group + 1) * width]).astype(BF16)


def time_back_in_kernel(
    part_ref, got_ref, stream_ref, vec_ref, before_ref, fused_ref, far_ref,
    grad_ref, low_ref, sums_ref, own_ref, send_ref,
):
    gain = vec_ref[4:5]
    sums_ref[...] = jnp.zeros_like(sums_ref)

    def through_norm(at):
        grad = part_ref[at, :].astype(F32) + got_ref[at, :].astype(F32)
        hat, factor = normed(stream_ref[at, :])
        dx = before_ref[at, :] + norm_grad(hat, factor, gain, grad)
        grad_ref[at, :] = dx
        low = dx.astype(BF16)
        low_ref[at, :] = low
        own_ref[at, :] = dot(low, fused_ref[...]).astype(BF16)
        send_ref[at, :] = dot(low, far_ref[...]).astype(BF16)
        sums_ref[0:4] += jnp.concatenate(
            [column_sum(low.astype(F32)), column_sum(dx), column_sum(grad * hat), column_sum(grad)], 0
        )

    chunk_loop(grad_ref.shape[0], through_norm)


def time_grads_kernel(place_ref, first_ref, grad_ref, row_sum_ref, send_ref, keep_ref, total_ref):
    half, rows, columns = keep_ref.shape
    width = columns - row_sum_ref.shape[1]
    z, y = place_ref[0], place_ref[1]
    total_ref[:, :width] = dot_tn(first_ref[...], grad_ref[...])
    total_ref[:, width:] = row_sum_ref[...]
    for k in range(half):
        mine = pl.ds(pl.multiple_of(((z ^ k) * 2 + y) * rows, 8), rows)
        theirs = pl.ds(pl.multiple_of(((z ^ k) * 2 + (1 - y)) * rows, 8), rows)
        send_ref[k] = total_ref[theirs, :].astype(BF16)
        keep_ref[k] = total_ref[mine, :]


def time_back_kernel(
    grad_ref, maps_ref, tokens_ref, back_ref, bias_ref, one_ref, two_ref, own_ref, sums_ref, *refs
):
    count, width = tokens_ref.shape[0], grad_ref.shape[1] // 3
    far_refs, sorted_ref = refs[:-1], refs[-1]
    sums_ref[...] = jnp.zeros_like(sums_ref)
    sums_ref[2:3] = 0.5 * bias_ref[0:1]
    sums_ref[3:6] = 0.5 * one_ref[1:4]
    sums_ref[6:10] = 0.5 * two_ref[0:4]

    def project(at):
        grad = dot_nt(grad_ref[at, :], maps_ref[:, : 3 * width])
        hat, _ = normed(tokens_ref[at, :].astype(F32))
        sums_ref[0:2] += jnp.concatenate([column_sum(grad * hat), column_sum(grad)], 0)
        sorted_ref[at, :] = grad.astype(BF16)

    chunk_loop(count, project)
    rows = count // 2
    cut = rows // len(far_refs)
    for i, far_ref in enumerate(far_refs):
        at = slice(rows + i * cut, rows + (i + 1) * cut)
        far_ref[...] = dot(back_ref[at, :], sorted_ref[...]).astype(BF16)
    for i in range(0, rows, CHUNK):
        own_ref[i : i + CHUNK, :] = dot(back_ref[i : i + CHUNK, :], sorted_ref[...]).astype(BF16)


def input_grad_kernel(part_ref, got_ref, tokens_ref, vec_ref, before_ref, out_ref):
    gain = vec_ref[0:1]

    def through_norm(at):
        grad = part_ref[at, :].astype(F32) + got_ref[at, :].astype(F32)
        hat, factor = normed(tokens_ref[at, :].astype(F32))
        out_ref[at, :] = before_ref[at, :] + norm_grad(hat, factor, gain, grad)

    chunk_loop(out_ref.shape[0], through_norm)


def layer_out_kernel(stream_ref, part_ref, got_ref, vec_ref, out_ref):
    out_ref[...] = stream_ref[...] + (part_ref[...].astype(F32) + got_ref[...].astype(F32)) + vec_ref[9:10]


def whole_rows_kernel(place_ref, own_ref, got_ref, out_ref, sem):
    core = place_ref[3]
    rows = own_ref.shape[0]
    copies = [
        pltpu.make_async_copy(ref, out_ref.at[pl.ds(pl.multiple_of(at * rows, rows), rows)], sem.at[i])
        for i, (ref, at) in enumerate(((own_ref, core), (got_ref, 1 - core)))
    ]
    for copy in copies:
        copy.start()
    for copy in copies:
        copy.wait()


def fused_grads_kernel(low_ref, heads_ref, got_heads_ref, own_ref, far_ref):
    ones = jnp.ones((low_ref.shape[0], own_ref.shape[1] - heads_ref.shape[1]), BF16)
    far_ref[...] = dot_tn(low_ref[...], jnp.concatenate([got_heads_ref[...], ones], 1)).astype(BF16)
    own_ref[...] = dot_tn(low_ref[...], jnp.concatenate([heads_ref[...], ones], 1))


def mix_grads_kernel(
    place_ref, fused_ref, got_ref, mix_ref, sums_ref, grad_out_ref, total_ref, row_sum_ref, bias_ref
):
    place = place_ref[2]
    width = total_ref.shape[1]
    both = fused_ref[...] + got_ref[...].astype(F32)
    row_sum_ref[...] = both[:, width:]
    fused = both[:, :width].astype(BF16)
    total_ref[...] = fused
    for j in range(4):
        block = mix_ref[place ^ j]
        grad_out_ref[j * width : (j + 1) * width, :] = dot_tn(block, fused).astype(BF16)
        bias_ref[:, j * width : (j + 1) * width] = dot(sums_ref[...].astype(BF16), block)


def mix_shard_kernel(place_ref, out_ref, *refs):
    ins, (grad_ref, keep_ref, send_ref) = refs[:-3], refs[-3:]
    place = place_ref[2]
    width = out_ref.shape[1]
    total = sum(ref[:, : 2 * width].astype(F32) for ref in ins)
    grad_ref[...] = total[:, :width]
    fused = total[:, width:].astype(BF16)
    for m in range(4):
        rows = out_ref[pl.ds(pl.multiple_of((place ^ m) * width, width), width), :]
        part = dot_nt(fused, rows)
        ref = send_ref if m % 2 else keep_ref
        ref[:, m // 2 * width : (m // 2 + 1) * width] = part.astype(ref.dtype)


def mix_sum_kernel(keep_ref, got_ref, own_ref, send_ref):
    width = own_ref.shape[1]
    total = keep_ref[...] + got_ref[...].astype(F32)
    own_ref[...] = total[:, :width]
    send_ref[...] = total[:, width:].astype(BF16)


def add_kernel(own_ref, *refs):
    got_refs, out_ref = refs[:-1], refs[-1]
    rows = got_refs[0].shape[0]
    for i, ref in enumerate(got_refs):
        at = slice(i * rows, (i + 1) * rows)
        out_ref[at, :] = (own_ref[at, :].astype(F32) + ref[...].astype(F32)).astype(BF16)


def whole_grad_kernel(head_ref, early_ref, grad_ref):
    columns = head_ref.shape[1]
    grad_ref[:, :columns] = head_ref[...]
    grad_ref[:, columns:] = early_ref[...]


def update_kernel(terms, shards, steps, place_ref, *refs):
    sums, refs = refs[:terms], refs[terms:]
    grad_ref, *matrix = refs[:5]
    vectors, refs = refs[5:9], refs[9:]
    new, (vector_grad_ref, norm_ref, *vectors_new) = refs[:4], refs[4:10]
    held_in, held_out, sem_in, sem_out = refs[10:14], refs[14:18], refs[18], refs[19]
    count = grad_ref.shape[0] // steps
    cuts = [pl.ds(i * count, count) for i in range(steps)]
    loads = [
        [pltpu.make_async_copy(a.at[cut], b.at[cut], sem_in.at[i, j]) for j, (a, b) in enumerate(zip(matrix, held_in))]
        for i, cut in enumerate(cuts)
    ]
    stores = [
        [
            pltpu.make_async_copy(a.at[cut], b.at[cut], sem_out.at[i, j])
            for j, (a, b) in enumerate(zip(held_out, new))
        ]
        for i, cut in enumerate(cuts)
    ]
    for step in loads:
        for copy in step:
            copy.start()
    total = sums[0][...]
    if terms > 1:
        total = total + sums[1][...]
    if terms > 2:
        total = total + (sums[2][...] + sums[3][...])
    rows = total[:VECTORS]
    norm = jnp.sqrt(total[VECTORS : VECTORS + 1, 0:1] + jnp.sum(rows * rows))
    norm_ref[...] = norm
    limit = 0.5 * math.sqrt(NPARAM)
    factor = limit / jnp.maximum(norm, limit)
    for i, cut in enumerate(cuts):
        for copy in loads[i]:
            copy.wait()
        states = [ref[cut, :] for ref in held_in]
        updated = adam_update(*states, grad_ref[cut, :], factor, MATRIX_RATE, MATRIX_DECAY)
        for ref, value in zip(held_out, updated):
            ref[cut, :] = value
        for copy in stores[i]:
            copy.start()
    width = vector_grad_ref.shape[1]
    vector_grad = 0.0
    for j in range(shards):
        part = rows[:, j * width : (j + 1) * width]
        vector_grad = vector_grad + jnp.where(place_ref[4] == j, part, 0.0)
    vector_grad_ref[...] = vector_grad
    updated = adam_update(*[ref[...] for ref in vectors], vector_grad, factor, VECTOR_RATE, 0.0)
    for ref, value in zip(vectors_new, updated):
        ref[...] = value
    for step in stores:
        for copy in step:
            copy.wait()


def adam_update(master, first_moment, second_moment, average, gradient, factor, rate, decay):
    clipped = gradient * factor
    first_new = BETA_FIRST * first_moment + (1.0 - BETA_FIRST) * clipped
    second_new = BETA_SECOND * second_moment + (1.0 - BETA_SECOND) * clipped * clipped
    first_hat = first_new / (1.0 - BETA_FIRST**STEP)
    second_hat = second_new / (1.0 - BETA_SECOND**STEP)
    master_new = master - rate * (first_hat / (jnp.sqrt(second_hat) + ADAM_EPS) + decay * master)
    average_new = AVERAGE_RATE * average + (1.0 - AVERAGE_RATE) * master_new
    return (master_new, first_new, second_new, average_new)


def local(
    tokens,
    cotangent,
    clip_ids,
    frame_ids,
    patch_ids,
    weights,
    weights_m,
    weights_v,
    weights_ema,
    vectors,
    vectors_m,
    vectors_v,
    vectors_ema,
):
    group_count = lax.axis_size("heads")
    core = lax.axis_index("heads") % 2
    place = places()
    count, features = tokens.shape
    width = features // group_count
    hidden = (weights.shape[1] - 9 * width) // 2
    rows = count // 2
    half = lax.axis_size("dp") // 2
    shard = weights.shape[0]

    wide = lambda n, dtype: shaped((rows, n), dtype)

    head_start = -(-(3 * width + 16) // 128) * 128
    head_piece, space_piece, up_piece, down_piece = local_call(
        "pack",
        pack_kernel,
        [shaped((shard, n), BF16) for n in (head_start + 2 * width, 4 * width, hidden, hidden)],
        weights, vectors,
    )
    head_z = z_blocks(head_piece)
    tokens_sorted, order, back, time_col, time_row, space_col, space_row, tokens_own, dy = local_call(
        "sort_rows",
        sort_kernel,
        [
            shaped((count, features), BF16),
            shaped((count, count), BF16),
            shaped((count, count), BF16),
            shaped((count, 8), F32),
            shaped((8, count), F32),
            shaped((count, 8), jnp.int32),
            shaped((8, count), jnp.int32),
            wide(features, BF16),
            wide(features, BF16),
        ],
        place, clip_ids, frame_ids, patch_ids, tokens, cotangent,
        smem=(0,),
        scratch=[pltpu.VMEM((count, features), BF16)],
    )
    head_y = [dp_swap(head_piece, 1)]
    before = tokens_sorted
    for k in range(1, half):
        head_z[k] = after(head_z[k], before)
        before = head_z[k]
        head_y.append(dp_swap(head_z[k], 1))
    space_z = z_blocks(after(space_piece, *head_z))
    (head_y,) = together(head_y)
    time_maps, mix_map, out_map = assemble(
        "gather_head", head_z, head_y, (head_start, head_start + width)
    )
    mix_x = x_swap(mix_map)

    vec, first, time_inputs, time_own, time_send, time_logs = local_call(
        "time_forward",
        time_forward_kernel,
        [
            shaped((16, features), F32),
            shaped((count, features), BF16),
            shaped((count, 3 * width), BF16),
            wide(width, BF16),
            wide(width, BF16),
            shaped((8, count), F32),
        ],
        time_maps, tokens_sorted, back, time_col, time_row,
        scratch=[pltpu.VMEM((count, width), BF16)],
    )
    space_z, (mix_x, time_send) = together(space_z, [mix_x, time_send])
    mix_core = core_swap(jnp.concatenate([mix_map, mix_x], 1))
    time_got = core_swap(time_send)

    mix_blocks, fused, mix_bias = local_call(
        "mix_maps",
        mix_kernel,
        [
            shaped((group_count, features, width), BF16),
            shaped((features, width), BF16),
            shaped((1, features), F32),
        ],
        place, out_map, mix_map, mix_x, mix_core, vec,
        smem=(0,),
    )
    fused_far = core_swap(fused)
    space_y = y_blocks(space_z)
    up_z = z_blocks(after(up_piece, *space_z))
    (time_part,) = local_call("time_out", time_out_kernel, [wide(features, BF16)], time_own, time_got, fused, fused_far)
    stream_one, second = local_call(
        "space_norm",
        partial(norm_in_kernel, 4),
        [wide(features, F32), wide(features, BF16)],
        tokens_own, time_part, x_swap(time_part), mix_bias, vec,
        flops=LONG,
    )

    space_own = assemble("gather_space", space_z, space_y)
    space_far = core_swap(space_own)
    space_q, space_pairs = local_call(
        "space_in",
        space_in_kernel,
        [wide(2 * width, BF16), wide(4 * width, BF16)],
        second, space_own, space_far,
    )
    up_z, (space_q, space_pairs) = together(up_z, [space_q, space_pairs])
    up_y = y_blocks(up_z)
    down_z = z_blocks(after(down_piece, *up_z))
    space_got = core_swap(space_pairs)
    space_heads, space_logs, class_logs, space_part = local_call(
        "space_forward",
        space_forward_kernel,
        [wide(2 * width, BF16), shaped((8, rows), F32), shaped((CLASSES, 8), F32), wide(features, BF16)],
        place, space_q, space_pairs, space_got, space_col, space_row, space_own, space_far,
        smem=(0,),
        scratch=[pltpu.VMEM((count, 4 * width), BF16), pltpu.VMEM((CLASSES, 4 * width), BF16)],
    )
    up_y, down_z, (space_part,) = together(up_y, down_z, [space_part])
    stream_two, third = local_call(
        "feed_norm",
        partial(norm_in_kernel, 7),
        [wide(features, F32), wide(features, BF16)],
        stream_one, space_part, x_swap(space_part), vec[6:8], vec,
        flops=LONG,
    )

    up_own = assemble("gather_up", up_z, up_y)
    up_far = core_swap(up_own)
    down_own = assemble("gather_down", down_z, y_blocks(down_z))
    down_far = core_swap(down_own)
    activ, grad_pre, third_part = local_call(
        "feed",
        feed_kernel,
        [wide(2 * hidden, BF16), wide(2 * hidden, BF16), wide(features, BF16)],
        third, dy, up_own, up_far, down_own, down_far,
    )
    third_got = x_swap(third_part)
    feed_grad_far, feed_grad_own = [
        local_call(
            name,
            partial(feed_grads_kernel, group),
            [shaped((features, 2 * hidden), BF16)],
            third, grad_pre, dy, activ,
        )[0]
        for name, group in (("feed_grads_far", 1), ("feed_grads_own", 0))
    ]
    (feed_part,) = local_call("feed_out", feed_out_kernel, [wide(features, BF16)], activ, down_own, down_far)
    (up_send, up_keep), (down_send, down_keep) = split_rows(
        "split_feed", [(feed_grad_own, core_swap(feed_grad_far))], (hidden,)
    )
    up_y, down_y = [dp_swap(up_send, 1)], [dp_swap(down_send, 1)]
    third_got, feed_part = lax.optimization_barrier((third_got, feed_part))

    grad_two, grad_two_low, sums_two, space_grad_heads = local_call(
        "space_back_in",
        space_back_in_kernel,
        [wide(features, F32), wide(features, BF16), shaped((8, features), F32), wide(2 * width, BF16)],
        third_part, third_got, stream_two, vec, dy, space_own, space_far,
    )
    space_dq, space_keep, space_send = local_call(
        "space_backward",
        space_backward_kernel,
        [wide(2 * width, BF16), wide(4 * width, F32), wide(4 * width, BF16)],
        place, space_grad_heads, space_q, space_pairs, space_got, space_logs, class_logs, space_col, space_row,
        smem=(0,),
        scratch=[
            pltpu.VMEM((count, 4 * width), BF16),
            pltpu.VMEM((CLASSES, 4 * width), BF16),
            pltpu.VMEM((count, 4 * width), F32),
            pltpu.VMEM((CLASSES, 4 * width), F32),
            pltpu.VMEM((CLASSES, 2 * width), BF16),
        ],
    )
    up_y, down_y, (space_send,) = together(up_y, down_y, [space_send])
    up_shards = z_swaps(y_sums("sum_up", [(up_keep, up_y)]))
    space_got_grads = core_swap(space_send)
    grad_space, grad_space_far, second_part = local_call(
        "space_back",
        space_back_kernel,
        [wide(3 * width, BF16), wide(3 * width, BF16), wide(features, BF16)],
        space_dq, space_keep, space_got_grads, space_own, space_far,
    )
    second_got = x_swap(second_part)
    space_grad_far, space_grad_own = [
        local_call(
            name,
            partial(space_grads_kernel, group),
            [shaped((features, 4 * width), BF16)],
            second, grad, grad_two_low, space_heads,
        )[0]
        for name, group, grad in (("space_grads_far", 1, grad_space_far), ("space_grads_own", 0, grad_space))
    ]

    def whole(name, value, got):
        return pl.pallas_call(
            whole_rows_kernel,
            name=name,
            out_shape=shaped((count, features), F32),
            in_specs=[SMEM, VMEM, VMEM],
            out_specs=ANY,
            scratch_shapes=[pltpu.SemaphoreType.DMA((2,))],
            compiler_params=pltpu.CompilerParams(vmem_limit_bytes=2**23),
            cost_estimate=pl.CostEstimate(flops=0, bytes_accessed=0, transcendentals=0),
        )(place, value, got)

    ((space_y_send, space_keep),) = split_rows("split_space", [(space_grad_own, core_swap(space_grad_far))])
    space_y = [dp_swap(space_y_send, 1)]
    up_shards, space_y, (second_got,) = together(up_shards, space_y, [second_got])
    feed_part_got = x_swap(after(feed_part, space_y_send))
    grad_one, grad_one_low, sums_one, time_grad_own, time_grad_send = local_call(
        "time_back_in",
        time_back_in_kernel,
        [
            wide(features, F32),
            wide(features, BF16),
            shaped((8, features), F32),
            wide(width, BF16),
            wide(width, BF16),
        ],
        second_part, second_got, stream_one, vec, grad_two, fused, fused_far,
    )
    down_shards = z_swaps(y_sums("sum_down", [(down_keep, down_y)]))
    time_grad_got = core_swap(time_grad_send)
    fused_grad, fused_grad_far = local_call(
        "fused_grads",
        fused_grads_kernel,
        [shaped((features, width + SPARE), F32), shaped((features, width + SPARE), BF16)],
        grad_one_low, time_own, time_got,
    )
    fused_grad_got = core_swap(fused_grad_far)
    grad_time_out, fused_total, row_sum, bias_grad = local_call(
        "mix_grads",
        mix_grads_kernel,
        [
            shaped((features, width), BF16),
            shaped((features, width), BF16),
            shaped((features, SPARE), F32),
            shaped((8, features), F32),
        ],
        place, fused_grad, fused_grad_got, mix_blocks, sums_one,
        smem=(0,),
    )
    ((out_send, out_keep),) = split_rows("split_out", [(grad_time_out, None), (fused_total, None)])
    out_send, time_grad_own, time_grad_got = lax.optimization_barrier((out_send, time_grad_own, time_grad_got))
    out_y = [dp_swap(out_send, 1)]
    (grad_time,) = local_call(
        "time_backward",
        time_backward_kernel,
        [shaped((count, 3 * width), BF16)],
        time_grad_own, time_grad_got, order, time_inputs, time_logs, time_col, time_row,
        scratch=[pltpu.VMEM((count, width), BF16), pltpu.VMEM((count, 2 * width), F32)],
    )
    down_shards, out_y, (grad_time, feed_part_got) = together(down_shards, out_y, [grad_time, feed_part_got])
    (layer_half,) = local_call(
        "layer_out", layer_out_kernel, [wide(features, F32)], stream_two, feed_part, feed_part_got, vec
    )
    layer_got = core_swap(layer_half)
    time_columns = 3 * width + SPARE
    time_send, time_keep = local_call(
        "time_grads",
        time_grads_kernel,
        [shaped((half, shard, time_columns), BF16), shaped((half, shard, time_columns), F32)],
        place, first, grad_time, row_sum,
        smem=(0,),
        scratch=[pltpu.VMEM((features, time_columns), F32)],
    )
    out_y, (time_send, grad_time, layer_got) = together(out_y, [time_send, grad_time, layer_got])
    time_y = [dp_swap(time_send, 1)]
    late_sums = jnp.concatenate(
        [keep + arrived[0].astype(F32) for keep, arrived in ((out_keep, out_y), (space_keep, space_y))], 2
    )
    late_shards = z_swaps([late_sums[0], *[late_sums[k].astype(BF16) for k in range(1, half)]])
    first_own, vector_sum, *first_sends = local_call(
        "time_back",
        time_back_kernel,
        [wide(features, BF16), shaped((16, features), F32), wide(features, BF16)],
        grad_time, time_maps, tokens_sorted, back, bias_grad, sums_one, sums_two,
        scratch=[pltpu.VMEM((count, features), BF16)],
    )
    first_got = [core_swap(one) for one in first_sends]
    (first_part,) = local_call("first_part", add_kernel, [wide(features, BF16)], first_own, *first_got)
    time_y, (first_part,) = together(time_y, [first_part])
    first_part_got = x_swap(first_part)
    time_shards = y_sums("sum_time", [(time_keep, time_y)])
    layer_rows = whole("layer_rows", after(layer_half, time_shards[0]), layer_got)
    late_shards = lax.optimization_barrier((*late_shards, time_shards[0], layer_rows))[: len(late_shards)]
    time_shards = z_swaps(time_shards)

    out_width = 2 * width
    out_grad, mix_keep, mix_send = local_call(
        "mix_shard",
        mix_shard_kernel,
        [shaped((shard, width), F32), shaped((shard, out_width), F32), shaped((shard, out_width), BF16)],
        place, out_map, *late_shards,
        smem=(0,),
        flops=LONG,
    )
    mix_own, mix_send = local_call(
        "mix_sum",
        mix_sum_kernel,
        [shaped((shard, width), F32), shaped((shard, width), BF16)],
        mix_keep, core_swap(mix_send),
    )
    mix_got = x_swap(mix_send)

    bias_part = lax.dynamic_slice_in_dim(vec[2:3], lax.axis_index("heads") * width, width, 1)
    late = [out_width, out_width + 4 * width]
    total = lambda shards: sum([one.astype(F32) for one in shards])
    up_shards, down_shards, _ = together(up_shards, down_shards, [first_part])
    early_grad = jnp.concatenate([total(late_shards)[:, out_width:], total(up_shards), total(down_shards)], 1)
    early_square = jnp.sum(early_grad * early_grad)
    time_shards, (early_grad, early_square, mix_got) = together(time_shards, [early_grad, early_square, mix_got])
    time_total = total(time_shards)
    mix_grad = mix_own + mix_got.astype(F32) + time_total[:, 3 * width : 3 * width + 1] * bias_part
    head_grad = jnp.concatenate([time_total[:, : 3 * width], out_grad, mix_grad], 1)
    square = early_square + jnp.sum(head_grad * head_grad)
    row = lax.broadcasted_iota(jnp.int32, vector_sum.shape, 0)
    sums = jnp.where(row == VECTORS, square, vector_sum)

    def input_half(ready):
        return local_call(
            "input_grad",
            input_grad_kernel,
            [wide(features, F32)],
            first_part, after(first_part_got, ready), tokens_own, vec, grad_one,
        )

    def last_results(ready, grad_half):
        grad_rows = whole("grad_rows", grad_half, core_swap(grad_half))
        (weight_grad,) = local_call(
            "whole_grad", whole_grad_kernel, [shaped(weights.shape, F32)], after(head_grad, ready), early_grad
        )
        return [grad_rows, weight_grad]

    terms, (grad_rows, weight_grad) = all_sum(sums, input_half, last_results)
    steps = max(one for one in (1, 2, 3, 4) if shard % (8 * one) == 0)
    states = [weights, weights_m, weights_v, weights_ema]
    vector_states = [vectors, vectors_m, vectors_v, vectors_ema]
    outs = pl.pallas_call(
        partial(update_kernel, len(terms), lax.axis_size("dp"), steps),
        name="update",
        out_shape=[shaped(weights.shape, F32)] * 4
        + [shaped(vectors.shape, F32), shaped((1, 1), F32)]
        + [shaped(vectors.shape, F32)] * 4,
        in_specs=[SMEM] + [VMEM] * (len(terms) + 1) + [ANY] * 4 + [VMEM] * 4,
        out_specs=[ANY] * 4 + [VMEM] * 6,
        scratch_shapes=[pltpu.VMEM(weights.shape, F32)] * 8
        + [pltpu.SemaphoreType.DMA((steps, 4)), pltpu.SemaphoreType.DMA((steps, 4))],
        compiler_params=pltpu.CompilerParams(vmem_limit_bytes=20 * 2**20),
    )(place, *terms, weight_grad, *states, *vector_states)
    weights_out, (vector_grad, grad_norm, *vectors_out) = outs[:4], outs[4:]
    return (
        layer_rows,
        grad_rows,
        weight_grad,
        vector_grad,
        grad_norm[0, 0],
        *weights_out,
        *vectors_out,
    )


def solution(mesh):
    rows, square, line = P("dp", None), P("dp", "heads"), P(None, "dp")
    placed = (rows,) * 5 + (square,) * 4 + (line,) * 4
    return jax.shard_map(
        local,
        mesh=mesh,
        in_specs=placed,
        out_specs=(rows, rows, square, line, P()) + (square,) * 4 + (line,) * 4,
        check_vma=False,
    )
```

```python
import math
from functools import partial

import jax
import jax.numpy as jnp
from jax import lax
from jax.experimental import pallas as pl
from jax.experimental.pallas import tpu as pltpu
from jax.sharding import PartitionSpec as P

HEAD_DIM = 64
STEP = 5
NPARAM = 10034688
VECTORS = 10

NORM_EPS = 1e-06
BETA_FIRST = 0.5
BETA_SECOND = 0.5
AVERAGE_RATE = 0.5
MATRIX_RATE = 0.03
VECTOR_RATE = 0.3
MATRIX_DECAY = 0.05
ADAM_EPS = 1e-08
MASKED = -1e30
SCALE = HEAD_DIM ** (-0.5)
F32 = jnp.float32
BF16 = jnp.bfloat16

BLOCK = 128
WINDOW = 256
CLASSES = 16
CHUNK = 256
UNROLL = 4
SPARE = 64
LONG = 40_000_000_000

VMEM = pl.BlockSpec(memory_space=pltpu.VMEM)
SMEM = pl.BlockSpec(memory_space=pltpu.SMEM)
ANY = pl.BlockSpec(memory_space=pl.ANY)


def core_swap(value):
    return lax.ppermute(value, "heads", [(i, i ^ 1) for i in range(4)])


def x_swap(value):
    return lax.ppermute(value, "heads", [(i, i ^ 2) for i in range(4)])


def dp_swap(value, mask):
    count = lax.axis_size("dp")
    return lax.ppermute(value, "dp", [(i, i ^ mask) for i in range(count)])


def all_sum(value, early, late):
    count = lax.axis_size("dp") * lax.axis_size("heads")
    value = value + core_swap(value)
    step, made = 2, None
    while step < count:
        masks = [step, 2 * step, 3 * step] if 2 * step < count else [step]
        got = [lax.ppermute(value, ("dp", "heads"), [(i, i ^ mask) for i in range(count)]) for mask in masks]
        step *= 4
        if made is None:
            made = early(value)
            got, made = together(got, made)
        if step >= count:
            break
        value = value + got[0]
        if len(got) > 1:
            value = value + (got[1] + got[2])
    made = late(value, *made)
    got, made = together(got, made)
    return [value, *got], made


def after(value, *others):
    return lax.optimization_barrier((value, *others))[0]


def together(*groups):
    flat = lax.optimization_barrier([one for group in groups for one in group])
    split, at = [], 0
    for group in groups:
        split.append(list(flat[at : at + len(group)]))
        at += len(group)
    return split


def shaped(shape, dtype):
    return jax.ShapeDtypeStruct(shape, dtype)


def local_call(name, kernel, outs, *operands, scratch=(), smem=(), extra=6, flops=0, staged=False):
    spec = VMEM
    if staged:
        spec, inner, count = ANY, kernel, len(operands)
        moved = [i for i in range(count) if i not in smem]

        def kernel(*refs):
            ins, rest, held, sem = list(refs[:count]), refs[count : -1 - len(moved)], refs[-1 - len(moved) : -1], refs[-1]
            copies = [pltpu.make_async_copy(ins[i], ref, sem.at[j]) for j, (i, ref) in enumerate(zip(moved, held))]
            for copy in copies:
                copy.start()
            for copy, i, ref in zip(copies, moved, held):
                copy.wait()
                ins[i] = ref
            inner(*ins, *rest)

        scratch = [*scratch, *[pltpu.VMEM(operands[i].shape, operands[i].dtype) for i in moved]]
    held = sum(math.prod(one.shape) * jnp.dtype(one.dtype).itemsize for one in scratch)
    return pl.pallas_call(
        kernel,
        name=name,
        out_shape=list(outs),
        in_specs=[SMEM if i in smem else spec for i in range(len(operands))],
        out_specs=[VMEM] * len(outs),
        scratch_shapes=[*scratch, *([pltpu.SemaphoreType.DMA((len(moved),))] if staged else [])],
        compiler_params=pltpu.CompilerParams(
            vmem_limit_bytes=held + extra * 2**20
        ),
        cost_estimate=pl.CostEstimate(flops=flops, bytes_accessed=0, transcendentals=0),
    )(*operands)


def dot(left, right):
    return jnp.dot(left, right, preferred_element_type=F32)


def dot_nt(left, right):
    return lax.dot_general(left, right, (((1,), (1,)), ((), ())), preferred_element_type=F32)


def dot_tn(left, right):
    return lax.dot_general(left, right, (((0,), (0,)), ((), ())), preferred_element_type=F32)


def chunk_loop(rows, body, size=CHUNK):
    def step(i, carry):
        body(pl.ds(pl.multiple_of(i * size, size), size))
        return carry

    lax.fori_loop(0, rows // size, step, 0)


def normed(stream):
    center = stream - jnp.mean(stream, -1, keepdims=True)
    factor = lax.rsqrt(jnp.mean(center * center, -1, keepdims=True) + NORM_EPS)
    return center * factor, factor


def norm_grad(hat, factor, gain, grad):
    scaled = grad * gain
    return factor * (
        scaled - jnp.mean(scaled, -1, keepdims=True) - hat * jnp.mean(scaled * hat, -1, keepdims=True)
    )


def column_sum(value):
    return jnp.sum(value, 0, keepdims=True)


def z_blocks(piece):
    order = range(lax.axis_size("dp") // 2 - 1, 0, -1)
    got = {k: dp_swap(piece, 2 * k) for k in order}
    return [piece] + [got[k] for k in sorted(got)]


def y_blocks(mine, fine=False):
    return [dp_swap(one, 1) for one in mine] if fine else [dp_swap(jnp.stack(mine), 1)]


def assemble(name, mine, other, cuts=()):
    half, count, fine = len(mine), lax.axis_size("dp"), len(other) > 1
    rows, columns = mine[0].shape
    bounds = [0, *cuts, columns]
    parts = [slice(start, stop) for start, stop in zip(bounds, bounds[1:])]

    def kernel(place_ref, *refs):
        z, y = place_ref[0], place_ref[1]
        for out_ref, part in zip(refs[half + len(other) :], parts):
            for k in range(half):
                out_ref[(z ^ k) * 2 + y] = refs[k][:, part]
                out_ref[(z ^ k) * 2 + (1 - y)] = refs[half + k][:, part] if fine else refs[half][k, :, part]

    outs = local_call(
        name,
        kernel,
        [shaped((count, rows, part.stop - part.start), mine[0].dtype) for part in parts],
        places(), *mine, *other,
        smem=(0,),
    )
    outs = [one.reshape(count * rows, -1) for one in outs]
    return outs if cuts else outs[0]


def places():
    dp, heads = lax.axis_index("dp"), lax.axis_index("heads")
    return jnp.stack([dp // 2, dp % 2, heads, heads % 2, dp]).astype(jnp.int32)


def split_rows(name, totals, cuts=()):
    count = lax.axis_size("dp")
    half = count // 2
    operands, columns = [], 0
    for own, received in totals:
        rows = own.shape[0] // count
        operands += [one.reshape(count, rows, own.shape[1]) for one in (own, received) if one is not None]
        columns += own.shape[1]
    bounds = [0, *cuts, columns]
    parts = list(zip(bounds, bounds[1:]))

    def kernel(place_ref, *refs):
        ins, outs = refs[: len(operands)], refs[len(operands) :]
        z, y = place_ref[0], place_ref[1]
        for k in range(half):
            for side in range(2):
                block = (z ^ k) * 2 + (1 - y if side == 0 else y)
                at, column = 0, 0
                for own, received in totals:
                    value = ins[at][block].astype(F32)
                    at += 1
                    if received is not None:
                        value = value + ins[at][block].astype(F32)
                        at += 1
                    for i, (start, stop) in enumerate(parts):
                        first, last = max(start, column), min(stop, column + own.shape[1])
                        if first < last:
                            ref = outs[2 * i + side]
                            ref[k, :, first - start : last - start] = value[:, first - column : last - column].astype(
                                ref.dtype
                            )
                    column += own.shape[1]

    outs = []
    for start, stop in parts:
        outs += [shaped((half, rows, stop - start), BF16), shaped((half, rows, stop - start), F32)]
    outs = local_call(name, kernel, outs, places(), *operands, smem=(0,))
    return list(zip(outs[::2], outs[1::2]))


def y_sums(name, pieces, flops=0):
    half, rows, _ = pieces[0][0].shape
    columns = [keep.shape[2] for keep, _ in pieces]
    fine = len(pieces[0][1]) > 1
    operands = [one for keep, arrived in pieces for one in (keep, *arrived)]
    step = 1 + len(pieces[0][1])

    def kernel(*refs):
        ins, outs = refs[: len(operands)], refs[len(operands) :]
        column = 0
        for i, width in enumerate(columns):
            part = slice(column, column + width)
            column += width
            for k in range(half):
                there = ins[i * step + 1 + k][...] if fine else ins[i * step + 1][k]
                value = ins[i * step][k] + there.astype(F32)
                outs[k][:, part] = value.astype(outs[k].dtype)

    outs = [shaped((rows, sum(columns)), F32)] + [shaped((rows, sum(columns)), BF16)] * (half - 1)
    return local_call(name, kernel, outs, *operands, flops=flops)


def z_swaps(summed):
    return [summed[0]] + [dp_swap(summed[k], 2 * k) for k in range(1, len(summed))]


def head_pairs(width):
    pair = 2 * HEAD_DIM
    return [(at, min(at + pair, width), min(2, (width - at) // HEAD_DIM)) for at in range(0, width, pair)]


def by_head(value, heads):
    if heads == 1:
        return value
    lane = lax.broadcasted_iota(jnp.int32, value.shape, 1)
    zero = jnp.zeros_like(value)
    return jnp.concatenate(
        [jnp.where(lane < HEAD_DIM, value, zero), jnp.where(lane < HEAD_DIM, zero, value)], 0
    )


def own_columns(value, heads):
    if heads == 1:
        return value
    count = value.shape[1] // 2
    return jnp.concatenate([value[:HEAD_DIM, :count], value[HEAD_DIM:, count:]], 0)


def own_rows(value, heads):
    if heads == 1:
        return value
    count = value.shape[0] // 2
    lane = lax.broadcasted_iota(jnp.int32, (count, value.shape[1]), 1)
    return jnp.where(lane < HEAD_DIM, value[:count], value[count:])


def masked_bias(allowed):
    return jnp.where(allowed, 0.0, MASKED).astype(F32)


def pair_forward(q, keys, values, bias, heads):
    scores = dot_nt(keys, by_head(q, heads)) + (bias if heads == 1 else jnp.concatenate([bias, bias], 1))
    top = jnp.max(scores, 0, keepdims=True)
    exps = jnp.exp(scores - top)
    total = jnp.sum(exps, 0, keepdims=True)
    out = dot_tn(values, exps.astype(BF16)) / total
    log = top + jnp.log(total)
    count = q.shape[0]
    return own_columns(out, heads), [log[:, h * count : (h + 1) * count] for h in range(heads)]


def pair_backward(q, grad, keys, values, bias, logs, heads):
    q, grad = by_head(q, heads), by_head(grad, heads)
    if heads > 1:
        bias, logs = jnp.concatenate([bias, bias], 1), [jnp.concatenate(logs, 1)]
    probs = jnp.exp(dot_nt(keys, q) + bias - logs[0])
    grad_probs = dot_nt(values, grad)
    delta = jnp.sum(probs * grad_probs, 0, keepdims=True)
    grad_scores = (probs * (grad_probs - delta)).astype(BF16)
    grad_q = own_columns(dot_tn(keys, grad_scores), heads) * SCALE
    return grad_q, dot(grad_scores, q), dot(probs.astype(BF16), grad)


def sort_kernel(
    place_ref, clip_ref, frame_ref, patch_ref, tokens_ref, dy_ref,
    sorted_ref, order_ref, back_ref, col_ref, row_ref, space_col_ref, space_row_ref, own_ref, own_dy_ref,
    all_ref,
):
    count = tokens_ref.shape[0]
    rows = count // 2
    core = place_ref[3]
    own = pl.ds(pl.multiple_of(core * rows, rows), rows)
    far = pl.ds(pl.multiple_of((1 - core) * rows, rows), rows)
    own_ref[...] = tokens_ref[own, :]
    own_dy_ref[...] = dy_ref[own, :]
    all_ref[:rows, :] = tokens_ref[own, :]
    all_ref[rows:, :] = tokens_ref[far, :]
    ids = [clip_ref, frame_ref, patch_ref]
    spare = jnp.zeros((5, count), jnp.int32)
    natural = jnp.concatenate([ref[...] for ref in ids] + [spare], 0)
    space_row_ref[...] = natural
    space_col_ref[...] = natural.astype(F32).T.astype(jnp.int32)
    ordered = jnp.concatenate(
        [jnp.concatenate([ref[:, own], ref[:, far]], 1) for ref in ids] + [spare], 0
    )
    ordered_col = ordered.astype(F32).T.astype(jnp.int32)
    key_row = (ordered[0:1] * 128 + ordered[2:3] + 1) * 64 + ordered[1:2] + 1
    key_col = (ordered_col[:, 0:1] * 128 + ordered_col[:, 2:3] + 1) * 64 + ordered_col[:, 1:2] + 1
    rank_row = jnp.zeros((1, count), jnp.int32)
    for i in range(0, count, CHUNK):
        smaller = key_col[i : i + CHUNK] < key_row
        rank_row = rank_row + jnp.sum(smaller.astype(jnp.int32), 0, keepdims=True)
    for i in range(0, count, CHUNK):
        at = slice(i, i + CHUNK)
        place = lax.broadcasted_iota(jnp.int32, (CHUNK, count), 0) + i
        order = (place == rank_row).astype(F32).astype(BF16)
        order_ref[at, :] = order
        rank_col = jnp.sum((key_row < key_col[at]).astype(jnp.int32), 1, keepdims=True)
        place = lax.broadcasted_iota(jnp.int32, (CHUNK, count), 1)
        back_ref[at, :] = (place == rank_col).astype(F32).astype(BF16)
        sorted_ref[at, :] = dot(order, all_ref[...]).astype(BF16)
        col_ref[at, :] = dot(order, ordered_col.astype(F32).astype(BF16))
        row_ref[:, at] = dot_nt(ordered.astype(F32).astype(BF16), order)


def pack_kernel(weights_ref, vectors_ref, head_ref, space_ref, up_ref, down_ref):
    width, hidden = space_ref.shape[1] // 4, up_ref.shape[1]
    rows = weights_ref.shape[0]
    start = head_ref.shape[1] - 2 * width
    unit = lax.broadcasted_iota(jnp.int32, (rows, rows), 0) == lax.broadcasted_iota(jnp.int32, (rows, rows), 1)
    vectors = jnp.concatenate([vectors_ref[...], jnp.zeros((16 - VECTORS, rows), F32)], 0).astype(BF16)
    head_ref[:, : 3 * width] = weights_ref[:, : 3 * width].astype(BF16)
    head_ref[:, 3 * width : start] = jnp.zeros((rows, start - 3 * width), BF16)
    head_ref[:, 3 * width : 3 * width + 16] = dot_nt(unit.astype(F32).astype(BF16), vectors).astype(BF16)
    head_ref[:, start : start + width] = weights_ref[:, 4 * width : 5 * width].astype(BF16)
    head_ref[:, start + width :] = weights_ref[:, 3 * width : 4 * width].astype(BF16)
    space_ref[...] = weights_ref[:, 5 * width : 9 * width].astype(BF16)
    up_ref[...] = weights_ref[:, 9 * width : 9 * width + hidden].astype(BF16)
    down_ref[...] = weights_ref[:, 9 * width + hidden :].astype(BF16)


def same_clip_patch(col_ref, row_ref, keys, queries):
    key = col_ref[keys, :]
    query = row_ref[:, queries]
    return (key[:, 0:1] * 128 + key[:, 2:3]) == (query[0:1] * 128 + query[2:3])


def temporal_window(i, count):
    first = i * BLOCK
    start = jnp.clip(first - (WINDOW - BLOCK) // 2, 0, count - WINDOW)
    return (
        pl.ds(pl.multiple_of(first, BLOCK), BLOCK),
        pl.ds(pl.multiple_of(start, (WINDOW - BLOCK) // 2), WINDOW),
    )


def time_forward_kernel(
    maps_ref, tokens_ref, back_ref, col_ref, row_ref,
    vec_ref, first_ref, inputs_ref, own_ref, far_ref, log_ref, heads_ref,
):
    count, width = tokens_ref.shape[0], own_ref.shape[1]
    columns = maps_ref.shape[1]
    lanes = maps_ref[:, columns - 128 :].astype(F32).T
    offset = 3 * width - (columns - 128)
    vec_ref[...] = lanes[offset : offset + 16]
    gain, shift = vec_ref[0:1], vec_ref[1:2]

    def project(at):
        hat, _ = normed(tokens_ref[at, :].astype(F32))
        first = (hat * gain + shift).astype(BF16)
        first_ref[at, :] = first
        inputs_ref[at, :] = dot(first, maps_ref[:, : 3 * width]).astype(BF16)

    chunk_loop(count, project)

    def step(i, carry):
        queries, keys = temporal_window(i, count)
        bias = masked_bias(same_clip_patch(col_ref, row_ref, keys, queries))
        outs, logs = [], []
        for start, stop, heads in head_pairs(width):
            out, log = pair_forward(
                inputs_ref[queries, start:stop] * BF16(SCALE),
                inputs_ref[keys, width + start : width + stop],
                inputs_ref[keys, 2 * width + start : 2 * width + stop],
                bias,
                heads,
            )
            outs.append(out)
            logs += log
        heads_ref[queries, :] = jnp.concatenate(outs, 0).T.astype(BF16)
        log_ref[:, queries] = jnp.concatenate(logs + [logs[0]] * (8 - len(logs)), 0)
        return carry

    lax.fori_loop(0, count // BLOCK, step, 0, unroll=8)
    rows = count // 2
    for i in range(0, rows, CHUNK):
        own_ref[i : i + CHUNK, :] = dot(back_ref[i : i + CHUNK, :], heads_ref[...]).astype(BF16)
        far_ref[i : i + CHUNK, :] = dot(back_ref[rows + i : rows + i + CHUNK, :], heads_ref[...]).astype(BF16)


def time_backward_kernel(
    own_ref, far_ref, order_ref, inputs_ref, log_ref, col_ref, row_ref,
    out_ref, grad_ref, sum_ref,
):
    count, width = inputs_ref.shape[0], own_ref.shape[1]
    rows = count // 2
    for i in range(0, count, CHUNK):
        grad_ref[i : i + CHUNK, :] = (
            dot(order_ref[i : i + CHUNK, :rows], own_ref[...]) + dot(order_ref[i : i + CHUNK, rows:], far_ref[...])
        ).astype(BF16)
    sum_ref[...] = jnp.zeros_like(sum_ref)

    def step(i, carry):
        queries, keys = temporal_window(i, count)
        bias = masked_bias(same_clip_patch(col_ref, row_ref, keys, queries))
        grad_qs, head = [], 0
        for start, stop, heads in head_pairs(width):
            grad_q, grad_k, grad_v = pair_backward(
                inputs_ref[queries, start:stop] * BF16(SCALE),
                grad_ref[queries, start:stop],
                inputs_ref[keys, width + start : width + stop],
                inputs_ref[keys, 2 * width + start : 2 * width + stop],
                bias,
                [log_ref[h : h + 1, queries] for h in range(head, head + heads)],
                heads,
            )
            head += heads
            grad_qs.append(grad_q)
            sum_ref[keys, start:stop] += grad_k
            sum_ref[keys, width + start : width + stop] += grad_v
        out_ref[queries, :width] = jnp.concatenate(grad_qs, 0).T.astype(BF16)
        return carry

    lax.fori_loop(0, count // BLOCK, step, 0, unroll=8)

    def store(at):
        out_ref[at, width:] = sum_ref[at, :].astype(BF16)

    chunk_loop(count, store)


def space_window(i, core, rows):
    first = core * rows + i * BLOCK
    start = jnp.clip(first - (WINDOW - BLOCK) // 2, 0, 2 * rows - WINDOW)
    return (
        pl.ds(pl.multiple_of(i * BLOCK, BLOCK), BLOCK),
        pl.ds(pl.multiple_of(first, BLOCK), BLOCK),
        pl.ds(pl.multiple_of(start, (WINDOW - BLOCK) // 2), WINDOW),
    )


def whole_pairs(core, pairs_ref, got_ref, whole_ref):
    rows, width = pairs_ref.shape[0], pairs_ref.shape[1] // 4
    whole_ref[pl.ds(pl.multiple_of(core * rows, rows), rows), :] = pairs_ref[...]
    there = pl.ds(pl.multiple_of((1 - core) * rows, rows), rows)
    for i, j in enumerate((1, 0, 3, 2)):
        whole_ref[there, i * width : (i + 1) * width] = got_ref[:, j * width : (j + 1) * width]


def class_rows(row):
    number = lax.broadcasted_iota(jnp.int32, (CLASSES, row.shape[1]), 0)
    return (row[0:1] == number) & (row[1:2] < 0)


def space_bias(col_ref, row_ref, queries, keys):
    key, query = col_ref[keys, :], row_ref[:, queries]
    frame = jnp.where(key[:, 1:2] < 0, -1, key[:, 0:1] * 128 + key[:, 1:2]) == query[0:1] * 128 + query[1:2]
    number = lax.broadcasted_iota(jnp.int32, (CLASSES, BLOCK), 0)
    return masked_bias(jnp.concatenate([frame & (query[1:2] >= 0), number == query[0:1]], 0))


def class_allowed(row_ref):
    number = lax.broadcasted_iota(jnp.int32, (CLASSES, row_ref.shape[1]), 0)
    return row_ref[0:1] == number


def space_forward_kernel(
    place_ref, q_ref, pairs_ref, got_ref, col_ref, row_ref, out_own_ref, out_far_ref,
    heads_ref, log_ref, class_log_ref, part_ref, whole_ref, class_ref,
):
    core = place_ref[3]
    rows, width = q_ref.shape
    whole_pairs(core, pairs_ref, got_ref, whole_ref)
    here = pl.ds(pl.multiple_of(core * rows, rows), rows)
    classes = class_rows(row_ref[...]).astype(F32).astype(BF16)
    own_classes = class_rows(row_ref[:, here]).astype(F32).astype(BF16)
    class_ref[...] = dot(classes, whole_ref[...]).astype(BF16)
    def both(keys, part):
        return jnp.concatenate([whole_ref[keys, part], class_ref[:, part]], 0)

    def step(i, carry):
        local, queries, keys = space_window(i, core, rows)
        bias = space_bias(col_ref, row_ref, queries, keys)
        outs, logs = [], []
        for start, stop, heads in head_pairs(width):
            out, log = pair_forward(
                q_ref[local, start:stop] * BF16(SCALE),
                both(keys, slice(start, stop)),
                both(keys, slice(width + start, width + stop)),
                bias,
                heads,
            )
            outs.append(out)
            logs += log
        heads_ref[local, :] = jnp.concatenate(outs, 0).T.astype(BF16)
        log_ref[:, local] = jnp.concatenate(logs + [logs[0]] * (8 - len(logs)), 0)
        return carry

    lax.fori_loop(0, rows // BLOCK, step, 0, unroll=UNROLL)

    bias = masked_bias(class_allowed(row_ref))
    class_q = dot(own_classes, q_ref[...]).astype(BF16) * BF16(SCALE)
    outs, logs = [], []
    for start, stop, heads in head_pairs(width):
        scores = dot_nt(by_head(class_q[:, start:stop], heads), whole_ref[:, start:stop])
        scores = scores + (bias if heads == 1 else jnp.concatenate([bias, bias], 0))
        top = jnp.max(scores, 1, keepdims=True)
        exps = jnp.exp(scores - top)
        total = jnp.sum(exps, 1, keepdims=True)
        outs.append(own_rows(dot(exps.astype(BF16), whole_ref[:, width + start : width + stop]) / total, heads))
        log = top + jnp.log(total)
        logs += [log[h * CLASSES : (h + 1) * CLASSES] for h in range(heads)]
    class_log_ref[...] = jnp.concatenate(logs + [logs[0]] * (8 - len(logs)), 1)
    class_out = jnp.concatenate(outs, 1).astype(BF16)
    is_class = col_ref[here, 1:2] < 0

    def replace(at):
        back = dot_tn(own_classes, class_out).astype(BF16)
        heads_ref[...] = jnp.where(is_class, back, heads_ref[...])

    replace(None)
    group = width // 2

    def project(at):
        part_ref[at, :] = (
            dot_nt(heads_ref[at, :group], out_own_ref[:, 3 * group :])
            + dot_nt(heads_ref[at, group:], out_far_ref[:, 3 * group :])
        ).astype(BF16)

    chunk_loop(rows, project)


def space_back_in_kernel(
    part_ref, got_ref, stream_ref, vec_ref, dy_ref, out_own_ref, out_far_ref,
    grad_ref, low_ref, sums_ref, heads_ref,
):
    group = heads_ref.shape[1] // 2
    gain = vec_ref[7:8]
    sums_ref[...] = jnp.zeros_like(sums_ref)

    def through_norm(at):
        grad = part_ref[at, :].astype(F32) + got_ref[at, :].astype(F32)
        hat, factor = normed(stream_ref[at, :])
        dy = dy_ref[at, :].astype(F32)
        dx = dy + norm_grad(hat, factor, gain, grad)
        grad_ref[at, :] = dx
        low = dx.astype(BF16)
        low_ref[at, :] = low
        heads_ref[at, :group] = dot(low, out_own_ref[:, 3 * group :]).astype(BF16)
        heads_ref[at, group:] = dot(low, out_far_ref[:, 3 * group :]).astype(BF16)
        sums_ref[0:4] += jnp.concatenate(
            [column_sum(dx), column_sum(grad * hat), column_sum(grad), column_sum(dy)], 0
        )

    chunk_loop(grad_ref.shape[0], through_norm)


def space_backward_kernel(
    place_ref, heads_ref, q_ref, pairs_ref, got_ref, log_ref, class_log_ref, col_ref, row_ref,
    dq_ref, keep_ref, send_ref,
    whole_ref, class_ref, total_ref, class_total_ref, class_dq_ref,
):
    core = place_ref[3]
    rows, width = q_ref.shape
    whole_pairs(core, pairs_ref, got_ref, whole_ref)
    here = pl.ds(pl.multiple_of(core * rows, rows), rows)
    there = pl.ds(pl.multiple_of((1 - core) * rows, rows), rows)
    classes = class_rows(row_ref[...]).astype(F32)
    own_classes = class_rows(row_ref[:, here]).astype(F32).astype(BF16)
    class_ref[...] = dot(classes.astype(BF16), whole_ref[...]).astype(BF16)
    class_total_ref[...] = jnp.zeros_like(class_total_ref)
    bias = masked_bias(class_allowed(row_ref))
    class_q = dot(own_classes, q_ref[...]).astype(BF16) * BF16(SCALE)
    class_g = dot(own_classes, heads_ref[...]).astype(BF16)
    head = 0
    for start, stop, heads in head_pairs(width):
        keys, values = whole_ref[:, start:stop], whole_ref[:, width + start : width + stop]
        q, grad = by_head(class_q[:, start:stop], heads), by_head(class_g[:, start:stop], heads)
        logs = [class_log_ref[:, h : h + 1] for h in range(head, head + heads)]
        head += heads
        scores = dot_nt(q, keys) + (bias if heads == 1 else jnp.concatenate([bias, bias], 0))
        probs = jnp.exp(scores - jnp.concatenate(logs, 0))
        grad_probs = dot_nt(grad, values)
        grad_scores = (probs * (grad_probs - jnp.sum(probs * grad_probs, 1, keepdims=True))).astype(BF16)
        class_dq_ref[:, start:stop] = own_rows(dot(grad_scores, keys) * SCALE, heads).astype(BF16)
        total_ref[:, start:stop] = dot_tn(grad_scores, q)
        total_ref[:, width + start : width + stop] = dot_tn(probs.astype(BF16), grad)

    def both(keys, part):
        return jnp.concatenate([whole_ref[keys, part], class_ref[:, part]], 0)

    def step(i, carry):
        local, queries, keys = space_window(i, core, rows)
        bias = space_bias(col_ref, row_ref, queries, keys)
        is_class = row_ref[1:2, queries] < 0
        grad_qs, head = [], 0
        for start, stop, heads in head_pairs(width):
            key_part, value_part = slice(start, stop), slice(width + start, width + stop)
            grad_q, grad_k, grad_v = pair_backward(
                q_ref[local, start:stop] * BF16(SCALE),
                heads_ref[local, start:stop],
                both(keys, key_part),
                both(keys, value_part),
                bias,
                [jnp.where(is_class, -MASKED, log_ref[h : h + 1, local]) for h in range(head, head + heads)],
                heads,
            )
            head += heads
            grad_qs.append(grad_q)
            total_ref[keys, key_part] += grad_k[:WINDOW]
            total_ref[keys, value_part] += grad_v[:WINDOW]
            class_total_ref[:, key_part] += grad_k[WINDOW:]
            class_total_ref[:, value_part] += grad_v[WINDOW:]
        dq_ref[local, :] = jnp.concatenate(grad_qs, 0).T.astype(BF16)
        return carry

    lax.fori_loop(0, rows // BLOCK, step, 0, unroll=UNROLL)
    dq_ref[...] = jnp.where(
        col_ref[here, 1:2] < 0, dot_tn(own_classes, class_dq_ref[...]).astype(BF16), dq_ref[...]
    )
    high = class_total_ref[...].astype(BF16)
    rest = (class_total_ref[...] - high.astype(F32)).astype(BF16)
    classes = classes.astype(BF16)
    total_ref[...] += dot_tn(jnp.concatenate([classes, classes], 0), jnp.concatenate([high, rest], 0))
    keep_ref[...] = total_ref[here, :]
    send_ref[...] = total_ref[there, :].astype(BF16)


def mix_kernel(place_ref, out_ref, own_ref, x_ref, core_ref, vec_ref, mix_ref, fused_ref, bias_ref):
    place = place_ref[2]
    width = out_ref.shape[1]
    mix_ref[0] = own_ref[...]
    mix_ref[1] = core_ref[:, :width]
    mix_ref[2] = x_ref[...]
    mix_ref[3] = core_ref[:, width:]
    total, bias = 0.0, 0.0
    low = vec_ref[...].astype(BF16)
    for j in range(4):
        block = mix_ref[place ^ j]
        total = total + dot(block, out_ref[j * width : (j + 1) * width, :])
        bias = bias + dot_nt(low[:, j * width : (j + 1) * width], block)
    fused_ref[...] = total.astype(BF16)
    bias_ref[...] = bias[2:3] + vec_ref[3:4]


def time_out_kernel(own_ref, got_ref, fused_ref, far_ref, part_ref):
    def project(at):
        part_ref[at, :] = (dot_nt(own_ref[at, :], fused_ref[...]) + dot_nt(got_ref[at, :], far_ref[...])).astype(BF16)

    chunk_loop(part_ref.shape[0], project)


def norm_in_kernel(gain_row, before_ref, part_ref, got_ref, shift_ref, vec_ref, stream_ref, normed_ref):
    gain, shift = vec_ref[gain_row : gain_row + 1], vec_ref[gain_row + 1 : gain_row + 2]

    def body(at):
        stream = (
            before_ref[at, :].astype(F32)
            + (part_ref[at, :].astype(F32) + got_ref[at, :].astype(F32))
            + shift_ref[0:1]
        )
        stream_ref[at, :] = stream
        hat, _ = normed(stream)
        normed_ref[at, :] = (hat * gain + shift).astype(BF16)

    chunk_loop(stream_ref.shape[0], body)


def space_in_kernel(second_ref, own_ref, far_ref, q_ref, pairs_ref):
    width = q_ref.shape[1] // 2

    def project(at):
        for g, maps_ref in enumerate((own_ref, far_ref)):
            inputs = dot(second_ref[at, :], maps_ref[:, : 3 * width]).astype(BF16)
            q_ref[at, g * width : (g + 1) * width] = inputs[:, :width]
            pairs_ref[at, g * width : (g + 1) * width] = inputs[:, width : 2 * width]
            pairs_ref[at, (2 + g) * width : (3 + g) * width] = inputs[:, 2 * width :]

    chunk_loop(q_ref.shape[0], project)


def gelu_parts(pre):
    cdf = 0.5 * (1.0 + lax.erf(pre * (0.5**0.5)))
    slope = cdf + pre * jnp.exp(-0.5 * pre * pre) * (1.0 / math.sqrt(2.0 * math.pi))
    return pre * cdf, slope


def feed_kernel(
    third_ref, dy_ref, up_ref, up_far_ref, down_ref, down_far_ref, activ_ref, grad_ref, back_ref
):
    hidden = activ_ref.shape[1] // 2

    def project(at):
        back = 0.0
        for g, (ups_ref, downs_ref) in enumerate(((up_ref, down_ref), (up_far_ref, down_far_ref))):
            act, slope = gelu_parts(dot(third_ref[at, :], ups_ref[...]))
            part = slice(g * hidden, (g + 1) * hidden)
            activ_ref[at, part] = act.astype(BF16)
            grad = (dot(dy_ref[at, :], downs_ref[...]) * slope).astype(BF16)
            grad_ref[at, part] = grad
            back = back + dot_nt(grad, ups_ref[...])
        back_ref[at, :] = back.astype(BF16)

    chunk_loop(third_ref.shape[0], project)


def feed_out_kernel(activ_ref, own_ref, far_ref, part_ref):
    hidden = activ_ref.shape[1] // 2

    def project(at):
        part_ref[at, :] = (
            dot_nt(activ_ref[at, :hidden], own_ref[...]) + dot_nt(activ_ref[at, hidden:], far_ref[...])
        ).astype(BF16)

    chunk_loop(part_ref.shape[0], project)


def feed_grads_kernel(group, third_ref, grad_ref, dy_ref, activ_ref, out_ref):
    hidden = out_ref.shape[1] // 2
    part = slice(group * hidden, (group + 1) * hidden)
    out_ref[:, :hidden] = dot_tn(third_ref[...], grad_ref[:, part]).astype(BF16)
    out_ref[:, hidden:] = dot_tn(dy_ref[...], activ_ref[:, part]).astype(BF16)


def space_back_kernel(
    dq_ref, keep_ref, got_ref, own_ref, far_ref, grad_own_ref, grad_far_ref, part_ref
):
    width = dq_ref.shape[1] // 2

    def project(at):
        total = 0.0
        for g, (maps_ref, grad_ref) in enumerate(((own_ref, grad_own_ref), (far_ref, grad_far_ref))):
            grad_ref[at, :width] = dq_ref[at, g * width : (g + 1) * width]
            for i in (1, 2):
                mine = slice((2 * i - 2 + g) * width, (2 * i - 1 + g) * width)
                theirs = slice((2 * i - 1 - g) * width, (2 * i - g) * width)
                grad_ref[at, i * width : (i + 1) * width] = (
                    keep_ref[at, mine] + got_ref[at, theirs].astype(F32)
                ).astype(BF16)
            total = total + dot_nt(grad_ref[at, :], maps_ref[:, : 3 * width])
        part_ref[at, :] = total.astype(BF16)

    chunk_loop(part_ref.shape[0], project)


def space_grads_kernel(group, second_ref, grad_ref, low_ref, heads_ref, out_ref):
    width = heads_ref.shape[1] // 2
    out_ref[:, : 3 * width] = dot_tn(second_ref[...], grad_ref[...]).astype(BF16)
    out_ref[:, 3 * width :] = dot_tn(low_ref[...], heads_ref[:, group * width : (group + 1) * width]).astype(BF16)


def time_back_in_kernel(
    part_ref, got_ref, stream_ref, vec_ref, before_ref, fused_ref, far_ref,
    grad_ref, low_ref, sums_ref, own_ref, send_ref,
):
    gain = vec_ref[4:5]
    sums_ref[...] = jnp.zeros_like(sums_ref)

    def through_norm(at):
        grad = part_ref[at, :].astype(F32) + got_ref[at, :].astype(F32)
        hat, factor = normed(stream_ref[at, :])
        dx = before_ref[at, :] + norm_grad(hat, factor, gain, grad)
        grad_ref[at, :] = dx
        low = dx.astype(BF16)
        low_ref[at, :] = low
        own_ref[at, :] = dot(low, fused_ref[...]).astype(BF16)
        send_ref[at, :] = dot(low, far_ref[...]).astype(BF16)
        sums_ref[0:4] += jnp.concatenate(
            [column_sum(low.astype(F32)), column_sum(dx), column_sum(grad * hat), column_sum(grad)], 0
        )

    chunk_loop(grad_ref.shape[0], through_norm)


def time_grads_kernel(place_ref, first_ref, grad_ref, row_sum_ref, send_ref, keep_ref, total_ref):
    half, rows, columns = keep_ref.shape
    width = columns - row_sum_ref.shape[1]
    z, y = place_ref[0], place_ref[1]
    total_ref[:, :width] = dot_tn(first_ref[...], grad_ref[...])
    total_ref[:, width:] = row_sum_ref[...]
    for k in range(half):
        mine = pl.ds(pl.multiple_of(((z ^ k) * 2 + y) * rows, 8), rows)
        theirs = pl.ds(pl.multiple_of(((z ^ k) * 2 + (1 - y)) * rows, 8), rows)
        send_ref[k] = total_ref[theirs, :].astype(BF16)
        keep_ref[k] = total_ref[mine, :]


def time_back_kernel(
    grad_ref, maps_ref, tokens_ref, back_ref, bias_ref, one_ref, two_ref, own_ref, far_ref, sums_ref, sorted_ref
):
    count, width = tokens_ref.shape[0], grad_ref.shape[1] // 3
    sums_ref[...] = jnp.zeros_like(sums_ref)
    sums_ref[2:3] = 0.5 * bias_ref[0:1]
    sums_ref[3:6] = 0.5 * one_ref[1:4]
    sums_ref[6:10] = 0.5 * two_ref[0:4]

    def project(at):
        grad = dot_nt(grad_ref[at, :], maps_ref[:, : 3 * width])
        hat, _ = normed(tokens_ref[at, :].astype(F32))
        sums_ref[0:2] += jnp.concatenate([column_sum(grad * hat), column_sum(grad)], 0)
        sorted_ref[at, :] = grad.astype(BF16)

    chunk_loop(count, project)
    rows = count // 2
    for i in range(0, rows, CHUNK):
        far_ref[i : i + CHUNK, :] = dot(back_ref[rows + i : rows + i + CHUNK, :], sorted_ref[...]).astype(BF16)
    for i in range(0, rows, CHUNK):
        own_ref[i : i + CHUNK, :] = dot(back_ref[i : i + CHUNK, :], sorted_ref[...]).astype(BF16)


def input_grad_kernel(part_ref, got_ref, tokens_ref, vec_ref, before_ref, out_ref):
    gain = vec_ref[0:1]

    def through_norm(at):
        grad = part_ref[at, :].astype(F32) + got_ref[at, :].astype(F32)
        hat, factor = normed(tokens_ref[at, :].astype(F32))
        out_ref[at, :] = before_ref[at, :] + norm_grad(hat, factor, gain, grad)

    chunk_loop(out_ref.shape[0], through_norm)


def layer_out_kernel(stream_ref, part_ref, got_ref, vec_ref, out_ref):
    out_ref[...] = stream_ref[...] + (part_ref[...].astype(F32) + got_ref[...].astype(F32)) + vec_ref[9:10]


def whole_rows_kernel(place_ref, own_ref, got_ref, out_ref, sem):
    core = place_ref[3]
    rows = own_ref.shape[0]
    copies = [
        pltpu.make_async_copy(ref, out_ref.at[pl.ds(pl.multiple_of(at * rows, rows), rows)], sem.at[i])
        for i, (ref, at) in enumerate(((own_ref, core), (got_ref, 1 - core)))
    ]
    for copy in copies:
        copy.start()
    for copy in copies:
        copy.wait()


def fused_grads_kernel(low_ref, heads_ref, got_heads_ref, own_ref, far_ref):
    ones = jnp.ones((low_ref.shape[0], own_ref.shape[1] - heads_ref.shape[1]), BF16)
    far_ref[...] = dot_tn(low_ref[...], jnp.concatenate([got_heads_ref[...], ones], 1)).astype(BF16)
    own_ref[...] = dot_tn(low_ref[...], jnp.concatenate([heads_ref[...], ones], 1))


def mix_grads_kernel(
    place_ref, fused_ref, got_ref, mix_ref, sums_ref, grad_out_ref, total_ref, row_sum_ref, bias_ref
):
    place = place_ref[2]
    width = total_ref.shape[1]
    both = fused_ref[...] + got_ref[...].astype(F32)
    row_sum_ref[...] = both[:, width:]
    fused = both[:, :width].astype(BF16)
    total_ref[...] = fused
    for j in range(4):
        block = mix_ref[place ^ j]
        grad_out_ref[j * width : (j + 1) * width, :] = dot_tn(block, fused).astype(BF16)
        bias_ref[:, j * width : (j + 1) * width] = dot(sums_ref[...].astype(BF16), block)


def mix_shard_kernel(place_ref, out_ref, *refs):
    ins, (grad_ref, keep_ref, send_ref) = refs[:-3], refs[-3:]
    place = place_ref[2]
    width = out_ref.shape[1]
    total = sum(ref[:, : 2 * width].astype(F32) for ref in ins)
    grad_ref[...] = total[:, :width]
    fused = total[:, width:].astype(BF16)
    for m in range(4):
        rows = out_ref[pl.ds(pl.multiple_of((place ^ m) * width, width), width), :]
        part = dot_nt(fused, rows)
        ref = send_ref if m % 2 else keep_ref
        ref[:, m // 2 * width : (m // 2 + 1) * width] = part.astype(ref.dtype)


def mix_sum_kernel(keep_ref, got_ref, own_ref, send_ref):
    width = own_ref.shape[1]
    total = keep_ref[...] + got_ref[...].astype(F32)
    own_ref[...] = total[:, :width]
    send_ref[...] = total[:, width:].astype(BF16)


def add_kernel(own_ref, got_ref, out_ref):
    out_ref[...] = (own_ref[...].astype(F32) + got_ref[...].astype(F32)).astype(BF16)


def whole_grad_kernel(head_ref, early_ref, grad_ref):
    columns = head_ref.shape[1]
    grad_ref[:, :columns] = head_ref[...]
    grad_ref[:, columns:] = early_ref[...]


def update_kernel(terms, shards, steps, place_ref, *refs):
    sums, refs = refs[:terms], refs[terms:]
    grad_ref, *matrix = refs[:5]
    vectors, refs = refs[5:9], refs[9:]
    new, (vector_grad_ref, norm_ref, *vectors_new) = refs[:4], refs[4:10]
    held_in, held_out, sem_in, sem_out = refs[10:14], refs[14:18], refs[18], refs[19]
    count = grad_ref.shape[0] // steps
    cuts = [pl.ds(i * count, count) for i in range(steps)]
    loads = [
        [pltpu.make_async_copy(a.at[cut], b.at[cut], sem_in.at[i, j]) for j, (a, b) in enumerate(zip(matrix, held_in))]
        for i, cut in enumerate(cuts)
    ]
    stores = [
        [
            pltpu.make_async_copy(a.at[cut], b.at[cut], sem_out.at[i, j])
            for j, (a, b) in enumerate(zip(held_out, new))
        ]
        for i, cut in enumerate(cuts)
    ]
    for step in loads:
        for copy in step:
            copy.start()
    total = sums[0][...]
    if terms > 1:
        total = total + sums[1][...]
    if terms > 2:
        total = total + (sums[2][...] + sums[3][...])
    rows = total[:VECTORS]
    norm = jnp.sqrt(total[VECTORS : VECTORS + 1, 0:1] + jnp.sum(rows * rows))
    norm_ref[...] = norm
    limit = 0.5 * math.sqrt(NPARAM)
    factor = limit / jnp.maximum(norm, limit)
    for i, cut in enumerate(cuts):
        for copy in loads[i]:
            copy.wait()
        states = [ref[cut, :] for ref in held_in]
        updated = adam_update(*states, grad_ref[cut, :], factor, MATRIX_RATE, MATRIX_DECAY)
        for ref, value in zip(held_out, updated):
            ref[cut, :] = value
        for copy in stores[i]:
            copy.start()
    width = vector_grad_ref.shape[1]
    vector_grad = 0.0
    for j in range(shards):
        part = rows[:, j * width : (j + 1) * width]
        vector_grad = vector_grad + jnp.where(place_ref[4] == j, part, 0.0)
    vector_grad_ref[...] = vector_grad
    updated = adam_update(*[ref[...] for ref in vectors], vector_grad, factor, VECTOR_RATE, 0.0)
    for ref, value in zip(vectors_new, updated):
        ref[...] = value
    for step in stores:
        for copy in step:
            copy.wait()


def adam_update(master, first_moment, second_moment, average, gradient, factor, rate, decay):
    clipped = gradient * factor
    first_new = BETA_FIRST * first_moment + (1.0 - BETA_FIRST) * clipped
    second_new = BETA_SECOND * second_moment + (1.0 - BETA_SECOND) * clipped * clipped
    first_hat = first_new / (1.0 - BETA_FIRST**STEP)
    second_hat = second_new / (1.0 - BETA_SECOND**STEP)
    master_new = master - rate * (first_hat / (jnp.sqrt(second_hat) + ADAM_EPS) + decay * master)
    average_new = AVERAGE_RATE * average + (1.0 - AVERAGE_RATE) * master_new
    return (master_new, first_new, second_new, average_new)


def local(
    tokens,
    cotangent,
    clip_ids,
    frame_ids,
    patch_ids,
    weights,
    weights_m,
    weights_v,
    weights_ema,
    vectors,
    vectors_m,
    vectors_v,
    vectors_ema,
):
    group_count = lax.axis_size("heads")
    core = lax.axis_index("heads") % 2
    place = places()
    count, features = tokens.shape
    width = features // group_count
    hidden = (weights.shape[1] - 9 * width) // 2
    rows = count // 2
    half = lax.axis_size("dp") // 2
    shard = weights.shape[0]

    wide = lambda n, dtype: shaped((rows, n), dtype)

    head_start = -(-(3 * width + 16) // 128) * 128
    head_piece, space_piece, up_piece, down_piece = local_call(
        "pack",
        pack_kernel,
        [shaped((shard, n), BF16) for n in (head_start + 2 * width, 4 * width, hidden, hidden)],
        weights, vectors,
    )
    head_z = z_blocks(head_piece)
    tokens_sorted, order, back, time_col, time_row, space_col, space_row, tokens_own, dy = local_call(
        "sort_rows",
        sort_kernel,
        [
            shaped((count, features), BF16),
            shaped((count, count), BF16),
            shaped((count, count), BF16),
            shaped((count, 8), F32),
            shaped((8, count), F32),
            shaped((count, 8), jnp.int32),
            shaped((8, count), jnp.int32),
            wide(features, BF16),
            wide(features, BF16),
        ],
        place, clip_ids, frame_ids, patch_ids, tokens, cotangent,
        smem=(0,),
        scratch=[pltpu.VMEM((count, features), BF16)],
    )
    head_y = [dp_swap(head_piece, 1)]
    before = tokens_sorted
    for k in range(1, half):
        head_z[k] = after(head_z[k], before)
        before = head_z[k]
        head_y.append(dp_swap(head_z[k], 1))
    space_z = z_blocks(after(space_piece, *head_z))
    (head_y,) = together(head_y)
    time_maps, mix_map, out_map = assemble(
        "gather_head", head_z, head_y, (head_start, head_start + width)
    )
    mix_x = x_swap(mix_map)

    vec, first, time_inputs, time_own, time_send, time_logs = local_call(
        "time_forward",
        time_forward_kernel,
        [
            shaped((16, features), F32),
            shaped((count, features), BF16),
            shaped((count, 3 * width), BF16),
            wide(width, BF16),
            wide(width, BF16),
            shaped((8, count), F32),
        ],
        time_maps, tokens_sorted, back, time_col, time_row,
        scratch=[pltpu.VMEM((count, width), BF16)],
    )
    space_z, (mix_x, time_send) = together(space_z, [mix_x, time_send])
    mix_core = core_swap(jnp.concatenate([mix_map, mix_x], 1))
    time_got = core_swap(time_send)

    mix_blocks, fused, mix_bias = local_call(
        "mix_maps",
        mix_kernel,
        [
            shaped((group_count, features, width), BF16),
            shaped((features, width), BF16),
            shaped((1, features), F32),
        ],
        place, out_map, mix_map, mix_x, mix_core, vec,
        smem=(0,),
    )
    fused_far = core_swap(fused)
    space_y = y_blocks(space_z)
    up_z = z_blocks(after(up_piece, *space_z))
    (time_part,) = local_call("time_out", time_out_kernel, [wide(features, BF16)], time_own, time_got, fused, fused_far)
    stream_one, second = local_call(
        "space_norm",
        partial(norm_in_kernel, 4),
        [wide(features, F32), wide(features, BF16)],
        tokens_own, time_part, x_swap(time_part), mix_bias, vec,
        flops=LONG,
    )

    space_own = assemble("gather_space", space_z, space_y)
    space_far = core_swap(space_own)
    space_q, space_pairs = local_call(
        "space_in",
        space_in_kernel,
        [wide(2 * width, BF16), wide(4 * width, BF16)],
        second, space_own, space_far,
    )
    up_z, (space_q, space_pairs) = together(up_z, [space_q, space_pairs])
    up_y = y_blocks(up_z)
    down_z = z_blocks(after(down_piece, *up_z))
    space_got = core_swap(space_pairs)
    space_heads, space_logs, class_logs, space_part = local_call(
        "space_forward",
        space_forward_kernel,
        [wide(2 * width, BF16), shaped((8, rows), F32), shaped((CLASSES, 8), F32), wide(features, BF16)],
        place, space_q, space_pairs, space_got, space_col, space_row, space_own, space_far,
        smem=(0,),
        scratch=[pltpu.VMEM((count, 4 * width), BF16), pltpu.VMEM((CLASSES, 4 * width), BF16)],
    )
    up_y, down_z, (space_part,) = together(up_y, down_z, [space_part])
    stream_two, third = local_call(
        "feed_norm",
        partial(norm_in_kernel, 7),
        [wide(features, F32), wide(features, BF16)],
        stream_one, space_part, x_swap(space_part), vec[6:8], vec,
        flops=LONG,
    )

    up_own = assemble("gather_up", up_z, up_y)
    up_far = core_swap(up_own)
    down_own = assemble("gather_down", down_z, y_blocks(down_z))
    down_far = core_swap(down_own)
    activ, grad_pre, third_part = local_call(
        "feed",
        feed_kernel,
        [wide(2 * hidden, BF16), wide(2 * hidden, BF16), wide(features, BF16)],
        third, dy, up_own, up_far, down_own, down_far,
    )
    third_got = x_swap(third_part)
    feed_grad_far, feed_grad_own = [
        local_call(
            name,
            partial(feed_grads_kernel, group),
            [shaped((features, 2 * hidden), BF16)],
            third, grad_pre, dy, activ,
        )[0]
        for name, group in (("feed_grads_far", 1), ("feed_grads_own", 0))
    ]
    (feed_part,) = local_call("feed_out", feed_out_kernel, [wide(features, BF16)], activ, down_own, down_far)
    (up_send, up_keep), (down_send, down_keep) = split_rows(
        "split_feed", [(feed_grad_own, core_swap(feed_grad_far))], (hidden,)
    )
    up_y = [dp_swap(up_send, 1)]
    third_got, feed_part = lax.optimization_barrier((third_got, feed_part))

    grad_two, grad_two_low, sums_two, space_grad_heads = local_call(
        "space_back_in",
        space_back_in_kernel,
        [wide(features, F32), wide(features, BF16), shaped((8, features), F32), wide(2 * width, BF16)],
        third_part, third_got, stream_two, vec, dy, space_own, space_far,
    )
    space_dq, space_keep, space_send = local_call(
        "space_backward",
        space_backward_kernel,
        [wide(2 * width, BF16), wide(4 * width, F32), wide(4 * width, BF16)],
        place, space_grad_heads, space_q, space_pairs, space_got, space_logs, class_logs, space_col, space_row,
        smem=(0,),
        scratch=[
            pltpu.VMEM((count, 4 * width), BF16),
            pltpu.VMEM((CLASSES, 4 * width), BF16),
            pltpu.VMEM((count, 4 * width), F32),
            pltpu.VMEM((CLASSES, 4 * width), F32),
            pltpu.VMEM((CLASSES, 2 * width), BF16),
        ],
    )
    up_y, (space_send,) = together(up_y, [space_send])
    up_shards = z_swaps(y_sums("sum_up", [(up_keep, up_y)]))
    space_got_grads = core_swap(space_send)
    down_y = [dp_swap(after(down_send, *up_y), 1)]
    grad_space, grad_space_far, second_part = local_call(
        "space_back",
        space_back_kernel,
        [wide(3 * width, BF16), wide(3 * width, BF16), wide(features, BF16)],
        space_dq, space_keep, space_got_grads, space_own, space_far,
    )
    second_got = x_swap(second_part)
    space_grad_far, space_grad_own = [
        local_call(
            name,
            partial(space_grads_kernel, group),
            [shaped((features, 4 * width), BF16)],
            second, grad, grad_two_low, space_heads,
        )[0]
        for name, group, grad in (("space_grads_far", 1, grad_space_far), ("space_grads_own", 0, grad_space))
    ]

    def whole(name, value, got):
        return pl.pallas_call(
            whole_rows_kernel,
            name=name,
            out_shape=shaped((count, features), F32),
            in_specs=[SMEM, VMEM, VMEM],
            out_specs=ANY,
            scratch_shapes=[pltpu.SemaphoreType.DMA((2,))],
            compiler_params=pltpu.CompilerParams(vmem_limit_bytes=2**23),
            cost_estimate=pl.CostEstimate(flops=0, bytes_accessed=0, transcendentals=0),
        )(place, value, got)

    ((space_y_send, space_keep),) = split_rows("split_space", [(space_grad_own, core_swap(space_grad_far))])
    space_y = [dp_swap(space_y_send, 1)]
    up_shards, (second_got, space_y_send) = together(up_shards, [second_got, space_y_send])
    grad_one, grad_one_low, sums_one, time_grad_own, time_grad_send = local_call(
        "time_back_in",
        time_back_in_kernel,
        [
            wide(features, F32),
            wide(features, BF16),
            shaped((8, features), F32),
            wide(width, BF16),
            wide(width, BF16),
        ],
        second_part, second_got, stream_one, vec, grad_two, fused, fused_far,
    )
    down_y, (time_grad_own, time_grad_send, grad_one_low) = together(
        down_y, [time_grad_own, time_grad_send, grad_one_low]
    )
    down_shards = z_swaps(y_sums("sum_down", [(down_keep, down_y)]))
    time_grad_got = core_swap(time_grad_send)
    fused_grad, fused_grad_far = local_call(
        "fused_grads",
        fused_grads_kernel,
        [shaped((features, width + SPARE), F32), shaped((features, width + SPARE), BF16)],
        grad_one_low, time_own, time_got,
    )
    fused_grad_got = core_swap(fused_grad_far)
    grad_time_out, fused_total, row_sum, bias_grad = local_call(
        "mix_grads",
        mix_grads_kernel,
        [
            shaped((features, width), BF16),
            shaped((features, width), BF16),
            shaped((features, SPARE), F32),
            shaped((8, features), F32),
        ],
        place, fused_grad, fused_grad_got, mix_blocks, sums_one,
        smem=(0,),
    )
    ((out_send, out_keep),) = split_rows("split_out", [(grad_time_out, None), (fused_total, None)])
    out_send, time_grad_own, time_grad_got = lax.optimization_barrier((out_send, time_grad_own, time_grad_got))
    out_y = [dp_swap(out_send, 1)]
    (grad_time,) = local_call(
        "time_backward",
        time_backward_kernel,
        [shaped((count, 3 * width), BF16)],
        time_grad_own, time_grad_got, order, time_inputs, time_logs, time_col, time_row,
        scratch=[pltpu.VMEM((count, width), BF16), pltpu.VMEM((count, 2 * width), F32)],
    )
    down_shards, space_y, out_y, (grad_time,) = together(down_shards, space_y, out_y, [grad_time])
    time_columns = 3 * width + SPARE
    time_send, time_keep = local_call(
        "time_grads",
        time_grads_kernel,
        [shaped((half, shard, time_columns), BF16), shaped((half, shard, time_columns), F32)],
        place, first, grad_time, row_sum,
        smem=(0,),
        scratch=[pltpu.VMEM((features, time_columns), F32)],
    )
    space_y, out_y, (time_send, grad_time) = together(space_y, out_y, [time_send, grad_time])
    time_y = [dp_swap(time_send, 1)]
    late_shards = z_swaps(y_sums("sum_late", [(out_keep, out_y), (space_keep, space_y)]))
    first_own, first_send, vector_sum = local_call(
        "time_back",
        time_back_kernel,
        [wide(features, BF16), wide(features, BF16), shaped((16, features), F32)],
        grad_time, time_maps, tokens_sorted, back, bias_grad, sums_one, sums_two,
        scratch=[pltpu.VMEM((count, features), BF16)],
    )
    feed_part_got = x_swap(after(feed_part, time_send))
    time_y, late_shards, (first_send, feed_part_got) = together(time_y, late_shards, [first_send, feed_part_got])
    first_got = core_swap(first_send)

    out_width = 2 * width
    out_grad, mix_keep, mix_send = local_call(
        "mix_shard",
        mix_shard_kernel,
        [shaped((shard, width), F32), shaped((shard, out_width), F32), shaped((shard, out_width), BF16)],
        place, out_map, *late_shards,
        smem=(0,),
    )
    (first_part,) = local_call("first_part", add_kernel, [wide(features, BF16)], first_own, first_got)
    mix_own, mix_send = local_call(
        "mix_sum",
        mix_sum_kernel,
        [shaped((shard, width), F32), shaped((shard, width), BF16)],
        mix_keep, core_swap(mix_send),
    )
    mix_got = x_swap(mix_send)
    first_part = after(first_part, mix_send)
    first_part_got = x_swap(first_part)
    (layer_half,) = local_call(
        "layer_out", layer_out_kernel, [wide(features, F32)], stream_two, feed_part, feed_part_got, vec
    )
    layer_got = core_swap(after(layer_half, first_got))
    time_shards = y_sums("sum_time", [(time_keep, time_y)])
    time_shards, (mix_got, layer_got) = together(time_shards, [mix_got, layer_got])
    time_shards = z_swaps(time_shards)
    layer_rows = whole("layer_rows", layer_half, layer_got)

    bias_part = lax.dynamic_slice_in_dim(vec[2:3], lax.axis_index("heads") * width, width, 1)
    late = [out_width, out_width + 4 * width]
    total = lambda shards: sum([one.astype(F32) for one in shards])
    up_shards, down_shards, _ = together(up_shards, down_shards, [first_part])
    early_grad = jnp.concatenate([total(late_shards)[:, out_width:], total(up_shards), total(down_shards)], 1)
    early_square = jnp.sum(early_grad * early_grad)
    time_shards, (early_grad, early_square, layer_rows) = together(time_shards, [early_grad, early_square, layer_rows])
    time_total = total(time_shards)
    mix_grad = mix_own + mix_got.astype(F32) + time_total[:, 3 * width : 3 * width + 1] * bias_part
    head_grad = jnp.concatenate([time_total[:, : 3 * width], out_grad, mix_grad], 1)
    square = early_square + jnp.sum(head_grad * head_grad)
    row = lax.broadcasted_iota(jnp.int32, vector_sum.shape, 0)
    sums = jnp.where(row == VECTORS, square, vector_sum)

    def input_half(ready):
        return local_call(
            "input_grad",
            input_grad_kernel,
            [wide(features, F32)],
            first_part, after(first_part_got, ready), tokens_own, vec, grad_one,
        )

    def last_results(ready, grad_half):
        grad_rows = whole("grad_rows", grad_half, core_swap(grad_half))
        (weight_grad,) = local_call(
            "whole_grad", whole_grad_kernel, [shaped(weights.shape, F32)], after(head_grad, ready), early_grad
        )
        return [grad_rows, weight_grad]

    terms, (grad_rows, weight_grad) = all_sum(sums, input_half, last_results)
    steps = max(one for one in (1, 2, 3, 4) if shard % (8 * one) == 0)
    states = [weights, weights_m, weights_v, weights_ema]
    vector_states = [vectors, vectors_m, vectors_v, vectors_ema]
    outs = pl.pallas_call(
        partial(update_kernel, len(terms), lax.axis_size("dp"), steps),
        name="update",
        out_shape=[shaped(weights.shape, F32)] * 4
        + [shaped(vectors.shape, F32), shaped((1, 1), F32)]
        + [shaped(vectors.shape, F32)] * 4,
        in_specs=[SMEM] + [VMEM] * (len(terms) + 1) + [ANY] * 4 + [VMEM] * 4,
        out_specs=[ANY] * 4 + [VMEM] * 6,
        scratch_shapes=[pltpu.VMEM(weights.shape, F32)] * 8
        + [pltpu.SemaphoreType.DMA((steps, 4)), pltpu.SemaphoreType.DMA((steps, 4))],
        compiler_params=pltpu.CompilerParams(vmem_limit_bytes=20 * 2**20),
    )(place, *terms, weight_grad, *states, *vector_states)
    weights_out, (vector_grad, grad_norm, *vectors_out) = outs[:4], outs[4:]
    return (
        layer_rows,
        grad_rows,
        weight_grad,
        vector_grad,
        grad_norm[0, 0],
        *weights_out,
        *vectors_out,
    )


def solution(mesh):
    rows, square, line = P("dp", None), P("dp", "heads"), P(None, "dp")
    placed = (rows,) * 5 + (square,) * 4 + (line,) * 4
    return jax.shard_map(
        local,
        mesh=mesh,
        in_specs=placed,
        out_specs=(rows, rows, square, line, P()) + (square,) * 4 + (line,) * 4,
        check_vma=False,
    )
```
